32 devices in a mesh: row: 8 (over y, x, core), col: 4 (over z).
Axes of the slice: x: 2, y: 2, z: 4, core: 2. Of those that a mesh axis runs over, the one named last changes fastest.
Arguments:
- front_matrix: float32 [3072, 16384], P('row', 'col'), may hold values from -6 to 6
- child_rows: float32 [512, 16384], P('row', 'col'), may hold values from -6 to 6
- child_owner: int32 [512, 1], P('row'), may hold values from 0 to 7; in each aligned block of 64 rows (0 to 63, 64 to 127, ...) at most 16 rows name the same one
- child_offset: int32 [512, 1], P('row'), may hold values from 0 to 383
Outputs:
- upper_rows: float32 [512, 16384], P(None, 'col')
- reduced_front: float32 [3072, 16384], P('row', 'col')
- basis_scaled: float32 [3072, 512], P('row')
The draws below stay inside these ranges and needn't reach their ends.
Inputs may be any that keep to these rules, and one draw needn't show every extreme that they name: `child_owner`: within the rows of one device (aligned blocks of 64 rows) no value occurs more than 16 times, and some value occurs exactly 16 times.
All inputs are finite; a program needn't handle non-finite values.
Results may differ from the reference program's by a relative error of at most 0.0001.
Values sent between devices are 32-bit elements; how exact they have to be, the bound alone decides.
No kernel may reach another device: no remote copies, remote signals or barrier semaphores. Data moves between devices by JAX's collectives and lax.ppermute only.
A program may use at most 128 MiB of HBM per device.

```python
import math
import jax
import jax.numpy as jnp
import numpy as np
from jax import lax

NC = 16384
PB = 128
PANELS = 4
ROWS_DEV = 384
CHILD_DEV = 64
M = 3072
CHILDREN = 512
MOST = 16
N_ROW = 8


def touch_ends(drawn, key, smallest, largest):
    index_at = [jax.random.randint(jax.random.fold_in(key, axis), (), 0, length) for axis, length in enumerate(drawn.shape)]
    main_axis = drawn.shape.index(max(drawn.shape))
    beside = index_at[:main_axis] + [(index_at[main_axis] + 1) % drawn.shape[main_axis]] + index_at[main_axis + 1:]
    return drawn.at[tuple(index_at)].set(smallest).at[tuple(beside)].set(largest)


def steps_of(own_key, extent, cuts, smallest, largest):
    def one(dim, parts):
        draws = jax.random.uniform(jax.random.fold_in(jax.random.fold_in(own_key, 6), dim), (parts,), jnp.float32, smallest / len(cuts), largest / len(cuts))
        return jnp.repeat(jnp.exp(draws), extent[dim] // parts).reshape((-1,) + (1,) * (len(extent) - dim - 1))

    factor_of = one(*cuts[0])
    for cut in cuts[1:]:
        factor_of = factor_of * one(*cut)
    return factor_of


def assign_block(rng, own, number, rows, count, top, limit, skew):
    order = jax.random.permutation(rng, count)
    packed, common = portions_of(count, rows * top, limit, skew, True), portions_of(count, rows * top, limit, skew, False)
    places = jnp.arange(count)

    def named(tallies, offset_by):
        used = int((tallies > 0).sum())
        fixed = max(1, used // 4)
        passed = fixed + (places - fixed + offset_by * (used - fixed)) % max(1, count - fixed)
        return jnp.zeros((count,), jnp.int32).at[order[jnp.where(places < fixed, places, passed)]].set(jnp.asarray(tallies, jnp.int32))

    tallies = jnp.where(number % 4 == 0, named(packed, number // 4), named(common, number - number // 4 - 1))
    mixed = jax.random.permutation(jax.random.fold_in(own, 3), count)
    donor, sink = mixed[0:count // 2 * 2:2], mixed[1:count // 2 * 2:2]
    room = jnp.minimum(tallies[donor] - 1, limit - tallies[sink]) // 2
    room = jnp.where((donor == order[0]) | (sink == order[0]) | (tallies[sink] == 0), 0, jnp.maximum(room, 0))
    passed = jax.random.randint(jax.random.fold_in(own, 4), (count // 2,), 0, 1 << 20) % (room + 1)
    tallies = tallies.at[donor].add(-passed).at[sink].add(passed)
    members = jnp.searchsorted(jnp.cumsum(tallies), jnp.arange(rows * top), side="right").astype(jnp.int32)
    grid = members.reshape(top, rows).T
    grid = grid[jax.random.permutation(jax.random.fold_in(own, 1), rows)]
    offset_by = jax.random.randint(jax.random.fold_in(own, 2), (rows, 1), 0, top)
    return jnp.take_along_axis(grid, (jnp.arange(top)[None, :] + offset_by) % top, axis=1)


def portions_of(number_of, total, most, skew, full):
    weights = [(1 << 20) // math.isqrt(rank ** skew) + 1 for rank in range(1, number_of + 1)]
    largest = most if full else min(most, max(-(-total // number_of), total * weights[0] // sum(weights)))
    least = 1 if total - largest >= number_of - 1 else 0
    given, surplus = [largest] + [least] * (number_of - 1), total - largest - least * (number_of - 1)
    while surplus > 0:
        movable = [i for i in range(1, number_of) if given[i] < largest] or [i for i in range(1, number_of) if given[i] < most]
        whole, left = sum([weights[i] for i in movable]), surplus
        for i in movable:
            addition = min(most - given[i], max(1, left * weights[i] // whole), surplus)
            given[i] = given[i] + addition
            surplus = surplus - addition
    return np.array(given)


def noise(key, shape, scale, reach, shards=(), kind=jnp.bfloat16):
    loudness = steps_of(key, shape, shards, -0.22, 0.18) if shards else 1.0
    result = jax.random.normal(key, shape, jnp.float32) * scale * loudness
    return jnp.minimum(jnp.maximum(result, -reach), reach).astype(kind)


def setup_inputs(seed: int = 0) -> dict:
    streams_of = jax.random.split(jax.random.key(seed), 5)
    front_matrix = noise(streams_of[0], (M, NC), 1.0, 6.0, ((0, 8), (1, 4)), jnp.float32)
    child_rows = noise(streams_of[1], (CHILDREN, NC), 1.0, 6.0, ((0, 8), (1, 4)), jnp.float32)
    child_owner_keys = jax.random.split(jax.random.fold_in(streams_of[2], 1), CHILDREN // CHILD_DEV)
    child_owner_turns = jax.random.permutation(jax.random.fold_in(streams_of[2], 3), CHILDREN // CHILD_DEV)
    child_owner = jax.vmap(lambda own, number: assign_block(jax.random.fold_in(streams_of[2], 2), own, number, CHILD_DEV, N_ROW, 1, MOST, 1))(child_owner_keys, child_owner_turns).reshape((CHILDREN, 1))
    child_offset = touch_ends(jax.random.randint(streams_of[3], (CHILDREN, 1), 0, ROWS_DEV), jax.random.fold_in(streams_of[3], 1), 0, ROWS_DEV - 1).astype(jnp.int32)
    return {"front_matrix": front_matrix, "child_rows": child_rows, "child_owner": child_owner, "child_offset": child_offset}


def product(left_op, right_op):
    return jnp.dot(left_op.astype(jnp.float32), right_op.astype(jnp.float32), precision=lax.Precision.HIGHEST, preferred_element_type=jnp.float32)

def factor_panel(panel_cols):
    gram_total = product(panel_cols.T, panel_cols)
    lower_factor = jnp.linalg.cholesky(gram_total)
    return lax.linalg.triangular_solve(lower_factor, panel_cols, left_side=False, lower=True, transpose_a=True)

def reference(front_matrix, child_rows, child_owner, child_offset):
    target = (child_owner[:, 0] * ROWS_DEV + child_offset[:, 0]).astype(jnp.int32)
    current = front_matrix.at[target].add(child_rows)
    top_list = []
    basis_list = []
    for panel_index in range(PANELS):
        basis = factor_panel(current[:, panel_index * PB:(panel_index + 1) * PB])
        top_rows = product(basis.T, current)
        current = current - product(basis, top_rows)
        top_list.append(top_rows)
        basis_list.append(basis)
    scaled = jnp.concatenate(basis_list, axis=1) * math.sqrt(M)
    return (jnp.concatenate(top_list, axis=0), current, scaled)
```

```python
import functools
import math

import jax
import jax.numpy as jnp
import numpy as np
from jax import lax
from jax.experimental import pallas as pl
from jax.experimental.pallas import tpu as pltpu
from jax.sharding import PartitionSpec as P

PB = 128
PANELS = 4
LEAD = PB * PANELS
GROUP = 256
VMEM_BYTES = 48 * 1024 * 1024
HIGHEST = lax.Precision.HIGHEST
F32 = jnp.float32
BF16 = jnp.bfloat16
SMEM = pltpu.SMEM
VMEM = pltpu.VMEM


def params():
    return pltpu.CompilerParams(vmem_limit_bytes=VMEM_BYTES)


def mask_orders(count):
    others = [1 << b for b in range(1, count.bit_length() - 1)]
    half = len(others) // 2
    return ([1] + others, [1] + others[half:] + others[:half])


def swap(value, step, count):
    orders = mask_orders(count)
    pairs = [(d, d ^ orders[d & 1][step]) for d in range(count)]
    return lax.ppermute(value, "row", pairs)


def upper_side(step, count):
    orders = mask_orders(count)
    me = lax.axis_index("row")
    mask = jnp.where(me & 1 == 0, orders[0][step], orders[1][step])
    return ((me & mask) != 0).astype(jnp.int32)


def shard_table(count):
    orders = mask_orders(count)
    steps = len(orders[0])
    return np.array(
        [
            sum(((d & orders[d & 1][t]) != 0) << (steps - 1 - t) for t in range(steps))
            for d in range(count)
        ]
    )


def piece_table(count):
    orders = mask_orders(count)
    steps = len(orders[0])
    shard = shard_table(count)

    def pieces(device, done):
        if done == 0:
            return [device]
        mask = orders[device & 1][steps - done]
        return pieces(device, done - 1) + pieces(device ^ mask, done - 1)

    return np.array([[shard[p] for p in pieces(d, steps)] for d in range(count)], np.int32)


def halve(value, other, axis, step, count):
    side = upper_side(step, count)
    size = value.shape[axis] // 2

    def take(which):
        mine = lax.dynamic_slice_in_dim(value, which * size, size, axis)
        if other is None:
            return mine
        return mine + lax.dynamic_slice_in_dim(other, which * size, size, axis)

    return take(side), take(1 - side)


def scatter_sum(keep, send, axis, count):
    steps = count.bit_length() - 1
    for step in range(steps):
        got = swap(send, step, count)
        if step == steps - 1:
            return keep + got
        keep, send = halve(keep, got, axis, step + 1, count)


def total_rows(value, count):
    keep, send = halve(value, None, 0, 0, count)
    mine = scatter_sum(keep, send, 0, count)
    for step in reversed(range(count.bit_length() - 1)):
        got = swap(mine, step, count)
        side = upper_side(step, count)
        mine = jnp.where(
            side == 0,
            jnp.concatenate([mine, got], axis=0),
            jnp.concatenate([got, mine], axis=0),
        )
    return mine


def spread(value, count):
    me = lax.axis_index("col")
    stride = count
    while stride > 1:
        half = stride // 2
        pairs = [(c, c + half) for c in range(0, count, stride)]
        got = lax.ppermute(value, "col", pairs)
        value = jnp.where(me % stride == half, got, value)
        stride = half
    return value


def parts3(x):
    hi = x.astype(BF16)
    rest = x - hi.astype(F32)
    mid = rest.astype(BF16)
    return hi, mid, (rest - mid.astype(F32)).astype(BF16)


def parts2(x):
    hi = x.astype(BF16)
    return hi, (x - hi.astype(F32)).astype(BF16)


def pack_kernel(row_count, capacity, sentinel, owner_ref, offset_ref, child_ref, out_ref, tag_ref, tally):
    out_ref[...] = jnp.zeros_like(out_ref)
    tag_ref[...] = jnp.full(tag_ref.shape, sentinel, F32)
    for d in range(row_count):
        tally[d] = 0

    def body(i, carry):
        owner = owner_ref[i]
        rank = tally[owner]
        tally[owner] = rank + 1
        slot = owner * capacity + rank
        out_ref[pl.ds(slot, 1), :] = child_ref[pl.ds(i, 1), :]
        tag_ref[pl.ds(slot, 1), :] = jnp.full((1, tag_ref.shape[1]), offset_ref[i].astype(F32))
        return carry

    lax.fori_loop(0, child_ref.shape[0], body, 0)


def pack(child_rows, owner, offset, row_count, capacity, sentinel):
    slots = row_count * capacity
    return pl.pallas_call(
        functools.partial(pack_kernel, row_count, capacity, float(sentinel)),
        out_shape=(
            jax.ShapeDtypeStruct((slots, child_rows.shape[1]), F32),
            jax.ShapeDtypeStruct((slots, PB), F32),
        ),
        in_specs=[
            pl.BlockSpec(memory_space=SMEM),
            pl.BlockSpec(memory_space=SMEM),
            pl.BlockSpec(memory_space=VMEM),
        ],
        out_specs=(pl.BlockSpec(memory_space=VMEM), pl.BlockSpec(memory_space=VMEM)),
        scratch_shapes=[pltpu.SMEM((row_count,), jnp.int32)],
        compiler_params=params(),
        name="pack_children",
    )(owner, offset, child_rows)


def assemble_kernel(front_ref, child_ref, tag_ref, out_ref):
    rows = front_ref.shape[0]
    slots = child_ref.shape[0]
    place = jnp.transpose(tag_ref[...])[0:1, :]
    at = lax.broadcasted_iota(jnp.int32, (rows, slots), 0).astype(F32)
    onehot = jnp.where(at == place, 1.0, 0.0).astype(BF16)
    added = jnp.zeros(front_ref.shape, F32)
    for part in reversed(parts3(child_ref[...])):
        added = added + jnp.dot(onehot, part, preferred_element_type=F32)
    out_ref[...] = front_ref[...] + added


def assemble(front, child, tags, columns, block):
    rows = front.shape[0]
    slots = child.shape[0]
    return pl.pallas_call(
        assemble_kernel,
        grid=(columns // block,),
        out_shape=jax.ShapeDtypeStruct((rows, columns), F32),
        in_specs=[
            pl.BlockSpec((rows, block), lambda i: (0, i)),
            pl.BlockSpec((slots, block), lambda i: (0, i)),
            pl.BlockSpec((slots, PB), lambda i: (0, 0)),
        ],
        out_specs=pl.BlockSpec((rows, block), lambda i: (0, i)),
        compiler_params=params(),
        name="assemble_front",
    )(front, child, tags)


def lead_product_kernel(half_ref, lead_ref, front_ref, out_ref):
    del half_ref
    lead_hi, lead_lo = parts2(jnp.transpose(lead_ref[...]))
    hi, lo = parts2(front_ref[...])
    left = jnp.concatenate([lead_hi, lead_hi, lead_lo], axis=1)
    right = jnp.concatenate([hi, lo, hi], axis=0)
    out_ref[...] = jnp.dot(left, right, preferred_element_type=F32)


def lead_product(half, lead, front, block):
    rows, columns = front.shape
    width = lead.shape[1]
    steps = columns // 2 // block
    return pl.pallas_call(
        lead_product_kernel,
        grid_spec=pltpu.PrefetchScalarGridSpec(
            num_scalar_prefetch=1,
            grid=(steps,),
            in_specs=[
                pl.BlockSpec((rows, width), lambda i, h: (0, 0)),
                pl.BlockSpec((rows, block), lambda i, h: (0, h[0] * steps + i)),
            ],
            out_specs=pl.BlockSpec((width, block), lambda i, h: (0, i)),
        ),
        out_shape=jax.ShapeDtypeStruct((width, columns // 2), F32),
        compiler_params=params(),
        name="lead_product",
    )(half, lead, front)


def dot_high(a, b, dims):
    return lax.dot_general(a, b, (dims, ((), ())), precision=HIGHEST, preferred_element_type=F32)


def invert_factor(block):
    lane = lax.broadcasted_iota(jnp.int32, (8, PB), 1)
    sub = lax.broadcasted_iota(jnp.int32, (8, PB), 0)
    tiles = [block[8 * t : 8 * t + 8, :] for t in range(PB // 8)]
    for j in range(PB):
        home, inner = divmod(j, 8)
        tile = tiles[home]
        row = tile[inner : inner + 1, :]
        inverse = 1.0 / row[:, j : j + 1]
        row = jnp.where(lane[0:1, :] == j, 1.0, row) * inverse
        here = lane == j
        for t in range(home, PB // 8):
            factor = tiles[t][:, j : j + 1]
            cleared = jnp.where(here, 0.0, tiles[t])
            updated = cleared - factor * row
            if t == home:
                updated = jnp.where(sub > inner, updated, tiles[t])
            tiles[t] = updated
    done = []
    for t in range(PB // 8):
        diagonal = lane == sub + 8 * t
        pivot = jnp.sum(jnp.where(diagonal, tiles[t], 0.0), axis=1, keepdims=True)
        scale = lax.rsqrt(pivot)
        scale = scale * (1.5 - 0.5 * pivot * scale * scale)
        unit = jnp.where(diagonal, 1.0, jnp.where(lane < sub + 8 * t, tiles[t], 0.0))
        done.append(unit * scale)
    return jnp.concatenate(done, axis=0)


def eliminate_kernel(k, in_ref, out_ref):
    lo, hi = k * PB, (k + 1) * PB
    inverse = invert_factor(in_ref[lo:hi, lo:hi])
    pieces = []
    for j in range(PANELS):
        if j == k:
            pieces.append(inverse)
        else:
            pieces.append(dot_high(inverse, in_ref[lo:hi, j * PB : (j + 1) * PB], ((1,), (0,))))
    row = jnp.concatenate(pieces, axis=1)
    if k > 0:
        out_ref[:lo, :] = in_ref[:lo, :]
    out_ref[lo:hi, :] = row
    if k < PANELS - 1:
        column = dot_high(in_ref[hi:, lo:hi], inverse, ((1,), (1,)))
        change = dot_high(column, row, ((1,), (0,)))
        out_ref[hi:, :] = in_ref[hi:, :] - change
        out_ref[hi:, lo:hi] = -change[:, lo:hi]


def eliminate(matrix, k):
    return pl.pallas_call(
        functools.partial(eliminate_kernel, k),
        out_shape=jax.ShapeDtypeStruct(matrix.shape, F32),
        in_specs=[pl.BlockSpec(memory_space=VMEM)],
        out_specs=pl.BlockSpec(memory_space=VMEM),
        compiler_params=params(),
        name="eliminate_panel",
    )(matrix)


def project_kernel(has_upper, places_ref, inverse_ref, basis_ref, sums_ref, front_ref, *rest):
    del places_ref
    rest = rest[1:] if has_upper else rest
    upper_ref, out_ref, inverse3, basis3 = rest

    @pl.when(pl.program_id(0) == 0)
    def _():
        for source, held in ((inverse_ref, inverse3), (basis_ref, basis3)):
            hi, lo = parts2(source[...])
            held[...] = jnp.concatenate([hi, hi, lo], axis=1)

    hi, lo = parts2(sums_ref[...])
    upper = jnp.dot(
        inverse3[...], jnp.concatenate([hi, lo, hi], axis=0), preferred_element_type=F32
    )
    upper_ref[...] = upper
    hi, lo = parts2(upper)
    out_ref[...] = front_ref[...] - jnp.dot(
        basis3[...], jnp.concatenate([hi, lo, hi], axis=0), preferred_element_type=F32
    )


def project(places, inverse, basis, sums, front, upper):
    rows, columns = front.shape
    piece = sums.shape[1]
    count = sums.shape[0] // LEAD
    has_upper = upper is not None
    in_specs = [
        pl.BlockSpec((LEAD, LEAD), lambda i, p: (0, 0)),
        pl.BlockSpec((rows, LEAD), lambda i, p: (0, 0)),
        pl.BlockSpec((LEAD, piece), lambda i, p: (i, 0)),
        pl.BlockSpec((rows, piece), lambda i, p: (0, p[i])),
    ]
    operands = [places, inverse, basis, sums, front]
    aliases = {4: 1}
    if has_upper:
        in_specs.append(pl.BlockSpec(memory_space=pl.ANY))
        operands.append(upper)
        aliases[5] = 0
    return pl.pallas_call(
        functools.partial(project_kernel, has_upper),
        grid_spec=pltpu.PrefetchScalarGridSpec(
            num_scalar_prefetch=1,
            grid=(count,),
            in_specs=in_specs,
            out_specs=(
                pl.BlockSpec((LEAD, piece), lambda i, p: (0, p[i])),
                pl.BlockSpec((rows, piece), lambda i, p: (0, p[i])),
            ),
            scratch_shapes=[
                pltpu.VMEM((LEAD, 3 * LEAD), BF16),
                pltpu.VMEM((rows, 3 * LEAD), BF16),
            ],
        ),
        out_shape=(
            jax.ShapeDtypeStruct((LEAD, columns), F32),
            jax.ShapeDtypeStruct((rows, columns), F32),
        ),
        input_output_aliases=aliases,
        compiler_params=params(),
        name="project_columns",
    )(*operands)


def exchange(value, row_count):
    slots, width = value.shape
    shaped = value.reshape(row_count, slots // row_count, width)
    return lax.all_to_all(shaped, "row", split_axis=0, concat_axis=0, tiled=True).reshape(
        slots, width
    )


def on_device(front_matrix, child_rows, child_owner, child_offset):
    row_count = lax.axis_size("row")
    col_count = lax.axis_size("col")
    local_rows, local_cols = front_matrix.shape
    child_count = child_rows.shape[0]
    capacity = 2 * child_count // row_count
    me = lax.axis_index("row")

    packed, tags = pack(
        child_rows, child_owner[:, 0], child_offset[:, 0], row_count, capacity, local_rows
    )
    lead_child = exchange(jnp.concatenate([packed[:, :LEAD], tags], axis=1), row_count)
    tags = lead_child[:, LEAD:]
    all_child = exchange(packed, row_count)
    own_lead = assemble(front_matrix, lead_child, tags, LEAD, LEAD)
    panels = [spread(own_lead[:, k * PB : (k + 1) * PB], col_count) for k in range(PANELS)]
    lead = jnp.concatenate(panels, axis=1)

    gram = total_rows(dot_high(lead, lead, ((0,), (0,))), row_count)
    for k in range(PANELS):
        gram = eliminate(gram, k)
    block_row = np.arange(LEAD) // PB
    inverse = jnp.where(block_row[:, None] >= block_row[None, :], gram, 0.0)
    basis = dot_high(lead, inverse, ((1,), (1,)))

    front = assemble(front_matrix, all_child, tags, local_cols, 512)
    side = upper_side(0, row_count)
    shards = []
    for g in range(LEAD // GROUP):
        group = jnp.concatenate(panels[g * GROUP // PB : (g + 1) * GROUP // PB], axis=1)
        send = lead_product((1 - side)[None], group, front, 512)
        keep = lead_product(side[None], group, front, 512)
        shards.append(scatter_sum(keep, send, 1, row_count))
    shard = jnp.concatenate(shards, axis=0)

    width = shard.shape[1]
    piece = min(256, width)
    chunks = width // piece
    places = jnp.asarray(piece_table(row_count))[me] * chunks
    steps = row_count.bit_length() - 1
    held = []
    for c in range(chunks):
        buf = shard[:, c * piece : (c + 1) * piece]
        for step in reversed(range(steps)):
            got = swap(buf, step, row_count)
            if step == 0:
                held.append((buf, got))
            else:
                buf = jnp.concatenate([buf, got], axis=0)
    upper = None
    for c in range(chunks):
        near = places + c
        for sums, at in zip(held[c], (near[: row_count // 2], near[row_count // 2 :])):
            upper, front = project(at, inverse, basis, sums, front, upper)
    return upper, front, basis * math.sqrt(local_rows * row_count)


def solution(mesh):
    placed = (P("row", "col"), P("row", "col"), P("row", None), P("row", None))
    return jax.shard_map(
        on_device,
        mesh=mesh,
        in_specs=placed,
        out_specs=(P(None, "col"), P("row", "col"), P("row", None)),
        check_vma=False,
    )
```

```python
import functools
import math

import jax
import jax.numpy as jnp
import numpy as np
from jax import lax
from jax.experimental import pallas as pl
from jax.experimental.pallas import tpu as pltpu
from jax.sharding import PartitionSpec as P

PB = 128
PANELS = 4
LEAD = PB * PANELS
HALF = LEAD // 2
BLOCK = 256
VMEM_BYTES = 24 * 1024 * 1024
HIGHEST = lax.Precision.HIGHEST
F32 = jnp.float32
BF16 = jnp.bfloat16
SMEM = pltpu.SMEM
VMEM = pltpu.VMEM


def params():
    return pltpu.CompilerParams(vmem_limit_bytes=VMEM_BYTES)


def cost(flops):
    return pl.CostEstimate(flops=flops, bytes_accessed=1 << 20, transcendentals=0)


def mask_orders(count):
    others = [1 << b for b in range(1, count.bit_length() - 1)]
    half = len(others) // 2
    return ([1] + others, [1] + others[half:] + others[:half])


def swap(value, step, count):
    orders = mask_orders(count)
    pairs = [(d, d ^ orders[d & 1][step]) for d in range(count)]
    return lax.ppermute(value, "row", pairs)


def upper_side(step, count):
    orders = mask_orders(count)
    me = lax.axis_index("row")
    mask = jnp.where(me & 1 == 0, orders[0][step], orders[1][step])
    return ((me & mask) != 0).astype(jnp.int32)


def shard_table(count):
    orders = mask_orders(count)
    steps = len(orders[0])
    return np.array(
        [
            sum(((d & orders[d & 1][t]) != 0) << (steps - 1 - t) for t in range(steps))
            for d in range(count)
        ]
    )


def piece_order(count):
    orders = mask_orders(count)
    steps = len(orders[0])
    shard = shard_table(count)

    def pieces(device, done):
        if done == 0:
            return [device]
        mask = orders[device & 1][steps - done]
        return pieces(device, done - 1) + pieces(device ^ mask, done - 1)

    half = count // 2
    order = np.zeros((count, 2, half), np.int32)
    for d in range(count):
        for at, piece in enumerate(pieces(d, steps)):
            order[d, at // half, shard[piece] % half] = at % half
    return order


def split_add_kernel(side_ref, keep_ref, got_ref, keep_out, send_out):
    half = keep_out.shape[1]
    for which, out in ((side_ref[0], keep_out), (1 - side_ref[0], send_out)):
        part = pl.ds(pl.multiple_of(which * half, 128), half)
        out[...] = keep_ref[:, part] + got_ref[:, part]


def split_add(side, keep, got):
    half = jax.ShapeDtypeStruct((keep.shape[0], keep.shape[1] // 2), F32)
    return pl.pallas_call(
        split_add_kernel,
        out_shape=(half, half),
        in_specs=[
            pl.BlockSpec(memory_space=SMEM),
            pl.BlockSpec(memory_space=VMEM),
            pl.BlockSpec(memory_space=VMEM),
        ],
        out_specs=(pl.BlockSpec(memory_space=VMEM), pl.BlockSpec(memory_space=VMEM)),
        compiler_params=params(),
        name="split_add",
    )(side[None], keep, got)


def scatter_sum(keep, send, count):
    steps = count.bit_length() - 1
    for step in range(steps):
        got = swap(send, step, count)
        if step == steps - 1:
            return keep + got
        keep, send = split_add(upper_side(step + 1, count), keep, got)


def total(value, count):
    side = upper_side(0, count)
    half = value.shape[0] // 2
    keep = lax.dynamic_slice_in_dim(value, side * half, half, 0)
    send = lax.dynamic_slice_in_dim(value, (1 - side) * half, half, 0)
    mine = keep + swap(send, 0, count)
    for step in range(1, count.bit_length() - 1):
        mine = mine + swap(mine, step, count)
    got = swap(mine, 0, count)
    return jnp.where(
        side == 0,
        jnp.concatenate([mine, got], axis=0),
        jnp.concatenate([got, mine], axis=0),
    )


def spread(value, count):
    me = lax.axis_index("col")
    stride = count
    while stride > 1:
        half = stride // 2
        pairs = [(c, c + half) for c in range(0, count, stride)]
        got = lax.ppermute(value, "col", pairs)
        value = jnp.where(me % stride == half, got, value)
        stride = half
    return value


def parts3(x):
    hi = x.astype(BF16)
    rest = x - hi.astype(F32)
    mid = rest.astype(BF16)
    return hi, mid, (rest - mid.astype(F32)).astype(BF16)


def parts2(x):
    hi = x.astype(BF16)
    return hi, (x - hi.astype(F32)).astype(BF16)


def pack_kernel(row_count, capacity, sentinel, owner_ref, offset_ref, child_ref, out_ref, tag_ref, tally):
    out_ref[...] = jnp.zeros_like(out_ref)
    tag_ref[...] = jnp.full(tag_ref.shape, sentinel, F32)
    for d in range(row_count):
        tally[d] = 0

    def body(i, carry):
        owner = owner_ref[i]
        rank = tally[owner]
        tally[owner] = rank + 1
        slot = owner * capacity + rank
        out_ref[pl.ds(slot, 1), :] = child_ref[pl.ds(i, 1), :]
        tag_ref[pl.ds(slot, 1), :] = jnp.full((1, tag_ref.shape[1]), offset_ref[i].astype(F32))
        return carry

    lax.fori_loop(0, child_ref.shape[0], body, 0)


def pack(child_rows, owner, offset, row_count, capacity, sentinel):
    slots = row_count * capacity
    return pl.pallas_call(
        functools.partial(pack_kernel, row_count, capacity, float(sentinel)),
        out_shape=(
            jax.ShapeDtypeStruct((slots, child_rows.shape[1]), F32),
            jax.ShapeDtypeStruct((slots, PB), F32),
        ),
        in_specs=[
            pl.BlockSpec(memory_space=SMEM),
            pl.BlockSpec(memory_space=SMEM),
            pl.BlockSpec(memory_space=VMEM),
        ],
        out_specs=(pl.BlockSpec(memory_space=VMEM), pl.BlockSpec(memory_space=VMEM)),
        scratch_shapes=[pltpu.SMEM((row_count,), jnp.int32)],
        compiler_params=params(),
        name="pack_children",
    )(owner, offset, child_rows)


def triple(x, axis):
    hi, lo = parts2(x)
    return jnp.concatenate([hi, hi, lo] if axis == 1 else [hi, lo, hi], axis=axis)


def lead_kernel(front_ref, child_ref, tag_ref, lead_ref, left_ref, place_ref, gram_ref):
    rows = front_ref.shape[0]
    slots = child_ref.shape[0]
    place = jnp.transpose(tag_ref[...])[0:1, :]
    at = lax.broadcasted_iota(jnp.int32, (rows, slots), 0).astype(F32)
    onehot = jnp.where(at == place, 1.0, 0.0).astype(BF16)
    spots = jnp.concatenate([onehot, onehot, onehot], axis=1)
    place_ref[...] = spots
    parts = jnp.concatenate(parts3(child_ref[...])[::-1], axis=0)
    lead = front_ref[...] + jnp.dot(spots, parts, preferred_element_type=F32)
    lead_ref[...] = lead
    turned = jnp.transpose(lead)
    left_ref[...] = triple(turned, 1)
    gram_ref[:, :HALF] = dot_high(turned[:HALF], lead[:, :HALF], ((1,), (0,)))
    gram_ref[:, HALF:] = dot_high(turned[HALF:], lead, ((1,), (0,)))


def lead_setup(front, child, tags):
    rows = front.shape[0]
    slots = child.shape[0]
    return pl.pallas_call(
        lead_kernel,
        out_shape=(
            jax.ShapeDtypeStruct((rows, LEAD), F32),
            jax.ShapeDtypeStruct((LEAD, 3 * rows), BF16),
            jax.ShapeDtypeStruct((rows, 3 * slots), BF16),
            jax.ShapeDtypeStruct((HALF, LEAD + HALF), F32),
        ),
        in_specs=[pl.BlockSpec(memory_space=VMEM)] * 3,
        out_specs=(pl.BlockSpec(memory_space=VMEM),) * 4,
        compiler_params=params(),
        name="lead_setup",
    )(front, child, tags)


def product_kernel(has_front, base_ref, left_ref, place_ref, front_ref, child_ref, *rest):
    del base_ref
    out_ref, whole_ref = rest[1:] if has_front else rest
    parts = jnp.concatenate(parts3(child_ref[...])[::-1], axis=0)
    whole = front_ref[...] + jnp.dot(place_ref[...], parts, preferred_element_type=F32)
    whole_ref[...] = whole
    out_ref[...] = jnp.dot(left_ref[...], triple(whole, 0), preferred_element_type=F32)


def product(base, left, place, front, child, whole, width):
    rows, columns = front.shape
    slots = child.shape[0]
    has_front = whole is not None
    in_specs = [
        pl.BlockSpec(left.shape, lambda i, b: (0, 0)),
        pl.BlockSpec(place.shape, lambda i, b: (0, 0)),
        pl.BlockSpec((rows, BLOCK), lambda i, b: (0, b[0] + i)),
        pl.BlockSpec((slots, BLOCK), lambda i, b: (0, b[0] + i)),
    ]
    operands = [base[None], left, place, front, child]
    aliases = {}
    if has_front:
        in_specs.append(pl.BlockSpec(memory_space=pl.ANY))
        operands.append(whole)
        aliases = {5: 1}
    return pl.pallas_call(
        functools.partial(product_kernel, has_front),
        grid_spec=pltpu.PrefetchScalarGridSpec(
            num_scalar_prefetch=1,
            grid=(width // BLOCK,),
            in_specs=in_specs,
            out_specs=(
                pl.BlockSpec((LEAD, BLOCK), lambda i, b: (0, i)),
                pl.BlockSpec((rows, BLOCK), lambda i, b: (0, b[0] + i)),
            ),
        ),
        out_shape=(
            jax.ShapeDtypeStruct((LEAD, width), F32),
            jax.ShapeDtypeStruct((rows, columns), F32),
        ),
        input_output_aliases=aliases,
        compiler_params=params(),
        name="lead_product",
    )(*operands)


def dot_high(a, b, dims):
    return lax.dot_general(a, b, (dims, ((), ())), precision=HIGHEST, preferred_element_type=F32)


def spread_lane(tile, at):
    return jnp.broadcast_to(tile[:, at : at + 1], tile.shape)


def invert_factor(block):
    lane = lax.broadcasted_iota(jnp.int32, (8, PB), 1)
    sub = lax.broadcasted_iota(jnp.int32, (8, PB), 0)
    count = PB // 8
    tiles = [block[8 * t : 8 * t + 8, :] for t in range(count)]
    for b in range(count):
        first = 8 * b
        rows = tiles[b]
        cols = [spread_lane(rows, first + c) for c in range(8)]
        heads, inverses = {}, []
        for c in range(8):
            inverse = 1.0 / cols[c][c : c + 1, :]
            inverses.append(inverse)
            factor = jnp.where(sub > c, cols[c] * inverse, 0.0)
            here = lane == first + c
            source = jnp.where(here[0:1, :], 1.0, rows[c : c + 1, :])
            rows = jnp.where(here & (sub > c), 0.0, rows) - factor * source
            for d in range(c + 1, 8):
                heads[c, d] = cols[d][c : c + 1, :]
                cols[d] = cols[d] - factor * heads[c, d]
        tiles[b] = rows
        inside = (lane >= first) & (lane < first + 8)
        past = inside & (lane - first >= sub)
        used = jnp.where(past, jnp.where(lane - first == sub, 1.0, 0.0), rows)
        for t in range(b + 1, count):
            tile = tiles[t]
            factors = []
            for c in range(8):
                factor = spread_lane(tile, first + c)
                for d in range(c):
                    factor = factor - factors[d] * heads[d, c]
                factors.append(factor * inverses[c])
            tile = jnp.where(inside, 0.0, tile)
            for c in range(8):
                tile = tile - factors[c] * used[c : c + 1, :]
            tiles[t] = tile
    done = []
    for t in range(count):
        diagonal = lane == sub + 8 * t
        pivot = jnp.sum(jnp.where(diagonal, tiles[t], 0.0), axis=1, keepdims=True)
        scale = lax.rsqrt(pivot)
        scale = scale * (1.5 - 0.5 * pivot * scale * scale)
        unit = jnp.where(diagonal, 1.0, jnp.where(lane < sub + 8 * t, tiles[t], 0.0))
        done.append(unit * scale)
    return jnp.concatenate(done, axis=0)


def eliminate_kernel(k, in_ref, out_ref):
    lo, hi = k * PB, (k + 1) * PB
    if k == 0:
        cross = in_ref[:, HALF:LEAD]
        out_ref[:HALF, :HALF] = in_ref[:, :HALF]
        out_ref[HALF:, :HALF] = cross
        out_ref[:HALF, HALF:] = jnp.transpose(cross)
        out_ref[HALF:, HALF:] = in_ref[:, LEAD:]
        in_ref = out_ref
    else:
        out_ref[:lo, :] = in_ref[:lo, :]
    inverse = invert_factor(in_ref[lo:hi, lo:hi])
    pieces = []
    for j in range(PANELS):
        if j == k:
            pieces.append(inverse)
        else:
            pieces.append(dot_high(inverse, in_ref[lo:hi, j * PB : (j + 1) * PB], ((1,), (0,))))
    row = jnp.concatenate(pieces, axis=1)
    out_ref[lo:hi, :] = row
    if k < PANELS - 1:
        column = dot_high(in_ref[hi:, lo:hi], inverse, ((1,), (1,)))
        change = dot_high(column, row, ((1,), (0,)))
        later = in_ref[hi:, :]
        out_ref[hi:, :] = later - change
        out_ref[hi:, lo:hi] = -change[:, lo:hi]


def eliminate(matrix, k):
    return pl.pallas_call(
        functools.partial(eliminate_kernel, k),
        out_shape=jax.ShapeDtypeStruct((LEAD, LEAD), F32),
        in_specs=[pl.BlockSpec(memory_space=VMEM)],
        out_specs=pl.BlockSpec(memory_space=VMEM),
        compiler_params=params(),
        cost_estimate=cost(6 * 10**9),
        name="eliminate_panel",
    )(matrix)


def finish_kernel(scale, matrix_ref, lead_ref, top_ref, bottom_ref, basis3_ref, basis_ref):
    own = lax.broadcasted_iota(jnp.int32, (LEAD, LEAD), 0) // PB
    other = lax.broadcasted_iota(jnp.int32, (LEAD, LEAD), 1) // PB
    inverse = jnp.where(own >= other, matrix_ref[...], 0.0)
    top_ref[...] = triple(inverse[:HALF, :HALF], 1)
    bottom_ref[...] = triple(inverse[HALF:], 1)
    basis = dot_high(lead_ref[...], inverse, ((1,), (1,)))
    basis3_ref[...] = triple(basis, 1)
    basis_ref[...] = basis * scale


def finish(matrix, lead, scale):
    rows = lead.shape[0]
    return pl.pallas_call(
        functools.partial(finish_kernel, scale),
        out_shape=(
            jax.ShapeDtypeStruct((HALF, 3 * HALF), BF16),
            jax.ShapeDtypeStruct((HALF, 3 * LEAD), BF16),
            jax.ShapeDtypeStruct((rows, 3 * LEAD), BF16),
            jax.ShapeDtypeStruct((rows, LEAD), F32),
        ),
        in_specs=[pl.BlockSpec(memory_space=VMEM)] * 2,
        out_specs=(pl.BlockSpec(memory_space=VMEM),) * 4,
        compiler_params=params(),
        cost_estimate=cost(2 * 10**9),
        name="finish_factor",
    )(matrix, lead)


def project_kernel(has_upper, places_ref, top_ref, bottom_ref, basis_ref, *rest):
    del places_ref
    even_ref, odd_ref, front_ref = rest[:3]
    upper_ref, out_ref = rest[4 if has_upper else 3 :]
    sums = jnp.concatenate([even_ref[...], odd_ref[...]], axis=1)
    hi, lo = parts2(sums)
    upper_ref[:HALF, :] = jnp.dot(
        top_ref[...],
        jnp.concatenate([hi[:HALF], lo[:HALF], hi[:HALF]], axis=0),
        preferred_element_type=F32,
    )
    upper_ref[HALF:, :] = jnp.dot(
        bottom_ref[...], jnp.concatenate([hi, lo, hi], axis=0), preferred_element_type=F32
    )
    out_ref[...] = front_ref[...] - jnp.dot(
        basis_ref[...], triple(upper_ref[...], 0), preferred_element_type=F32
    )


def project(places, factor, sums, front, upper):
    top, bottom, basis = factor
    rows, columns = front.shape
    count = sums.shape[0] // LEAD
    has_upper = upper is not None
    in_specs = [
        pl.BlockSpec(top.shape, lambda i, p: (0, 0)),
        pl.BlockSpec(bottom.shape, lambda i, p: (0, 0)),
        pl.BlockSpec(basis.shape, lambda i, p: (0, 0)),
        pl.BlockSpec((LEAD, PB), lambda i, p: (p[1 + 2 * i], 0)),
        pl.BlockSpec((LEAD, PB), lambda i, p: (p[2 + 2 * i], 0)),
        pl.BlockSpec((rows, BLOCK), lambda i, p: (0, p[0] + i)),
    ]
    operands = [places, top, bottom, basis, sums, sums, front]
    aliases = {6: 1}
    if has_upper:
        in_specs.append(pl.BlockSpec(memory_space=pl.ANY))
        operands.append(upper)
        aliases[7] = 0
    return pl.pallas_call(
        functools.partial(project_kernel, has_upper),
        grid_spec=pltpu.PrefetchScalarGridSpec(
            num_scalar_prefetch=1,
            grid=(count // 2,),
            in_specs=in_specs,
            out_specs=(
                pl.BlockSpec((LEAD, BLOCK), lambda i, p: (0, p[0] + i)),
                pl.BlockSpec((rows, BLOCK), lambda i, p: (0, p[0] + i)),
            ),
        ),
        out_shape=(
            jax.ShapeDtypeStruct((LEAD, columns), F32),
            jax.ShapeDtypeStruct((rows, columns), F32),
        ),
        input_output_aliases=aliases,
        compiler_params=params(),
        cost_estimate=cost(3 * 10**9),
        name="project_columns",
    )(*operands)


def exchange(value, row_count):
    slots, width = value.shape
    shaped = value.reshape(row_count, slots // row_count, width)
    return lax.all_to_all(shaped, "row", split_axis=0, concat_axis=0, tiled=True).reshape(
        slots, width
    )


def on_device(front_matrix, child_rows, child_owner, child_offset):
    row_count = lax.axis_size("row")
    col_count = lax.axis_size("col")
    local_rows, local_cols = front_matrix.shape
    child_count = child_rows.shape[0]
    capacity = 2 * child_count // row_count
    me = lax.axis_index("row")

    owner, offset = child_owner[:, 0], child_offset[:, 0]
    lead_child = spread(child_rows[:, :LEAD], col_count)
    cut = local_rows // 2
    lead_front = jnp.concatenate(
        [
            spread(front_matrix[:cut, :LEAD], col_count),
            spread(front_matrix[cut:, :LEAD], col_count),
        ],
        axis=0,
    )
    packed, tags = pack(child_rows, owner, offset, row_count, capacity, local_rows)
    child = exchange(packed, row_count)
    packed, tags = pack(lead_child, owner, offset, row_count, capacity, local_rows)
    lead_child = exchange(jnp.concatenate([packed, tags], axis=1), row_count)
    lead, left, place, gram = lead_setup(lead_front, lead_child[:, :LEAD], lead_child[:, LEAD:])

    matrix = total(gram, row_count)
    for k in range(PANELS):
        matrix = eliminate(matrix, k)
    scale = math.sqrt(local_rows * row_count)
    top, bottom, basis, scaled = finish(matrix, lead, scale)

    chunks = max(1, min(4, local_cols // (PB * row_count)))
    width = local_cols // 2 // chunks
    blocks = width // BLOCK
    core = upper_side(0, row_count)
    front = None
    shards = []
    for c in range(chunks):
        made = []
        for half in (1 - core, core):
            base = (half * chunks + c) * blocks
            sums, front = product(base, left, place, front_matrix, child, front, width)
            made.append(sums)
        shards.append(scatter_sum(made[1], made[0], row_count))
    steps = row_count.bit_length() - 1
    held = []
    for c in range(chunks):
        buf = shards[c]
        for step in reversed(range(steps)):
            got = swap(buf, step, row_count)
            if step == 0:
                held.append((buf, got))
            else:
                buf = jnp.concatenate([buf, got], axis=0)
    order = jnp.asarray(piece_order(row_count))[me]
    upper = None
    for c in range(chunks):
        for which, half in enumerate((core, 1 - core)):
            base = (half * chunks + c) * blocks
            places = jnp.concatenate([base[None], order[which]])
            upper, front = project(places, (top, bottom, basis), held[c][which], front, upper)
    return upper, front, scaled


def solution(mesh):
    placed = (P("row", "col"), P("row", "col"), P("row", None), P("row", None))
    return jax.shard_map(
        on_device,
        mesh=mesh,
        in_specs=placed,
        out_specs=(P(None, "col"), P("row", "col"), P("row", None)),
        check_vma=False,
    )
```

```python
import functools
import math

import jax
import jax.numpy as jnp
import numpy as np
from jax import lax
from jax.experimental import pallas as pl
from jax.experimental.pallas import tpu as pltpu
from jax.sharding import PartitionSpec as P

PB = 128
PANELS = 4
LEAD = PB * PANELS
HALF = LEAD // 2
BLOCK = 256
VMEM_BYTES = 24 * 1024 * 1024
HIGHEST = lax.Precision.HIGHEST
F32 = jnp.float32
BF16 = jnp.bfloat16
WHOLE = pl.BlockSpec(memory_space=pltpu.VMEM)
SCALARS = pl.BlockSpec(memory_space=pltpu.SMEM)
ANYWHERE = pl.BlockSpec(memory_space=pl.ANY)


def f32(*shape):
    return jax.ShapeDtypeStruct(shape, F32)


def bf16(*shape):
    return jax.ShapeDtypeStruct(shape, BF16)


class Chain:
    def __init__(self):
        self.token = None

    def __call__(self, name, body, operands, in_specs, outs, out_specs, scalars=(), grid=None, aliases=None):
        taken = len(scalars) + len(operands)
        given = len(outs)
        has_token = self.token is not None
        operands, in_specs = list(operands), list(in_specs)
        if has_token:
            operands.append(self.token)
            in_specs.append(ANYWHERE)

        def kernel(*refs):
            ins, rest = refs[:taken], refs[taken + has_token :]
            rest[given][...] = jnp.zeros((8, PB), F32)
            body(*ins, *rest[:given])

        token_spec = WHOLE if grid is None else pl.BlockSpec((8, PB), lambda *at: (0, 0))
        settings = dict(
            out_shape=tuple(outs) + (f32(8, PB),),
            input_output_aliases=aliases or {},
            compiler_params=pltpu.CompilerParams(vmem_limit_bytes=VMEM_BYTES),
            cost_estimate=pl.CostEstimate(flops=1 << 20, bytes_accessed=1 << 16, transcendentals=0),
            name=name,
        )
        out_specs = tuple(out_specs) + (token_spec,)
        if grid is None:
            settings.update(in_specs=in_specs, out_specs=out_specs)
        else:
            settings.update(
                grid_spec=pltpu.PrefetchScalarGridSpec(
                    num_scalar_prefetch=len(scalars),
                    grid=grid,
                    in_specs=in_specs,
                    out_specs=out_specs,
                )
            )
        results = pl.pallas_call(kernel, **settings)(*scalars, *operands)
        self.token = results[-1]
        return results[:-1] if given > 1 else results[0]


def mask_orders(count):
    others = [1 << b for b in range(1, count.bit_length() - 1)]
    half = len(others) // 2
    return ([1] + others, [1] + others[half:] + others[:half])


def swap(value, step, count):
    orders = mask_orders(count)
    pairs = [(d, d ^ orders[d & 1][step]) for d in range(count)]
    return lax.ppermute(value, "row", pairs)


def upper_side(step, count):
    orders = mask_orders(count)
    me = lax.axis_index("row")
    mask = jnp.where(me % 2 == 0, orders[0][step], orders[1][step])
    return ((me & mask) != 0).astype(jnp.int32)


def shard_table(count):
    orders = mask_orders(count)
    steps = len(orders[0])
    return np.array(
        [
            sum(((d & orders[d & 1][t]) != 0) << (steps - 1 - t) for t in range(steps))
            for d in range(count)
        ]
    )


def piece_order(count):
    orders = mask_orders(count)
    steps = len(orders[0])
    shard = shard_table(count)

    def pieces(device, done):
        if done == 0:
            return [device]
        mask = orders[device & 1][steps - done]
        return pieces(device, done - 1) + pieces(device ^ mask, done - 1)

    half = count // 2
    order = np.zeros((count, 2, half), np.int32)
    for d in range(count):
        for at, piece in enumerate(pieces(d, steps)):
            order[d, at // half, shard[piece] % half] = at % half
    return order


def spread(value, count):
    middle = count // 2
    first = lax.ppermute(value, "col", [(0, middle)])
    others = [c for c in range(count - 1, 0, -1) if c != middle]
    return [first] + [lax.ppermute(first, "col", [(middle, c)]) for c in others]


def exchange(value, row_count):
    slots, width = value.shape
    shaped = value.reshape(row_count, slots // row_count, width)
    return lax.all_to_all(shaped, "row", split_axis=0, concat_axis=0, tiled=True).reshape(
        slots, width
    )


def parts3(x):
    hi = x.astype(BF16)
    rest = x - hi.astype(F32)
    mid = rest.astype(BF16)
    return hi, mid, (rest - mid.astype(F32)).astype(BF16)


def parts2(x):
    hi = x.astype(BF16)
    return hi, (x - hi.astype(F32)).astype(BF16)


def triple(x, axis):
    hi, lo = parts2(x)
    return jnp.concatenate([hi, hi, lo] if axis == 1 else [hi, lo, hi], axis=axis)


def dot_high(a, b, dims):
    return lax.dot_general(a, b, (dims, ((), ())), precision=HIGHEST, preferred_element_type=F32)


def dot(a, b):
    return jnp.dot(a, b, preferred_element_type=F32)


def pick(own, gots):
    arrived = gots[0][...]
    for got in gots[1:]:
        arrived = arrived + got[...]
    return jnp.where(lax.axis_index("col") == 0, own[...], arrived)


def cut_body(child_ref, front_ref, *outs):
    at = 0
    stacked = [(child_ref, child_ref.shape[0]), (front_ref, front_ref.shape[0])]
    starts = [0, child_ref.shape[0]]
    for out in outs:
        for (ref, length), start in zip(stacked, starts):
            lo, hi = max(at, start), min(at + out.shape[0], start + length)
            if lo < hi:
                out[lo - at : hi - at, :] = ref[lo - start : hi - start, :]
        at += out.shape[0]


def place_rows(row_count, capacity, owner_ref, read, write, width, child_count):
    def body(i, counts):
        owner = owner_ref[i]
        rank = jnp.int32(0)
        for d in range(row_count):
            rank = jnp.where(owner == d, counts[d], rank)
        write(owner * capacity + rank, read(i), i)
        return tuple(counts[d] + (owner == d).astype(jnp.int32) for d in range(row_count))

    lax.fori_loop(0, child_count, body, (jnp.int32(0),) * row_count)


def pack_body(row_count, capacity, owner_ref, child_ref, out_ref):
    out_ref[...] = jnp.zeros_like(out_ref)

    def write(slot, row, i):
        out_ref[pl.ds(slot, 1), :] = row

    place_rows(
        row_count, capacity, owner_ref, lambda i: child_ref[pl.ds(i, 1), :], write,
        out_ref.shape[1], child_ref.shape[0],
    )


def pack_lead_body(row_count, capacity, sentinel, child_count, owner_ref, offset_ref, *refs):
    own, gots = refs[0], refs[1:-4]
    out_ref, child_ref, rows_ref, tag_ref = refs[-4:]
    child_ref[...] = pick(own, gots)
    rows_ref[...] = jnp.zeros_like(rows_ref)
    tag_ref[...] = jnp.full(tag_ref.shape, sentinel, F32)

    def write(slot, row, i):
        rows_ref[pl.ds(slot, 1), :] = row
        tag_ref[pl.ds(slot, 1), :] = jnp.full((1, PB), offset_ref[i].astype(F32))

    place_rows(
        row_count, capacity, owner_ref, lambda i: child_ref[pl.ds(i, 1), :], write,
        LEAD, child_count,
    )
    out_ref[:, :LEAD] = rows_ref[...]
    out_ref[:, LEAD:] = tag_ref[...]


def lead_body(child_count, chunk_count, *refs):
    each = (len(refs) - 6) // chunk_count
    chunks = [refs[i * each : (i + 1) * each] for i in range(chunk_count)]
    slots_ref = refs[each * chunk_count]
    lead_ref, left_ref, place_ref, keep_ref, send_ref = refs[each * chunk_count + 1 :]
    front = jnp.concatenate([pick(c[0], c[1:]) for c in chunks], axis=0)[child_count:]
    rows, slots = front.shape[0], slots_ref.shape[0]
    place = jnp.transpose(slots_ref[:, LEAD:])[0:1, :]
    at = lax.broadcasted_iota(jnp.int32, (rows, slots), 0).astype(F32)
    onehot = jnp.where(at == place, 1.0, 0.0).astype(BF16)
    spots = jnp.concatenate([onehot, onehot, onehot], axis=1)
    place_ref[...] = spots
    lead = front + dot(spots, jnp.concatenate(parts3(slots_ref[:, :LEAD])[::-1], axis=0))
    lead_ref[...] = lead
    turned = jnp.transpose(lead)
    left_ref[...] = triple(turned, 1)
    first = dot_high(turned[:HALF], lead[:, :HALF], ((1,), (0,)))
    second = dot_high(turned[HALF:], lead, ((1,), (0,)))
    side = lax.axis_index("row") % 2 == 0
    for out, flip in ((keep_ref, False), (send_ref, True)):
        low = jnp.logical_xor(side, flip)
        out[:, :HALF] = jnp.where(low, first[:PB], first[PB:])
        out[:, HALF:] = jnp.where(low, second[:PB], second[PB:])


def add_body(a_ref, b_ref, out_ref):
    out_ref[...] = a_ref[...] + b_ref[...]


def join_body(a_ref, b_ref, out_ref):
    half = a_ref.shape[0]
    out_ref[:half, :] = a_ref[...]
    out_ref[half:, :] = b_ref[...]


def split_add_body(step, count, keep_ref, got_ref, keep_out, send_out):
    half = keep_out.shape[1]
    side = upper_side(step, count)
    for which, out in ((side, keep_out), (1 - side, send_out)):
        part = pl.ds(pl.multiple_of(which * half, 128), half)
        out[...] = keep_ref[:, part] + got_ref[:, part]


def product_body(blocks, halves, base_ref, left_ref, place_ref, front_ref, child_ref, *rest):
    del base_ref
    outs, whole_ref = rest[-1 - halves : -1], rest[-1]
    parts = jnp.concatenate(parts3(child_ref[...])[::-1], axis=0)
    whole = front_ref[...] + dot(place_ref[...], parts)
    whole_ref[...] = whole
    result = dot(left_ref[...], triple(whole, 0))
    if halves == 1:
        outs[0][...] = result
    else:
        first = pl.program_id(0) < blocks

        @pl.when(first)
        def _():
            outs[0][...] = result

        @pl.when(jnp.logical_not(first))
        def _():
            outs[1][...] = result


def spread_lane(tile, at):
    return jnp.broadcast_to(tile[:, at : at + 1], tile.shape)


def invert_factor(block):
    lane = lax.broadcasted_iota(jnp.int32, (8, PB), 1)
    sub = lax.broadcasted_iota(jnp.int32, (8, PB), 0)
    count = PB // 8
    tiles = [block[8 * t : 8 * t + 8, :] for t in range(count)]
    for b in range(count):
        first = 8 * b
        rows = tiles[b]
        cols = [spread_lane(rows, first + c) for c in range(8)]
        heads, inverses = {}, []
        for c in range(8):
            inverse = 1.0 / cols[c][c : c + 1, :]
            inverses.append(inverse)
            factor = jnp.where(sub > c, cols[c] * inverse, 0.0)
            here = lane == first + c
            source = jnp.where(here[0:1, :], 1.0, rows[c : c + 1, :])
            rows = jnp.where(here & (sub > c), 0.0, rows) - factor * source
            for d in range(c + 1, 8):
                heads[c, d] = cols[d][c : c + 1, :]
                cols[d] = cols[d] - factor * heads[c, d]
        tiles[b] = rows
        inside = (lane >= first) & (lane < first + 8)
        past = inside & (lane - first >= sub)
        used = jnp.where(past, jnp.where(lane - first == sub, 1.0, 0.0), rows)
        for t in range(b + 1, count):
            tile = tiles[t]
            factors = []
            for c in range(8):
                factor = spread_lane(tile, first + c)
                for d in range(c):
                    factor = factor - factors[d] * heads[d, c]
                factors.append(factor * inverses[c])
            tile = jnp.where(inside, 0.0, tile)
            for c in range(8):
                tile = tile - factors[c] * used[c : c + 1, :]
            tiles[t] = tile
    done = []
    for t in range(count):
        diagonal = lane == sub + 8 * t
        pivot = jnp.sum(jnp.where(diagonal, tiles[t], 0.0), axis=1, keepdims=True)
        scale = lax.rsqrt(pivot)
        scale = scale * (1.5 - 0.5 * pivot * scale * scale)
        unit = jnp.where(diagonal, 1.0, jnp.where(lane < sub + 8 * t, tiles[t], 0.0))
        done.append(unit * scale)
    return jnp.concatenate(done, axis=0)


def eliminate_body(k, *refs):
    out_ref = refs[-1]
    lo, hi = k * PB, (k + 1) * PB
    if k == 0:
        mine, got = refs[0][...], refs[1][...]
        low = lax.axis_index("row") % 2 == 0
        packed = jnp.concatenate([jnp.where(low, mine, got), jnp.where(low, got, mine)], axis=0)
        cross = packed[:, HALF:LEAD]
        out_ref[:HALF, :HALF] = packed[:, :HALF]
        out_ref[HALF:, :HALF] = cross
        out_ref[:HALF, HALF:] = jnp.transpose(cross)
        out_ref[HALF:, HALF:] = packed[:, LEAD:]
        in_ref = out_ref
    else:
        in_ref = refs[0]
        out_ref[:lo, :] = in_ref[:lo, :]
    inverse = invert_factor(in_ref[lo:hi, lo:hi])
    pieces = []
    for j in range(PANELS):
        if j == k:
            pieces.append(inverse)
        else:
            pieces.append(dot_high(inverse, in_ref[lo:hi, j * PB : (j + 1) * PB], ((1,), (0,))))
    row = jnp.concatenate(pieces, axis=1)
    out_ref[lo:hi, :] = row
    if k < PANELS - 1:
        column = dot_high(in_ref[hi:, lo:hi], inverse, ((1,), (1,)))
        change = dot_high(column, row, ((1,), (0,)))
        later = in_ref[hi:, :]
        out_ref[hi:, :] = later - change
        out_ref[hi:, lo:hi] = -change[:, lo:hi]


def finish_body(scale, matrix_ref, lead_ref, top_ref, bottom_ref, basis3_ref, basis_ref):
    own = lax.broadcasted_iota(jnp.int32, (LEAD, LEAD), 0) // PB
    other = lax.broadcasted_iota(jnp.int32, (LEAD, LEAD), 1) // PB
    inverse = jnp.where(own >= other, matrix_ref[...], 0.0)
    top_ref[...] = triple(inverse[:HALF, :HALF], 1)
    bottom_ref[...] = triple(inverse[HALF:], 1)
    basis = dot_high(lead_ref[...], inverse, ((1,), (1,)))
    basis3_ref[...] = triple(basis, 1)
    basis_ref[...] = basis * scale


def project_body(blocks, places_ref, top_ref, bottom_ref, basis_ref, *refs):
    del places_ref
    near_even, near_odd, far_even, far_odd, front_ref = refs[:5]
    upper_ref, out_ref = refs[-2:]
    near = pl.program_id(0) < blocks
    sums = jnp.concatenate(
        [
            jnp.where(near, near_even[...], far_even[...]),
            jnp.where(near, near_odd[...], far_odd[...]),
        ],
        axis=1,
    )
    hi, lo = parts2(sums)
    upper_ref[:HALF, :] = dot(
        top_ref[...], jnp.concatenate([hi[:HALF], lo[:HALF], hi[:HALF]], axis=0)
    )
    upper_ref[HALF:, :] = dot(bottom_ref[...], jnp.concatenate([hi, lo, hi], axis=0))
    out_ref[...] = front_ref[...] - dot(basis_ref[...], triple(upper_ref[...], 0))


def plan(tasks, link_rate, near_rate, lag):
    ready_link = {"near": 0.0, "far": 0.0}
    arrival, order, now = {}, [], 0.0
    left = dict(tasks)
    ended = {}

    def when(name):
        latest = 0.0
        for before, way, size in tasks[name][2]:
            if before not in ended:
                return None
            latest = max(latest, arrival.get((before, way), ended[before]))
        return latest

    while left:
        known = [(when(name), left[name][0], at, name) for at, name in enumerate(left)]
        known = [entry for entry in known if entry[0] is not None]
        free = [entry for entry in known if entry[0] <= now]
        chosen = min(free, key=lambda e: (e[1], e[2])) if free else min(known)
        name = chosen[3]
        now = max(now, chosen[0]) + tasks[name][1]
        ended[name] = now
        order.append((name, now))
        del left[name]
        sent = {}
        for other in tasks:
            for before, way, size in tasks[other][2]:
                if before == name and way:
                    sent[way] = max(size, sent.get(way, 0))
        for way, size in sent.items():
            begin = max(now, ready_link[way])
            ready_link[way] = begin + size / (near_rate if way == "near" else link_rate)
            arrival[name, way] = ready_link[way] + lag
    return order


def task_list(steps, chunks, width):
    tasks = {}
    gram = HALF // 2 * (LEAD + HALF) * 4e-6
    for t in range(steps):
        before = [("lead", None, 0), ("lead", "near", gram)] if t == 0 else [
            (("gram", t - 1), None, 0), (("gram", t - 1), "far", gram)
        ]
        tasks["gram", t] = (0, 1.0, before)
    tasks["lead"] = (0, 0.0, [])
    for k in range(PANELS):
        before = [(("factor", k - 1), None, 0)] if k else [(("gram", steps - 1), "near", gram)]
        tasks["factor", k] = (3, 5.2, before)
    tasks["finish"] = (3, 2.4, [(("factor", PANELS - 1), None, 0)])
    for c in range(chunks):
        if c == 0:
            tasks["send", c] = (2, 2.9, [("lead", None, 0)])
            tasks["keep", c] = (2, 2.9, [(("send", c), None, 0)])
        else:
            tasks["send", c] = (2, 4.8, [("lead", None, 0)])
        size = LEAD * width * 4e-6
        last = ("send", c)
        for t in range(1, steps):
            way = "near" if t == 1 else "far"
            before = [(last, way, size)] + ([(("keep", c), None, 0)] if t == 1 and c == 0 else [])
            tasks["split", c, t] = (1, 1.4, before)
            size = size / 2
            last = ("split", c, t)
        tasks["sum", c] = (1, 0.8, [(last, "far", size)])
        last = ("sum", c)
        for t in reversed(range(1, steps)):
            tasks["join", c, t] = (1, 0.9, [(last, "far", size)])
            size = size * 2
            last = ("join", c, t)
        tasks["project", c] = (4, 6.2, [(last, "near", size), ("finish", None, 0)])
    return tasks


def on_device(front_matrix, child_rows, child_owner, child_offset):
    row_count = lax.axis_size("row")
    col_count = lax.axis_size("col")
    local_rows, local_cols = front_matrix.shape
    child_count = child_rows.shape[0]
    capacity = 2 * child_count // row_count
    slots = row_count * capacity
    steps = row_count.bit_length() - 1
    owner, offset = child_owner[:, 0], child_offset[:, 0]
    run = Chain()

    stacked = child_count + local_rows
    pieces = 3
    size = -(-stacked // pieces // 16) * 16
    sizes = [size] * (pieces - 1) + [stacked - size * (pieces - 1)]
    own = run(
        "cut_lead", cut_body, [child_rows, front_matrix],
        [pl.BlockSpec((child_count, LEAD), lambda i: (0, 0)), pl.BlockSpec((local_rows, LEAD), lambda i: (0, 0))],
        [f32(n, LEAD) for n in sizes], [pl.BlockSpec((n, LEAD), lambda i: (0, 0)) for n in sizes],
        grid=(1,),
    )
    got = [spread(piece, col_count) for piece in own]
    packed = run(
        "pack_children", functools.partial(pack_body, row_count, capacity),
        [owner, child_rows], [SCALARS, WHOLE], [f32(slots, local_cols)], [WHOLE],
    )
    child = exchange(packed, row_count)
    packed, _, _, _ = run(
        "pack_lead",
        functools.partial(pack_lead_body, row_count, capacity, float(local_rows), child_count),
        [owner, offset, own[0]] + got[0], [SCALARS, SCALARS] + [WHOLE] * (1 + len(got[0])),
        [f32(slots, LEAD + PB), f32(sizes[0], LEAD), f32(slots, LEAD), f32(slots, PB)], [WHOLE] * 4,
    )
    lead_child = exchange(packed, row_count)
    operands = [ref for piece, arrived in zip(own, got) for ref in [piece] + arrived]
    lead, left, place, gram, gram_send = run(
        "lead_setup", functools.partial(lead_body, child_count, pieces),
        operands + [lead_child], [WHOLE] * (len(operands) + 1),
        [f32(local_rows, LEAD), bf16(LEAD, 3 * local_rows), bf16(local_rows, 3 * slots),
         f32(HALF // 2, LEAD + HALF), f32(HALF // 2, LEAD + HALF)],
        [WHOLE] * 5,
    )

    chunks = max(1, min(4, local_cols // (PB * row_count)))
    width = local_cols // 2 // chunks
    blocks = width // BLOCK
    core = upper_side(0, row_count)
    order = jnp.asarray(piece_order(row_count))[lax.axis_index("row")]
    scale = math.sqrt(local_rows * row_count)
    front = upper = matrix = factor = scaled = None
    gram_got = swap(gram_send, 0, row_count)
    keep, arrived, far = {}, {}, {}

    def make(halves, c, front):
        at = [(half * chunks + c) * blocks for half in halves]
        bases = jnp.concatenate([base + jnp.arange(blocks, dtype=jnp.int32) for base in at])
        operands = [left, place, front_matrix, child]
        in_specs = [
            pl.BlockSpec(left.shape, lambda i, b: (0, 0)),
            pl.BlockSpec(place.shape, lambda i, b: (0, 0)),
            pl.BlockSpec((local_rows, BLOCK), lambda i, b: (0, b[i])),
            pl.BlockSpec((slots, BLOCK), lambda i, b: (0, b[i])),
        ]
        aliases = {}
        if front is not None:
            operands.append(front)
            in_specs.append(ANYWHERE)
            aliases = {5: len(halves)}
        out_specs = [pl.BlockSpec((LEAD, BLOCK), lambda i, b: (0, jnp.minimum(i, blocks - 1)))]
        if len(halves) == 2:
            out_specs.append(pl.BlockSpec((LEAD, BLOCK), lambda i, b: (0, jnp.maximum(i - blocks, 0))))
        out_specs.append(pl.BlockSpec((local_rows, BLOCK), lambda i, b: (0, b[i])))
        return run(
            "lead_product", functools.partial(product_body, blocks, len(halves)), operands, in_specs,
            [f32(LEAD, width)] * len(halves) + [f32(local_rows, local_cols)], out_specs,
            scalars=[bases], grid=(blocks * len(halves),), aliases=aliases,
        )

    def cast(c, value, step):
        keep[c], arrived[c] = value, swap(value, step, row_count)

    for task, _ in plan(task_list(steps, chunks, width), 0.09, 0.4, 5.0):
        kind, c = task[0], task[1]
        if task == "lead":
            continue
        if task == "finish":
            top, bottom, basis, scaled = run(
                "finish_factor", functools.partial(finish_body, scale), [matrix, lead], [WHOLE] * 2,
                [bf16(HALF, 3 * HALF), bf16(HALF, 3 * LEAD), bf16(local_rows, 3 * LEAD), f32(local_rows, LEAD)],
                [WHOLE] * 4,
            )
        elif kind == "gram":
            gram = run("add_gram", add_body, [gram, gram_got], [WHOLE] * 2, [f32(*gram.shape)], [WHOLE])
            gram_got = swap(gram, (c + 1) % steps, row_count)
        elif kind == "factor":
            operands = [gram, gram_got] if c == 0 else [matrix]
            matrix = run(
                "eliminate_panel", functools.partial(eliminate_body, c), operands,
                [WHOLE] * len(operands), [f32(LEAD, LEAD)], [WHOLE],
            )
        elif kind == "send":
            if c == 0:
                send, front = make([1 - core], c, front)
            else:
                send, keep[c], front = make([1 - core, core], c, front)
            arrived[c] = swap(send, 0, row_count)
        elif kind == "keep":
            keep[c], front = make([core], c, front)
        elif kind == "split":
            t = task[2]
            shape = f32(LEAD, keep[c].shape[1] // 2)
            keep[c], send = run(
                "split_add", functools.partial(split_add_body, t, row_count), [keep[c], arrived[c]],
                [WHOLE] * 2, [shape, shape], [WHOLE] * 2,
            )
            arrived[c] = swap(send, t, row_count)
        elif kind == "sum":
            value = run("add_shard", add_body, [keep[c], arrived[c]], [WHOLE] * 2, [f32(*keep[c].shape)], [WHOLE])
            cast(c, value, steps - 1)
        elif kind == "join":
            rows = keep[c].shape[0]
            value = run("join_pieces", join_body, [keep[c], arrived[c]], [WHOLE] * 2, [f32(2 * rows, PB)], [WHOLE])
            cast(c, value, task[2] - 1)
        elif kind == "project":
            starts = [(half * chunks + c) * blocks for half in (core, 1 - core)]
            columns = jnp.concatenate([s + jnp.arange(blocks, dtype=jnp.int32) for s in starts])
            scalars = [jnp.concatenate([columns, order[0], order[1]])]
            near = 2 * blocks
            far_at = near + 2 * blocks

            def near_piece(odd):
                return lambda i, p: (p[near + 2 * jnp.minimum(i, blocks - 1) + odd], 0)

            def far_piece(odd):
                return lambda i, p: (p[far_at + 2 * jnp.maximum(i - blocks, 0) + odd], 0)

            operands = [top, bottom, basis, keep[c], keep[c], arrived[c], arrived[c], front]
            in_specs = [
                pl.BlockSpec(top.shape, lambda i, p: (0, 0)),
                pl.BlockSpec(bottom.shape, lambda i, p: (0, 0)),
                pl.BlockSpec(basis.shape, lambda i, p: (0, 0)),
                pl.BlockSpec((LEAD, PB), near_piece(0)),
                pl.BlockSpec((LEAD, PB), near_piece(1)),
                pl.BlockSpec((LEAD, PB), far_piece(0)),
                pl.BlockSpec((LEAD, PB), far_piece(1)),
                pl.BlockSpec((local_rows, BLOCK), lambda i, p: (0, p[i])),
            ]
            aliases = {8: 1}
            if upper is not None:
                operands.append(upper)
                in_specs.append(ANYWHERE)
                aliases[9] = 0
            upper, front = run(
                "project_columns", functools.partial(project_body, blocks), operands, in_specs,
                [f32(LEAD, local_cols), f32(local_rows, local_cols)],
                [pl.BlockSpec((LEAD, BLOCK), lambda i, p: (0, p[i])), pl.BlockSpec((local_rows, BLOCK), lambda i, p: (0, p[i]))],
                scalars=scalars, grid=(2 * blocks,), aliases=aliases,
            )
    return upper, front, scaled


def solution(mesh):
    placed = (P("row", "col"), P("row", "col"), P("row", None), P("row", None))
    return jax.shard_map(
        on_device,
        mesh=mesh,
        in_specs=placed,
        out_specs=(P(None, "col"), P("row", "col"), P("row", None)),
        check_vma=False,
    )
```

```python
import functools
import math

import jax
import jax.numpy as jnp
import numpy as np
from jax import lax
from jax.experimental import pallas as pl
from jax.experimental.pallas import tpu as pltpu
from jax.sharding import PartitionSpec as P

PB = 128
PANELS = 4
LEAD = PB * PANELS
HALF = LEAD // 2
BLOCK = 256
VMEM_BYTES = 24 * 1024 * 1024
CHUNKS = 2
HIGHEST = lax.Precision.HIGHEST
F32 = jnp.float32
BF16 = jnp.bfloat16
WHOLE = pl.BlockSpec(memory_space=pltpu.VMEM)
SCALARS = pl.BlockSpec(memory_space=pltpu.SMEM)
ANYWHERE = pl.BlockSpec(memory_space=pl.ANY)


def f32(*shape):
    return jax.ShapeDtypeStruct(shape, F32)


def bf16(*shape):
    return jax.ShapeDtypeStruct(shape, BF16)


def full(shape):
    return pl.BlockSpec(shape, lambda *at: (0,) * len(shape))


class Chain:
    def __init__(self):
        self.token = None

    def __call__(self, name, body, operands, in_specs, outs, out_specs, scalars=(), grid=None, aliases=None, scratch=()):
        taken = len(scalars) + len(operands)
        given = len(outs)
        has_token = self.token is not None
        operands, in_specs = list(operands), list(in_specs)
        if grid is None:
            grid = (1,)
            in_specs = [full(x.shape) if spec is WHOLE else spec for x, spec in zip(operands, in_specs)]
            out_specs = [full(x.shape) for x in outs]
        if has_token:
            operands.append(self.token)
            in_specs.append(ANYWHERE)

        def kernel(*refs):
            ins, rest = refs[:taken], refs[taken + has_token :]
            rest[given][...] = jnp.zeros((8, PB), F32)
            body(*ins, *rest[:given], *rest[given + 1 :])

        settings = dict(
            out_shape=tuple(outs) + (f32(8, PB),),
            input_output_aliases=aliases or {},
            compiler_params=pltpu.CompilerParams(vmem_limit_bytes=VMEM_BYTES),
            cost_estimate=pl.CostEstimate(flops=1 << 20, bytes_accessed=1 << 16, transcendentals=0),
            name=name,
        )
        grid_spec = pltpu.PrefetchScalarGridSpec(
            num_scalar_prefetch=len(scalars),
            grid=grid,
            in_specs=in_specs,
            out_specs=tuple(out_specs) + (full((8, PB)),),
            scratch_shapes=scratch,
        )
        results = pl.pallas_call(kernel, grid_spec=grid_spec, **settings)(*scalars, *operands)
        self.token = results[-1]
        return results[:-1] if given > 1 else results[0]


def mask_orders(count):
    others = [1 << b for b in range(1, count.bit_length() - 1)]
    half = len(others) // 2
    return ([1] + others, [1] + others[half:] + others[:half])


def swap(value, step, count):
    orders = mask_orders(count)
    pairs = [(d, d ^ orders[d & 1][step]) for d in range(count)]
    return lax.ppermute(value, "row", pairs)


def upper_side(step, count):
    orders = mask_orders(count)
    me = lax.axis_index("row")
    mask = jnp.where(me % 2 == 0, orders[0][step], orders[1][step])
    return ((me & mask) != 0).astype(jnp.int32)


def shard_table(count):
    orders = mask_orders(count)
    steps = len(orders[0])
    return np.array(
        [
            sum(((d & orders[d & 1][t]) != 0) << (steps - 1 - t) for t in range(steps))
            for d in range(count)
        ]
    )


def piece_order(count):
    orders = mask_orders(count)
    steps = len(orders[0])
    shard = shard_table(count)

    def pieces(device, done):
        if done == 0:
            return [device]
        mask = orders[device & 1][steps - done]
        return pieces(device, done - 1) + pieces(device ^ mask, done - 1)

    half = count // 2
    order = np.zeros((count, 2, half), np.int32)
    for d in range(count):
        for at, piece in enumerate(pieces(d, steps)):
            order[d, at // half, shard[piece] % half] = at % half
    return order


def relay(first, count):
    middle = count // 2
    others = [c for c in range(count - 1, 0, -1) if c != middle]
    return [lax.ppermute(first, "col", [(middle, c)]) for c in others]


def exchange(value, row_count):
    slots, width = value.shape
    shaped = value.reshape(row_count, slots // row_count, width)
    return lax.all_to_all(shaped, "row", split_axis=0, concat_axis=0, tiled=True).reshape(
        slots, width
    )


def parts3(x):
    hi = x.astype(BF16)
    rest = x - hi.astype(F32)
    mid = rest.astype(BF16)
    return hi, mid, (rest - mid.astype(F32)).astype(BF16)


def parts2(x):
    hi = x.astype(BF16)
    return hi, (x - hi.astype(F32)).astype(BF16)


def triple(x, axis):
    hi, lo = parts2(x)
    return jnp.concatenate([hi, hi, lo] if axis == 1 else [hi, lo, hi], axis=axis)


def dot_high(a, b, dims):
    return lax.dot_general(a, b, (dims, ((), ())), precision=HIGHEST, preferred_element_type=F32)


def dot(a, b):
    return jnp.dot(a, b, preferred_element_type=F32)


def pick(own, gots):
    arrived = gots[0][...]
    for got in gots[1:]:
        arrived = arrived + got[...]
    return jnp.where(lax.axis_index("col") == 0, own[...], arrived)


def pack_body(row_count, capacity, sentinel, pieces, owner_ref, offset_ref, child_ref, front_ref, *refs):
    outs, (out_ref, rows_ref, tag_ref) = refs[:pieces], refs[pieces:]
    at = 0
    for out in outs:
        out[...] = front_ref[at : at + out.shape[0], :]
        at += out.shape[0]
    rows_ref[...] = jnp.zeros_like(rows_ref)
    tag_ref[...] = jnp.full(tag_ref.shape, sentinel, F32)

    def body(i, counts):
        owner = owner_ref[i]
        rank = jnp.int32(0)
        for d in range(row_count):
            rank = jnp.where(owner == d, counts[d], rank)
        slot = owner * capacity + rank
        rows_ref[pl.ds(slot, 1), :] = child_ref[pl.ds(i, 1), :]
        tag_ref[pl.ds(slot, 1), :] = jnp.full((1, PB), offset_ref[i].astype(F32))
        return tuple(counts[d] + (owner == d).astype(jnp.int32) for d in range(row_count))

    lax.fori_loop(0, child_ref.shape[0], body, (jnp.int32(0),) * row_count)
    width = rows_ref.shape[1]
    out_ref[:, :width] = rows_ref[...]
    out_ref[:, width:] = tag_ref[...]


def gather_body(rows_in, tags_in, *refs):
    rows_ref, tag_ref = refs[-2:]
    rows_ref[...] = rows_in[...]
    tag_ref[...] = tags_in[...]


def lead_body(chunk_count, *refs):
    each = (len(refs) - 6) // (chunk_count + 1)
    chunks = [refs[i * each : (i + 1) * each] for i in range(chunk_count + 1)]
    tag_ref = refs[each * (chunk_count + 1)]
    lead_ref, left_ref, place_ref, keep_ref, send_ref = refs[-5:]
    slots_value = pick(chunks[-1][0], chunks[-1][1:])
    front = jnp.concatenate([pick(c[0], c[1:]) for c in chunks[:-1]], axis=0)
    rows, slots = front.shape[0], slots_value.shape[0]
    at = lax.broadcasted_iota(jnp.int32, (rows, slots), 0).astype(F32)

    onehot = jnp.where(at == jnp.transpose(tag_ref[...])[0:1, :], 1.0, 0.0).astype(BF16)
    spots = jnp.concatenate([onehot, onehot, onehot], axis=1)
    place_ref[...] = spots
    lead = front + dot(spots, jnp.concatenate(parts3(slots_value)[::-1], axis=0))
    lead_ref[...] = lead
    turned = jnp.transpose(lead)
    left_ref[...] = triple(turned, 1)
    first = dot_high(turned[:HALF], lead[:, :HALF], ((1,), (0,)))
    second = dot_high(turned[HALF:], lead, ((1,), (0,)))
    side = lax.axis_index("row") % 2 == 0
    for out, flip in ((keep_ref, False), (send_ref, True)):
        low = jnp.logical_xor(side, flip)
        out[:, :HALF] = jnp.where(low, first[:PB], first[PB:])
        out[:, HALF:] = jnp.where(low, second[:PB], second[PB:])


def add_body(a_ref, b_ref, out_ref):
    out_ref[...] = a_ref[...] + b_ref[...]


def join_body(a_ref, b_ref, out_ref):
    half = a_ref.shape[0]
    out_ref[:half, :] = a_ref[...]
    out_ref[half:, :] = b_ref[...]


def split_add_body(step, count, keep_ref, got_ref, keep_out, send_out):
    half = keep_out.shape[1]
    side = upper_side(step, count)
    for which, out in ((side, keep_out), (1 - side, send_out)):
        part = pl.ds(pl.multiple_of(which * half, 128), half)
        out[...] = keep_ref[:, part] + got_ref[:, part]


def product_body(blocks, count, base_ref, left_ref, place_ref, front_ref, child_ref, *rest):
    del base_ref
    outs, whole_ref = rest[-1 - count : -1], rest[-1]
    parts = jnp.concatenate(parts3(child_ref[...])[::-1], axis=0)
    whole = front_ref[...] + dot(place_ref[...], parts)
    whole_ref[...] = whole
    result = dot(left_ref[...], triple(whole, 0))
    for at, out in enumerate(outs):

        @pl.when(pl.program_id(0) // blocks == at)
        def _():
            out[...] = result


def spread_lane(tile, at):
    return jnp.broadcast_to(tile[:, at : at + 1], tile.shape)


def invert_factor(block):
    lane = lax.broadcasted_iota(jnp.int32, (8, PB), 1)
    sub = lax.broadcasted_iota(jnp.int32, (8, PB), 0)
    count = PB // 8
    tiles = [block[8 * t : 8 * t + 8, :] for t in range(count)]
    for b in range(count):
        first = 8 * b
        rows = tiles[b]
        cols = [spread_lane(rows, first + c) for c in range(8)]
        heads, inverses = {}, []
        for c in range(8):
            inverse = 1.0 / cols[c][c : c + 1, :]
            inverses.append(inverse)
            factor = jnp.where(sub > c, cols[c] * inverse, 0.0)
            here = lane == first + c
            source = jnp.where(here[0:1, :], 1.0, rows[c : c + 1, :])
            rows = jnp.where(here & (sub > c), 0.0, rows) - factor * source
            for d in range(c + 1, 8):
                heads[c, d] = cols[d][c : c + 1, :]
                cols[d] = cols[d] - factor * heads[c, d]
        tiles[b] = rows
        inside = (lane >= first) & (lane < first + 8)
        past = inside & (lane - first >= sub)
        used = jnp.where(past, jnp.where(lane - first == sub, 1.0, 0.0), rows)
        for t in range(b + 1, count):
            tile = tiles[t]
            factors = []
            for c in range(8):
                factor = spread_lane(tile, first + c)
                for d in range(c):
                    factor = factor - factors[d] * heads[d, c]
                factors.append(factor * inverses[c])
            tile = jnp.where(inside, 0.0, tile)
            for c in range(8):
                tile = tile - factors[c] * used[c : c + 1, :]
            tiles[t] = tile
    done = []
    for t in range(count):
        diagonal = lane == sub + 8 * t
        pivot = jnp.sum(jnp.where(diagonal, tiles[t], 0.0), axis=1, keepdims=True)
        scale = lax.rsqrt(pivot)
        scale = scale * (1.5 - 0.5 * pivot * scale * scale)
        unit = jnp.where(diagonal, 1.0, jnp.where(lane < sub + 8 * t, tiles[t], 0.0))
        done.append(unit * scale)
    return jnp.concatenate(done, axis=0)


def eliminate_body(k, *refs):
    out_ref = refs[-1]
    lo, hi = k * PB, (k + 1) * PB
    if k == 0:
        mine, got = refs[0][...], refs[1][...]
        low = lax.axis_index("row") % 2 == 0
        packed = jnp.concatenate([jnp.where(low, mine, got), jnp.where(low, got, mine)], axis=0)
        cross = packed[:, HALF:LEAD]
        out_ref[:HALF, :HALF] = packed[:, :HALF]
        out_ref[HALF:, :HALF] = cross
        out_ref[:HALF, HALF:] = jnp.transpose(cross)
        out_ref[HALF:, HALF:] = packed[:, LEAD:]
        in_ref = out_ref
    else:
        in_ref = refs[0]
        out_ref[:lo, :] = in_ref[:lo, :]
    inverse = invert_factor(in_ref[lo:hi, lo:hi])
    pieces = []
    for j in range(PANELS):
        if j == k:
            pieces.append(inverse)
        else:
            pieces.append(dot_high(inverse, in_ref[lo:hi, j * PB : (j + 1) * PB], ((1,), (0,))))
    row = jnp.concatenate(pieces, axis=1)
    out_ref[lo:hi, :] = row
    if k < PANELS - 1:
        column = dot_high(in_ref[hi:, lo:hi], inverse, ((1,), (1,)))
        change = dot_high(column, row, ((1,), (0,)))
        later = in_ref[hi:, :]
        out_ref[hi:, :] = later - change
        out_ref[hi:, lo:hi] = -change[:, lo:hi]


def finish_body(scale, matrix_ref, lead_ref, top_ref, bottom_ref, basis3_ref, basis_ref):
    own = lax.broadcasted_iota(jnp.int32, (LEAD, LEAD), 0) // PB
    other = lax.broadcasted_iota(jnp.int32, (LEAD, LEAD), 1) // PB
    inverse = jnp.where(own >= other, matrix_ref[...], 0.0)
    top_ref[...] = triple(inverse[:HALF, :HALF], 1)
    bottom_ref[...] = triple(inverse[HALF:], 1)
    basis = dot_high(lead_ref[...], inverse, ((1,), (1,)))
    basis3_ref[...] = triple(basis, 1)
    basis_ref[...] = basis * scale


def project_body(blocks, places_ref, top_ref, bottom_ref, basis_ref, *refs):
    del places_ref
    near_even, near_odd, far_even, far_odd, front_ref = refs[:5]
    upper_ref, out_ref = refs[-2:]
    near = pl.program_id(0) < blocks
    sums = jnp.concatenate(
        [
            jnp.where(near, near_even[...], far_even[...]),
            jnp.where(near, near_odd[...], far_odd[...]),
        ],
        axis=1,
    )
    hi, lo = parts2(sums)
    upper_ref[:HALF, :] = dot(
        top_ref[...], jnp.concatenate([hi[:HALF], lo[:HALF], hi[:HALF]], axis=0)
    )
    upper_ref[HALF:, :] = dot(bottom_ref[...], jnp.concatenate([hi, lo, hi], axis=0))
    out_ref[...] = front_ref[...] - dot(basis_ref[...], triple(upper_ref[...], 0))


def plan(tasks, link_rate, near_rate, lag):
    ready_link = {"near": 0.0, "far": 0.0}
    arrival, order, now = {}, [], 0.0
    left = dict(tasks)
    ended = {}

    def when(name):
        latest = 0.0
        for before, way, size in tasks[name][2]:
            if before not in ended:
                return None
            latest = max(latest, arrival.get((before, way), ended[before]))
        return latest

    while left:
        known = [(when(name), left[name][0], at, name) for at, name in enumerate(left)]
        known = [entry for entry in known if entry[0] is not None]
        free = [entry for entry in known if entry[0] <= now]
        chosen = min(free, key=lambda e: (e[1], e[2])) if free else min(known)
        name = chosen[3]
        now = max(now, chosen[0]) + tasks[name][1]
        ended[name] = now
        order.append((name, now))
        del left[name]
        sent = {}
        for other in tasks:
            for before, way, size in tasks[other][2]:
                if before == name and way:
                    sent[way] = max(size, sent.get(way, 0))
        for way, size in sent.items():
            begin = max(now, ready_link[way])
            ready_link[way] = begin + size / (near_rate if way == "near" else link_rate)
            arrival[name, way] = ready_link[way] + lag
    return order


def task_list(steps, chunks, width):
    tasks = {}
    gram = HALF // 2 * (LEAD + HALF) * 4e-6
    for t in range(steps):
        before = [("lead", None, 0), ("lead", "near", gram)] if t == 0 else [
            (("gram", t - 1), None, 0), (("gram", t - 1), "far", gram)
        ]
        tasks["gram", t] = (0, 1.0, before)
    tasks["lead"] = (0, 0.0, [])
    for k in range(PANELS):
        before = [(("factor", k - 1), None, 0)] if k else [(("gram", steps - 1), "near", gram)]
        tasks["factor", k] = (3, 5.2, before)
    tasks["finish"] = (3, 2.4, [(("factor", PANELS - 1), None, 0)])
    tasks["send", 0] = (2, 8.0, [("lead", None, 0)])
    tasks["keep", 0] = (2, 8.0, [(("send", 0), None, 0)])
    for c in range(chunks):
        size = LEAD * width * 4e-6
        last = ("send", 0)
        for t in range(1, steps):
            way = "near" if t == 1 else "far"
            before = [(last, way, size)] + ([(("keep", 0), None, 0)] if t == 1 else [])
            tasks["split", c, t] = (1, 1.4, before)
            size = size / 2
            last = ("split", c, t)
        tasks["sum", c] = (1, 0.8, [(last, "far", size)])
        last = ("sum", c)
        for t in reversed(range(1, steps)):
            tasks["join", c, t] = (1, 0.9, [(last, "far", size)])
            size = size * 2
            last = ("join", c, t)
        tasks["project", c] = (4, 6.2, [(last, "near", size), ("finish", None, 0)])
    return tasks


ORDER = (
    "G0 P0 G1 K0 S01 S11 G2 S02 S12 E0 A0 E1 A1 J02 E2 J12 E3 F J01 J11 X0 X1 "
)
KINDS = {"P": "send", "K": "keep", "S": "split", "G": "gram", "E": "factor", "A": "sum", "J": "join", "X": "project"}


def sequence(steps, chunks, width):
    tasks = task_list(steps, chunks, width)
    named = []
    for word in ORDER.split():
        named.append("finish" if word == "F" else (KINDS[word[0]],) + tuple(int(d) for d in word[1:]))
    if set(named) == set(tasks) - {"lead"}:
        return named
    return [task for task, _ in plan(tasks, 0.09, 0.4, 5.0)]


def on_device(front_matrix, child_rows, child_owner, child_offset):
    row_count = lax.axis_size("row")
    col_count = lax.axis_size("col")
    local_rows, local_cols = front_matrix.shape
    child_count = child_rows.shape[0]
    capacity = 2 * child_count // row_count
    slots = row_count * capacity
    steps = row_count.bit_length() - 1
    owner, offset = child_owner[:, 0], child_offset[:, 0]
    run = Chain()

    pieces = 2
    sizes = [local_rows // pieces] * pieces
    *own, packed = run(
        "pack_children", functools.partial(pack_body, row_count, capacity, float(local_rows), pieces),
        [owner, offset, child_rows, front_matrix],
        [SCALARS, SCALARS, full(child_rows.shape), full((local_rows, LEAD))],
        [f32(n, LEAD) for n in sizes] + [f32(slots, local_cols + PB)],
        [full((n, LEAD)) for n in sizes] + [full((slots, local_cols + PB))],
        grid=(1,), scratch=[pltpu.VMEM((slots, local_cols), F32), pltpu.VMEM((slots, PB), F32)],
    )
    got = [[lax.ppermute(piece, "col", [(0, col_count // 2)])] for piece in own]
    child = exchange(packed, row_count)
    rows, tags = run(
        "gather_lead", gather_body, [child, child] + [first for first, in got],
        [full((slots, LEAD)), pl.BlockSpec((slots, PB), lambda i: (0, local_cols // PB))] + [ANYWHERE] * pieces,
        [f32(slots, LEAD), f32(slots, PB)], [full((slots, LEAD)), full((slots, PB))], grid=(1,),
    )
    own.append(rows)
    got.append([lax.ppermute(rows, "col", [(0, col_count // 2)])])
    for arrived_here in got:
        arrived_here.extend(relay(arrived_here[0], col_count))
    operands = [ref for piece, arrived in zip(own, got) for ref in [piece] + arrived]
    lead, left, place, gram, gram_send = run(
        "lead_setup", functools.partial(lead_body, pieces),
        operands + [tags], [WHOLE] * (len(operands) + 1),
        [f32(local_rows, LEAD), bf16(LEAD, 3 * local_rows), bf16(local_rows, 3 * slots),
         f32(HALF // 2, LEAD + HALF), f32(HALF // 2, LEAD + HALF)],
        [WHOLE] * 5,
    )

    chunks = max(1, min(CHUNKS, local_cols // (PB * row_count)))
    width = local_cols // 2 // chunks
    blocks = width // BLOCK
    core = upper_side(0, row_count)
    order = jnp.asarray(piece_order(row_count))[lax.axis_index("row")]
    scale = math.sqrt(local_rows * row_count)
    front = upper = matrix = factor = scaled = None
    gram_got = swap(gram_send, 0, row_count)
    keep, arrived, far = {}, {}, {}

    def make(half, front):
        base = (half * chunks * blocks + jnp.arange(chunks * blocks)).astype(jnp.int32)
        operands = [left, place, front_matrix, child]
        in_specs = [
            full(left.shape),
            full(place.shape),
            pl.BlockSpec((local_rows, BLOCK), lambda i, b: (0, b[i])),
            pl.BlockSpec((slots, BLOCK), lambda i, b: (0, b[i])),
        ]
        aliases = {}
        if front is not None:
            operands.append(front)
            in_specs.append(ANYWHERE)
            aliases = {5: chunks}

        def out_block(at):
            return lambda i, b: (0, jnp.clip(i - at * blocks, 0, blocks - 1))

        out_specs = [pl.BlockSpec((LEAD, BLOCK), out_block(at)) for at in range(chunks)]
        out_specs.append(pl.BlockSpec((local_rows, BLOCK), lambda i, b: (0, b[i])))
        return run(
            "lead_product", functools.partial(product_body, blocks, chunks), operands, in_specs,
            [f32(LEAD, width)] * chunks + [f32(local_rows, local_cols)], out_specs,
            scalars=[base], grid=(blocks * chunks,), aliases=aliases,
        )

    def cast(c, value, step):
        keep[c], arrived[c] = value, swap(value, step, row_count)

    for task in sequence(steps, chunks, width):
        kind, c = task[0], task[1]
        if task == "lead":
            continue
        if task == "finish":
            top, bottom, basis, scaled = run(
                "finish_factor", functools.partial(finish_body, scale), [matrix, lead], [WHOLE] * 2,
                [bf16(HALF, 3 * HALF), bf16(HALF, 3 * LEAD), bf16(local_rows, 3 * LEAD), f32(local_rows, LEAD)],
                [WHOLE] * 4,
            )
        elif kind == "gram":
            gram = run("add_gram", add_body, [gram, gram_got], [WHOLE] * 2, [f32(*gram.shape)], [WHOLE])
            gram_got = swap(gram, (c + 1) % steps, row_count)
        elif kind == "factor":
            operands = [gram, gram_got] if c == 0 else [matrix]
            matrix = run(
                "eliminate_panel", functools.partial(eliminate_body, c), operands,
                [WHOLE] * len(operands), [f32(LEAD, LEAD)], [WHOLE],
            )
        elif kind == "send":
            *made, front = make(1 - core, front)
            for at, value in enumerate(made):
                arrived[at] = swap(value, 0, row_count)
        elif kind == "keep":
            *made, front = make(core, front)
            for at, value in enumerate(made):
                keep[at] = value
        elif kind == "split":
            t = task[2]
            shape = f32(LEAD, keep[c].shape[1] // 2)
            keep[c], send = run(
                "split_add", functools.partial(split_add_body, t, row_count), [keep[c], arrived[c]],
                [WHOLE] * 2, [shape, shape], [WHOLE] * 2,
            )
            arrived[c] = swap(send, t, row_count)
        elif kind == "sum":
            value = run("add_shard", add_body, [keep[c], arrived[c]], [WHOLE] * 2, [f32(*keep[c].shape)], [WHOLE])
            cast(c, value, steps - 1)
        elif kind == "join":
            rows, value_width = keep[c].shape
            value = run("join_pieces", join_body, [keep[c], arrived[c]], [WHOLE] * 2, [f32(2 * rows, value_width)], [WHOLE])
            cast(c, value, task[2] - 1)
        elif kind == "project":
            starts = [(half * chunks + c) * blocks for half in (core, 1 - core)]
            columns = jnp.concatenate([s + jnp.arange(blocks, dtype=jnp.int32) for s in starts])
            scalars = [jnp.concatenate([columns, order[0], order[1]])]
            near, per = 2 * blocks, keep[c].shape[1] // PB
            far_at = near + 2 * blocks // per

            def near_piece(odd):
                def at(i, p):
                    place = 2 * jnp.minimum(i, blocks - 1) + odd
                    return p[near + place // per], place % per

                return at

            def far_piece(odd):
                def at(i, p):
                    place = 2 * jnp.maximum(i - blocks, 0) + odd
                    return p[far_at + place // per], place % per

                return at

            operands = [top, bottom, basis, keep[c], keep[c], arrived[c], arrived[c], front]
            in_specs = [
                pl.BlockSpec(top.shape, lambda i, p: (0, 0)),
                pl.BlockSpec(bottom.shape, lambda i, p: (0, 0)),
                pl.BlockSpec(basis.shape, lambda i, p: (0, 0)),
                pl.BlockSpec((LEAD, PB), near_piece(0)),
                pl.BlockSpec((LEAD, PB), near_piece(1)),
                pl.BlockSpec((LEAD, PB), far_piece(0)),
                pl.BlockSpec((LEAD, PB), far_piece(1)),
                pl.BlockSpec((local_rows, BLOCK), lambda i, p: (0, p[i])),
            ]
            aliases = {8: 1}
            if upper is not None:
                operands.append(upper)
                in_specs.append(ANYWHERE)
                aliases[9] = 0
            upper, front = run(
                "project_columns", functools.partial(project_body, blocks), operands, in_specs,
                [f32(LEAD, local_cols), f32(local_rows, local_cols)],
                [pl.BlockSpec((LEAD, BLOCK), lambda i, p: (0, p[i])), pl.BlockSpec((local_rows, BLOCK), lambda i, p: (0, p[i]))],
                scalars=scalars, grid=(2 * blocks,), aliases=aliases,
            )
    return upper, front, scaled


def solution(mesh):
    placed = (P("row", "col"), P("row", "col"), P("row", None), P("row", None))
    return jax.shard_map(
        on_device,
        mesh=mesh,
        in_specs=placed,
        out_specs=(P(None, "col"), P("row", "col"), P("row", None)),
        check_vma=False,
    )
```

```python
import functools
import math

import jax
import jax.numpy as jnp
import numpy as np
from jax import lax
from jax.experimental import pallas as pl
from jax.experimental.pallas import tpu as pltpu
from jax.sharding import PartitionSpec as P

PB = 128
PANELS = 4
LEAD = PB * PANELS
HALF = LEAD // 2
BLOCK = 256
VMEM_BYTES = 32 * 1024 * 1024
CHUNKS = 4
HIGHEST = lax.Precision.HIGHEST
F32 = jnp.float32
BF16 = jnp.bfloat16
WHOLE = pl.BlockSpec(memory_space=pltpu.VMEM)
SCALARS = pl.BlockSpec(memory_space=pltpu.SMEM)
ANYWHERE = pl.BlockSpec(memory_space=pl.ANY)
IN_HBM = pl.BlockSpec(memory_space=pltpu.HBM)


def f32(*shape):
    return jax.ShapeDtypeStruct(shape, F32)


def bf16(*shape):
    return jax.ShapeDtypeStruct(shape, BF16)


def full(shape):
    return pl.BlockSpec(shape, lambda *at: (0,) * len(shape))


class Chain:
    def __init__(self):
        self.token = None

    def __call__(self, name, body, operands, in_specs, outs, out_specs, scalars=(), grid=(1,), aliases=None, scratch=()):
        count, has_token = len(operands), self.token is not None
        smem = [at for at, spec in enumerate(in_specs) if spec is SCALARS]
        moved = [at for at, spec in enumerate(in_specs) if spec is not SCALARS and spec is not ANYWHERE]
        blocks_in = [full(operands[at].shape) if in_specs[at] is WHOLE else in_specs[at] for at in moved]
        blocks_out = [full(out.shape) if spec is WHOLE else spec for out, spec in zip(outs, out_specs)]
        first = len(scalars)

        def kernel(*refs):
            counts, ins = refs[:first], refs[first : first + count]
            results = refs[first + count + has_token :][: len(outs)]
            held = refs[first + count + has_token + len(outs) + 1 :]

            def located(spec):
                return pl.BlockSpec(spec.block_shape, lambda *at: spec.index_map(*at, *counts))

            def step(*blocks):
                body(*counts, *[ins[at] for at in smem], *blocks, *held)

            pltpu.emit_pipeline(
                step,
                grid=grid,
                in_specs=[located(spec) for spec in blocks_in],
                out_specs=[located(spec) for spec in blocks_out],
            )(*[ins[at] for at in moved], *results)

        places = [SCALARS] * first + [SCALARS if at in smem else IN_HBM for at in range(count)]
        arrays = list(scalars) + list(operands)
        if has_token:
            arrays.append(self.token)
            places.append(IN_HBM)
        results = pl.pallas_call(
            kernel,
            out_shape=tuple(outs) + (f32(8, PB),),
            in_specs=places,
            out_specs=(IN_HBM,) * (len(outs) + 1),
            scratch_shapes=scratch,
            input_output_aliases=aliases or {},
            compiler_params=pltpu.CompilerParams(vmem_limit_bytes=VMEM_BYTES),
            cost_estimate=pl.CostEstimate(flops=1 << 20, bytes_accessed=1 << 16, transcendentals=0),
            name=name,
        )(*arrays)
        self.token = results[-1]
        return results[:-1] if len(outs) > 1 else results[0]


def mask_orders(count):
    others = [1 << b for b in range(1, count.bit_length() - 1)]
    half = len(others) // 2
    return ([1] + others, [1] + others[half:] + others[:half])


def swap(value, step, count):
    orders = mask_orders(count)
    pairs = [(d, d ^ orders[d & 1][step]) for d in range(count)]
    return lax.ppermute(value, "row", pairs)


def upper_side(step, count):
    orders = mask_orders(count)
    me = lax.axis_index("row")
    mask = jnp.where(me % 2 == 0, orders[0][step], orders[1][step])
    return ((me & mask) != 0).astype(jnp.int32)


def shard_table(count):
    orders = mask_orders(count)
    steps = len(orders[0])
    return np.array(
        [
            sum(((d & orders[d & 1][t]) != 0) << (steps - 1 - t) for t in range(steps))
            for d in range(count)
        ]
    )


def piece_order(count):
    orders = mask_orders(count)
    steps = len(orders[0])
    shard = shard_table(count)

    def pieces(device, done):
        if done == 0:
            return [device]
        mask = orders[device & 1][steps - done]
        return pieces(device, done - 1) + pieces(device ^ mask, done - 1)

    half = count // 2
    order = np.zeros((count, 2, half), np.int32)
    for d in range(count):
        for at, piece in enumerate(pieces(d, steps)):
            order[d, at // half, shard[piece] % half] = at % half
    return order


def spread(value, count):
    middle = count // 2
    first = lax.ppermute(value, "col", [(0, middle)])
    others = [c for c in range(count - 1, 0, -1) if c != middle]
    return [first] + [lax.ppermute(first, "col", [(middle, c)]) for c in others]


def exchange(value, row_count):
    slots, width = value.shape
    shaped = value.reshape(row_count, slots // row_count, width)
    return lax.all_to_all(shaped, "row", split_axis=0, concat_axis=0, tiled=True).reshape(
        slots, width
    )


def parts3(x):
    hi = x.astype(BF16)
    rest = x - hi.astype(F32)
    mid = rest.astype(BF16)
    return hi, mid, (rest - mid.astype(F32)).astype(BF16)


def parts2(x):
    hi = x.astype(BF16)
    return hi, (x - hi.astype(F32)).astype(BF16)


def triple(x, axis):
    hi, lo = parts2(x)
    return jnp.concatenate([hi, hi, lo] if axis == 1 else [hi, lo, hi], axis=axis)


def dot_high(a, b, dims):
    return lax.dot_general(a, b, (dims, ((), ())), precision=HIGHEST, preferred_element_type=F32)


def dot(a, b):
    return jnp.dot(a, b, preferred_element_type=F32)


def pick(own, gots):
    arrived = gots[0][...]
    for got in gots[1:]:
        arrived = arrived + got[...]
    return jnp.where(lax.axis_index("col") == 0, own[...], arrived)


def place_rows(row_count, capacity, owner_ref, child_count, write):
    def body(i, counts):
        owner = owner_ref[i]
        rank = jnp.int32(0)
        for d in range(row_count):
            rank = jnp.where(owner == d, counts[d], rank)
        write(i, owner, rank)
        return tuple(counts[d] + (owner == d).astype(jnp.int32) for d in range(row_count))

    lax.fori_loop(0, child_count, body, (jnp.int32(0),) * row_count)


def pack_body(row_count, capacity, sentinel, pieces, owner_ref, offset_ref, child_ref, front_ref, *refs):
    outs, (lead_ref, out_ref, rows_ref, tag_ref) = refs[:pieces], refs[pieces:]
    lead_ref[...] = child_ref[:, :LEAD]
    at = 0
    for out in outs:
        out[...] = front_ref[at : at + out.shape[0], :]
        at += out.shape[0]
    rows_ref[...] = jnp.zeros_like(rows_ref)
    tag_ref[...] = jnp.full(tag_ref.shape, sentinel, F32)

    def write(i, owner, rank):
        slot = owner * capacity + rank
        rows_ref[pl.ds(slot, 1), :] = child_ref[pl.ds(i, 1), :]
        tag_ref[pl.ds(slot, 1), :] = jnp.full((1, PB), offset_ref[i].astype(F32))

    place_rows(row_count, capacity, owner_ref, child_ref.shape[0], write)
    width = rows_ref.shape[1]
    out_ref[:, :width] = rows_ref[...]
    out_ref[:, width:] = tag_ref[...]


def pack_lead_body(row_count, capacity, child_count, owner_ref, *refs):
    outs = refs[-2 - row_count : -2]
    own, gots = refs[0], refs[1 : len(refs) - 2 - row_count]
    child_ref, rows_ref = refs[-2:]
    child_ref[...] = pick(own, gots)
    rows_ref[...] = jnp.zeros_like(rows_ref)
    me = lax.axis_index("row")

    def write(i, owner, rank):
        rows_ref[pl.ds((owner ^ me) * capacity + rank, 1), :] = child_ref[pl.ds(i, 1), :]

    place_rows(row_count, capacity, owner_ref, child_count, write)
    for at, out in enumerate(outs):
        out[...] = rows_ref[at * capacity : (at + 1) * capacity, :]


def lead_body(chunk_count, row_count, *refs):
    each = (len(refs) - 6 - row_count) // chunk_count
    chunks = [refs[i * each : (i + 1) * each] for i in range(chunk_count)]
    pieces = refs[chunk_count * each : chunk_count * each + row_count]
    tag_ref = refs[chunk_count * each + row_count]
    lead_ref, left_ref, place_ref, keep_ref, send_ref = refs[-5:]
    me = lax.axis_index("row")
    values = [ref[...] for ref in pieces]
    bit = 1
    while bit < row_count:
        swapped = [values[at ^ bit] for at in range(row_count)]
        values = [jnp.where((me & bit) != 0, b, a) for a, b in zip(values, swapped)]
        bit *= 2
    slots_value = jnp.concatenate(values, axis=0)
    front = jnp.concatenate([pick(c[0], c[1:]) for c in chunks], axis=0)
    rows, slots = front.shape[0], slots_value.shape[0]
    at = lax.broadcasted_iota(jnp.int32, (rows, slots), 0).astype(F32)

    onehot = jnp.where(at == jnp.transpose(tag_ref[...])[0:1, :], 1.0, 0.0).astype(BF16)
    spots = jnp.concatenate([onehot, onehot, onehot], axis=1)
    place_ref[...] = spots
    lead = front + dot(spots, jnp.concatenate(parts3(slots_value)[::-1], axis=0))
    lead_ref[...] = lead
    turned = jnp.transpose(lead)
    left_ref[...] = triple(turned, 1)
    first = dot_high(turned[:HALF], lead[:, :HALF], ((1,), (0,)))
    second = dot_high(turned[HALF:], lead, ((1,), (0,)))
    side = lax.axis_index("row") % 2 == 0
    for out, flip in ((keep_ref, False), (send_ref, True)):
        low = jnp.logical_xor(side, flip)
        out[:, :HALF] = jnp.where(low, first[:PB], first[PB:])
        out[:, HALF:] = jnp.where(low, second[:PB], second[PB:])


def add_body(a_ref, b_ref, out_ref):
    out_ref[...] = a_ref[...] + b_ref[...]


def join_body(a_ref, b_ref, out_ref):
    half = a_ref.shape[0]
    out_ref[:half, :] = a_ref[...]
    out_ref[half:, :] = b_ref[...]


def split_add_body(step, count, keep_ref, got_ref, keep_out, send_out):
    half = keep_out.shape[1]
    side = upper_side(step, count)
    for which, out in ((side, keep_out), (1 - side, send_out)):
        part = pl.ds(pl.multiple_of(which * half, 128), half)
        out[...] = keep_ref[:, part] + got_ref[:, part]


def product_body(blocks, count, base_ref, left_ref, place_ref, front_ref, child_ref, *rest):
    del base_ref
    outs, whole_ref = rest[-1 - count : -1], rest[-1]
    parts = jnp.concatenate(parts3(child_ref[...])[::-1], axis=0)
    whole = front_ref[...] + dot(place_ref[...], parts)
    whole_ref[...] = whole
    result = dot(left_ref[...], triple(whole, 0))
    for at, out in enumerate(outs):

        @pl.when(pl.program_id(0) // blocks == at)
        def _():
            out[...] = result


def spread_lane(tile, at):
    return jnp.broadcast_to(tile[:, at : at + 1], tile.shape)


def invert_factor(block):
    lane = lax.broadcasted_iota(jnp.int32, (8, PB), 1)
    sub = lax.broadcasted_iota(jnp.int32, (8, PB), 0)
    count = PB // 8
    tiles = [block[8 * t : 8 * t + 8, :] for t in range(count)]
    for b in range(count):
        first = 8 * b
        rows = tiles[b]
        cols = [spread_lane(rows, first + c) for c in range(8)]
        heads, inverses = {}, []
        for c in range(8):
            inverse = 1.0 / cols[c][c : c + 1, :]
            inverses.append(inverse)
            factor = jnp.where(sub > c, cols[c] * inverse, 0.0)
            here = lane == first + c
            source = jnp.where(here[0:1, :], 1.0, rows[c : c + 1, :])
            rows = jnp.where(here & (sub > c), 0.0, rows) - factor * source
            for d in range(c + 1, 8):
                heads[c, d] = cols[d][c : c + 1, :]
                cols[d] = cols[d] - factor * heads[c, d]
        tiles[b] = rows
        inside = (lane >= first) & (lane < first + 8)
        past = inside & (lane - first >= sub)
        used = jnp.where(past, jnp.where(lane - first == sub, 1.0, 0.0), rows)
        for t in range(b + 1, count):
            tile = tiles[t]
            factors = []
            for c in range(8):
                factor = spread_lane(tile, first + c)
                for d in range(c):
                    factor = factor - factors[d] * heads[d, c]
                factors.append(factor * inverses[c])
            tile = jnp.where(inside, 0.0, tile)
            for c in range(8):
                tile = tile - factors[c] * used[c : c + 1, :]
            tiles[t] = tile
    done = []
    for t in range(count):
        diagonal = lane == sub + 8 * t
        pivot = jnp.sum(jnp.where(diagonal, tiles[t], 0.0), axis=1, keepdims=True)
        scale = lax.rsqrt(pivot)
        scale = scale * (1.5 - 0.5 * pivot * scale * scale)
        unit = jnp.where(diagonal, 1.0, jnp.where(lane < sub + 8 * t, tiles[t], 0.0))
        done.append(unit * scale)
    return jnp.concatenate(done, axis=0)


def eliminate_body(k, *refs):
    out_ref = refs[-1]
    lo, hi = k * PB, (k + 1) * PB
    if k == 0:
        mine, got = refs[0][...], refs[1][...]
        low = lax.axis_index("row") % 2 == 0
        packed = jnp.concatenate([jnp.where(low, mine, got), jnp.where(low, got, mine)], axis=0)
        cross = packed[:, HALF:LEAD]
        out_ref[:HALF, :HALF] = packed[:, :HALF]
        out_ref[HALF:, :HALF] = cross
        out_ref[:HALF, HALF:] = jnp.transpose(cross)
        out_ref[HALF:, HALF:] = packed[:, LEAD:]
        in_ref = out_ref
    else:
        in_ref = refs[0]
        out_ref[:lo, :] = in_ref[:lo, :]
    inverse = invert_factor(in_ref[lo:hi, lo:hi])
    pieces = []
    for j in range(PANELS):
        if j == k:
            pieces.append(inverse)
        else:
            pieces.append(dot_high(inverse, in_ref[lo:hi, j * PB : (j + 1) * PB], ((1,), (0,))))
    row = jnp.concatenate(pieces, axis=1)
    out_ref[lo:hi, :] = row
    if k < PANELS - 1:
        column = dot_high(in_ref[hi:, lo:hi], inverse, ((1,), (1,)))
        change = dot_high(column, row, ((1,), (0,)))
        later = in_ref[hi:, :]
        out_ref[hi:, :] = later - change
        out_ref[hi:, lo:hi] = -change[:, lo:hi]


def finish_body(scale, matrix_ref, lead_ref, top_ref, bottom_ref, basis3_ref, basis_ref):
    own = lax.broadcasted_iota(jnp.int32, (LEAD, LEAD), 0) // PB
    other = lax.broadcasted_iota(jnp.int32, (LEAD, LEAD), 1) // PB
    inverse = jnp.where(own >= other, matrix_ref[...], 0.0)
    top_ref[...] = triple(inverse[:HALF, :HALF], 1)
    bottom_ref[...] = triple(inverse[HALF:], 1)
    basis = dot_high(lead_ref[...], inverse, ((1,), (1,)))
    basis3_ref[...] = triple(basis, 1)
    basis_ref[...] = basis * scale


def project_body(blocks, places_ref, top_ref, bottom_ref, basis_ref, *refs):
    del places_ref
    near_even, near_odd, far_even, far_odd, front_ref = refs[:5]
    upper_ref, out_ref = refs[-2:]
    near = pl.program_id(0) < blocks
    sums = jnp.concatenate(
        [
            jnp.where(near, near_even[...], far_even[...]),
            jnp.where(near, near_odd[...], far_odd[...]),
        ],
        axis=1,
    )
    hi, lo = parts2(sums)
    upper_ref[:HALF, :] = dot(
        top_ref[...], jnp.concatenate([hi[:HALF], lo[:HALF], hi[:HALF]], axis=0)
    )
    upper_ref[HALF:, :] = dot(bottom_ref[...], jnp.concatenate([hi, lo, hi], axis=0))
    out_ref[...] = front_ref[...] - dot(basis_ref[...], triple(upper_ref[...], 0))


def plan(tasks, link_rate, near_rate, lag):
    ready_link = {"near": 0.0, "far": 0.0}
    arrival, order, now = {}, [], 0.0
    left = dict(tasks)
    ended = {}

    def when(name):
        latest = 0.0
        for before, way, size in tasks[name][2]:
            if before not in ended:
                return None
            latest = max(latest, arrival.get((before, way), ended[before]))
        return latest

    while left:
        known = [(when(name), left[name][0], at, name) for at, name in enumerate(left)]
        known = [entry for entry in known if entry[0] is not None]
        free = [entry for entry in known if entry[0] <= now]
        chosen = min(free, key=lambda e: (e[1], e[2])) if free else min(known)
        name = chosen[3]
        now = max(now, chosen[0]) + tasks[name][1]
        ended[name] = now
        order.append((name, now))
        del left[name]
        sent = {}
        for other in tasks:
            for before, way, size in tasks[other][2]:
                if before == name and way:
                    sent[way] = max(size, sent.get(way, 0))
        for way, size in sent.items():
            begin = max(now, ready_link[way])
            ready_link[way] = begin + size / (near_rate if way == "near" else link_rate)
            arrival[name, way] = ready_link[way] + lag
    return order


def task_list(steps, chunks, width):
    tasks = {}
    gram = HALF // 2 * (LEAD + HALF) * 4e-6
    for t in range(steps):
        before = [("lead", None, 0), ("lead", "near", gram)] if t == 0 else [
            (("gram", t - 1), None, 0), (("gram", t - 1), "far", gram)
        ]
        tasks["gram", t] = (0, 1.0, before)
    tasks["lead"] = (0, 0.0, [])
    for k in range(PANELS):
        before = [(("factor", k - 1), None, 0)] if k else [(("gram", steps - 1), "near", gram)]
        tasks["factor", k] = (3, 5.2, before)
    tasks["finish"] = (3, 2.4, [(("factor", PANELS - 1), None, 0)])
    tasks["send", 0] = (2, 8.0, [("lead", None, 0)])
    tasks["keep", 0] = (2, 8.0, [(("send", 0), None, 0)])
    for c in range(chunks):
        size = LEAD * width * 4e-6
        last = ("send", 0)
        for t in range(1, steps):
            way = "near" if t == 1 else "far"
            before = [(last, way, size)] + ([(("keep", 0), None, 0)] if t == 1 else [])
            tasks["split", c, t] = (1, 1.4, before)
            size = size / 2
            last = ("split", c, t)
        tasks["sum", c] = (1, 0.8, [(last, "far", size)])
        last = ("sum", c)
        for t in reversed(range(1, steps)):
            tasks["join", c, t] = (1, 0.9, [(last, "far", size)])
            size = size * 2
            last = ("join", c, t)
        tasks["project", c] = (4, 6.2, [(last, "near", size), ("finish", None, 0)])
    return tasks


ORDER = (
    "G0 P0 G1 K0 S01 S11 S21 S31 G2 S02 S12 E0 S22 S32 A0 E1 A1 A2 E2 A3 J02 J12 E3 J22 J01 F J32 J11 X0 J21 X1 J31 X2 X3"
)
KINDS = {"P": "send", "K": "keep", "S": "split", "G": "gram", "E": "factor", "A": "sum", "J": "join", "X": "project"}


def sequence(steps, chunks, width):
    tasks = task_list(steps, chunks, width)
    named = []
    for word in ORDER.split():
        named.append("finish" if word == "F" else (KINDS[word[0]],) + tuple(int(d) for d in word[1:]))
    if set(named) == set(tasks) - {"lead"}:
        return named
    return [task for task, _ in plan(tasks, 0.09, 0.4, 5.0)]


def on_device(front_matrix, child_rows, child_owner, child_offset):
    row_count = lax.axis_size("row")
    col_count = lax.axis_size("col")
    local_rows, local_cols = front_matrix.shape
    child_count = child_rows.shape[0]
    capacity = 2 * child_count // row_count
    slots = row_count * capacity
    steps = row_count.bit_length() - 1
    owner, offset = child_owner[:, 0], child_offset[:, 0]
    run = Chain()

    pieces = 2
    sizes = [local_rows // pieces] * pieces
    *own, lead_child, packed = run(
        "pack_children", functools.partial(pack_body, row_count, capacity, float(local_rows), pieces),
        [owner, offset, child_rows, front_matrix],
        [SCALARS, SCALARS, WHOLE, full((local_rows, LEAD))],
        [f32(n, LEAD) for n in sizes] + [f32(child_count, LEAD), f32(slots, local_cols + PB)],
        [WHOLE] * (pieces + 2),
        scratch=[pltpu.VMEM((slots, local_cols), F32), pltpu.VMEM((slots, PB), F32)],
    )
    child = exchange(packed, row_count)
    lead_got = spread(lead_child, col_count)
    got = [spread(piece, col_count) for piece in own]
    lead_pieces = list(
        run(
            "pack_lead", functools.partial(pack_lead_body, row_count, capacity, child_count),
            [owner, lead_child] + lead_got + [child] + got[0],
            [SCALARS] + [WHOLE] * (1 + len(lead_got)) + [ANYWHERE] * (1 + len(got[0])),
            [f32(capacity, LEAD)] * row_count, [WHOLE] * row_count,
            scratch=[pltpu.VMEM((child_count, LEAD), F32), pltpu.VMEM((slots, LEAD), F32)],
        )
    )
    for mask in range(1, row_count):
        pairs = [(d, d ^ mask) for d in range(row_count)]
        lead_pieces[mask] = lax.ppermute(lead_pieces[mask], "row", pairs)
    operands = [ref for piece, arrived in zip(own, got) for ref in [piece] + arrived]
    lead, left, place, gram, gram_send = run(
        "lead_setup", functools.partial(lead_body, pieces, row_count),
        operands + lead_pieces + [child],
        [WHOLE] * (len(operands) + row_count) + [pl.BlockSpec((slots, PB), lambda i: (0, local_cols // PB))],
        [f32(local_rows, LEAD), bf16(LEAD, 3 * local_rows), bf16(local_rows, 3 * slots),
         f32(HALF // 2, LEAD + HALF), f32(HALF // 2, LEAD + HALF)],
        [WHOLE] * 5,
    )

    chunks = max(1, min(CHUNKS, local_cols // (PB * row_count)))
    width = local_cols // 2 // chunks
    blocks = width // BLOCK
    core = upper_side(0, row_count)
    order = jnp.asarray(piece_order(row_count))[lax.axis_index("row")]
    scale = math.sqrt(local_rows * row_count)
    front = upper = matrix = factor = scaled = None
    gram_got = swap(gram_send, 0, row_count)
    keep, arrived, far = {}, {}, {}

    def make(half, front):
        base = (half * chunks * blocks + jnp.arange(chunks * blocks)).astype(jnp.int32)
        operands = [left, place, front_matrix, child]
        in_specs = [
            full(left.shape),
            full(place.shape),
            pl.BlockSpec((local_rows, BLOCK), lambda i, b: (0, b[i])),
            pl.BlockSpec((slots, BLOCK), lambda i, b: (0, b[i])),
        ]
        aliases = {}
        if front is not None:
            operands.append(front)
            in_specs.append(ANYWHERE)
            aliases = {5: chunks}

        def out_block(at):
            return lambda i, b: (0, jnp.clip(i - at * blocks, 0, blocks - 1))

        out_specs = [pl.BlockSpec((LEAD, BLOCK), out_block(at)) for at in range(chunks)]
        out_specs.append(pl.BlockSpec((local_rows, BLOCK), lambda i, b: (0, b[i])))
        return run(
            "lead_product", functools.partial(product_body, blocks, chunks), operands, in_specs,
            [f32(LEAD, width)] * chunks + [f32(local_rows, local_cols)], out_specs,
            scalars=[base], grid=(blocks * chunks,), aliases=aliases,
        )

    def cast(c, value, step):
        keep[c], arrived[c] = value, swap(value, step, row_count)

    for task in sequence(steps, chunks, width):
        kind, c = task[0], task[1]
        if task == "lead":
            continue
        if task == "finish":
            top, bottom, basis, scaled = run(
                "finish_factor", functools.partial(finish_body, scale), [matrix, lead], [WHOLE] * 2,
                [bf16(HALF, 3 * HALF), bf16(HALF, 3 * LEAD), bf16(local_rows, 3 * LEAD), f32(local_rows, LEAD)],
                [WHOLE] * 4,
            )
        elif kind == "gram":
            gram = run("add_gram", add_body, [gram, gram_got], [WHOLE] * 2, [f32(*gram.shape)], [WHOLE])
            gram_got = swap(gram, (c + 1) % steps, row_count)
        elif kind == "factor":
            operands = [gram, gram_got] if c == 0 else [matrix]
            matrix = run(
                "eliminate_panel", functools.partial(eliminate_body, c), operands,
                [WHOLE] * len(operands), [f32(LEAD, LEAD)], [WHOLE],
            )
        elif kind == "send":
            *made, front = make(1 - core, front)
            for at, value in enumerate(made):
                arrived[at] = swap(value, 0, row_count)
        elif kind == "keep":
            *made, front = make(core, front)
            for at, value in enumerate(made):
                keep[at] = value
        elif kind == "split":
            t = task[2]
            shape = f32(LEAD, keep[c].shape[1] // 2)
            keep[c], send = run(
                "split_add", functools.partial(split_add_body, t, row_count), [keep[c], arrived[c]],
                [WHOLE] * 2, [shape, shape], [WHOLE] * 2,
            )
            arrived[c] = swap(send, t, row_count)
        elif kind == "sum":
            value = run("add_shard", add_body, [keep[c], arrived[c]], [WHOLE] * 2, [f32(*keep[c].shape)], [WHOLE])
            cast(c, value, steps - 1)
        elif kind == "join":
            rows, value_width = keep[c].shape
            value = run("join_pieces", join_body, [keep[c], arrived[c]], [WHOLE] * 2, [f32(2 * rows, value_width)], [WHOLE])
            cast(c, value, task[2] - 1)
        elif kind == "project":
            starts = [(half * chunks + c) * blocks for half in (core, 1 - core)]
            columns = jnp.concatenate([s + jnp.arange(blocks, dtype=jnp.int32) for s in starts])
            scalars = [jnp.concatenate([columns, order[0], order[1]])]
            near, per = 2 * blocks, keep[c].shape[1] // PB
            far_at = near + 2 * blocks // per

            def near_piece(odd):
                def at(i, p):
                    place = 2 * jnp.minimum(i, blocks - 1) + odd
                    return p[near + place // per], place % per

                return at

            def far_piece(odd):
                def at(i, p):
                    place = 2 * jnp.maximum(i - blocks, 0) + odd
                    return p[far_at + place // per], place % per

                return at

            operands = [top, bottom, basis, keep[c], keep[c], arrived[c], arrived[c], front]
            in_specs = [
                pl.BlockSpec(top.shape, lambda i, p: (0, 0)),
                pl.BlockSpec(bottom.shape, lambda i, p: (0, 0)),
                pl.BlockSpec(basis.shape, lambda i, p: (0, 0)),
                pl.BlockSpec((LEAD, PB), near_piece(0)),
                pl.BlockSpec((LEAD, PB), near_piece(1)),
                pl.BlockSpec((LEAD, PB), far_piece(0)),
                pl.BlockSpec((LEAD, PB), far_piece(1)),
                pl.BlockSpec((local_rows, BLOCK), lambda i, p: (0, p[i])),
            ]
            aliases = {8: 1}
            if upper is not None:
                operands.append(upper)
                in_specs.append(ANYWHERE)
                aliases[9] = 0
            upper, front = run(
                "project_columns", functools.partial(project_body, blocks), operands, in_specs,
                [f32(LEAD, local_cols), f32(local_rows, local_cols)],
                [pl.BlockSpec((LEAD, BLOCK), lambda i, p: (0, p[i])), pl.BlockSpec((local_rows, BLOCK), lambda i, p: (0, p[i]))],
                scalars=scalars, grid=(2 * blocks,), aliases=aliases,
            )
    return upper, front, scaled


def solution(mesh):
    placed = (P("row", "col"), P("row", "col"), P("row", None), P("row", None))
    return jax.shard_map(
        on_device,
        mesh=mesh,
        in_specs=placed,
        out_specs=(P(None, "col"), P("row", "col"), P("row", None)),
        check_vma=False,
    )
```

```python
import functools
import math

import jax
import jax.numpy as jnp
import numpy as np
from jax import lax
from jax.experimental import pallas as pl
from jax.experimental.pallas import tpu as pltpu
from jax.sharding import PartitionSpec as P

PB = 128
PANELS = 4
LEAD = PB * PANELS
HALF = LEAD // 2
BLOCK = 256
LAG = 2
VMEM_BYTES = 48 * 1024 * 1024
HIGHEST = lax.Precision.HIGHEST
F32 = jnp.float32
BF16 = jnp.bfloat16
SMEM = pltpu.SMEM
VMEM = pltpu.VMEM


def params():
    return pltpu.CompilerParams(vmem_limit_bytes=VMEM_BYTES)


def cost(flops):
    return pl.CostEstimate(flops=flops, bytes_accessed=1 << 20, transcendentals=0)


def mask_orders(count):
    others = [1 << b for b in range(1, count.bit_length() - 1)]
    half = len(others) // 2
    return ([1] + others, [1] + others[half:] + others[:half])


def swap(value, step, count):
    orders = mask_orders(count)
    pairs = [(d, d ^ orders[d & 1][step]) for d in range(count)]
    return lax.ppermute(value, "row", pairs)


def upper_side(step, count):
    orders = mask_orders(count)
    me = lax.axis_index("row")
    mask = jnp.where(me & 1 == 0, orders[0][step], orders[1][step])
    return ((me & mask) != 0).astype(jnp.int32)


def shard_table(count):
    orders = mask_orders(count)
    steps = len(orders[0])
    return np.array(
        [
            sum(((d & orders[d & 1][t]) != 0) << (steps - 1 - t) for t in range(steps))
            for d in range(count)
        ]
    )


def piece_order(count):
    orders = mask_orders(count)
    steps = len(orders[0])
    shard = shard_table(count)

    def pieces(device, done):
        if done == 0:
            return [device]
        mask = orders[device & 1][steps - done]
        return pieces(device, done - 1) + pieces(device ^ mask, done - 1)

    half = count // 2
    order = np.zeros((count, 2, half), np.int32)
    for d in range(count):
        for at, piece in enumerate(pieces(d, steps)):
            order[d, at // half, shard[piece] % half] = at % half
    return order


def split_add_kernel(side_ref, keep_ref, got_ref, keep_out, send_out):
    half = keep_out.shape[1]
    for which, out in ((side_ref[0], keep_out), (1 - side_ref[0], send_out)):
        part = pl.ds(pl.multiple_of(which * half, 128), half)
        out[...] = keep_ref[:, part] + got_ref[:, part]


def split_add(side, keep, got):
    half = jax.ShapeDtypeStruct((keep.shape[0], keep.shape[1] // 2), F32)
    return pl.pallas_call(
        split_add_kernel,
        out_shape=(half, half),
        in_specs=[
            pl.BlockSpec(memory_space=SMEM),
            pl.BlockSpec(memory_space=VMEM),
            pl.BlockSpec(memory_space=VMEM),
        ],
        out_specs=(pl.BlockSpec(memory_space=VMEM), pl.BlockSpec(memory_space=VMEM)),
        compiler_params=params(),
        name="split_add",
    )(side[None], keep, got)


def scatter_sum(keep, send, count):
    steps = count.bit_length() - 1
    for step in range(steps):
        got = swap(send, step, count)
        if step == steps - 1:
            return keep + got
        keep, send = split_add(upper_side(step + 1, count), keep, got)


def total(value, count):
    side = upper_side(0, count)
    half = value.shape[0] // 2
    keep = lax.dynamic_slice_in_dim(value, side * half, half, 0)
    send = lax.dynamic_slice_in_dim(value, (1 - side) * half, half, 0)
    mine = keep + swap(send, 0, count)
    for step in range(1, count.bit_length() - 1):
        mine = mine + swap(mine, step, count)
    got = swap(mine, 0, count)
    return jnp.where(
        side == 0,
        jnp.concatenate([mine, got], axis=0),
        jnp.concatenate([got, mine], axis=0),
    )


def spread(value, count):
    me = lax.axis_index("col")
    stride = count
    while stride > 1:
        half = stride // 2
        pairs = [(c, c + half) for c in range(0, count, stride)]
        got = lax.ppermute(value, "col", pairs)
        value = jnp.where(me % stride == half, got, value)
        stride = half
    return value


def parts3(x):
    hi = x.astype(BF16)
    rest = x - hi.astype(F32)
    mid = rest.astype(BF16)
    return hi, mid, (rest - mid.astype(F32)).astype(BF16)


def parts2(x):
    hi = x.astype(BF16)
    return hi, (x - hi.astype(F32)).astype(BF16)


def pack_kernel(row_count, capacity, sentinel, owner_ref, offset_ref, child_ref, *rest):
    out_ref, tag_ref, tally = rest[-3:]
    out_ref[...] = jnp.zeros_like(out_ref)
    tag_ref[...] = jnp.full(tag_ref.shape, sentinel, F32)
    for d in range(row_count):
        tally[d] = 0

    def body(i, carry):
        owner = owner_ref[i]
        rank = tally[owner]
        tally[owner] = rank + 1
        slot = owner * capacity + rank
        out_ref[pl.ds(slot, 1), :] = child_ref[pl.ds(i, 1), :]
        tag_ref[pl.ds(slot, 1), :] = jnp.full((1, tag_ref.shape[1]), offset_ref[i].astype(F32))
        return carry

    lax.fori_loop(0, child_ref.shape[0], body, 0)


def pack(child_rows, owner, offset, row_count, capacity, sentinel, after=()):
    slots = row_count * capacity
    return pl.pallas_call(
        functools.partial(pack_kernel, row_count, capacity, float(sentinel)),
        out_shape=(
            jax.ShapeDtypeStruct((slots, child_rows.shape[1]), F32),
            jax.ShapeDtypeStruct((slots, PB), F32),
        ),
        in_specs=[
            pl.BlockSpec(memory_space=SMEM),
            pl.BlockSpec(memory_space=SMEM),
            pl.BlockSpec(memory_space=VMEM),
        ]
        + [pl.BlockSpec(memory_space=pl.ANY)] * len(after),
        out_specs=(pl.BlockSpec(memory_space=VMEM), pl.BlockSpec(memory_space=VMEM)),
        scratch_shapes=[pltpu.SMEM((row_count,), jnp.int32)],
        compiler_params=params(),
        name="pack_children",
    )(owner, offset, child_rows, *after)


def triple(x, axis):
    hi, lo = parts2(x)
    return jnp.concatenate([hi, hi, lo] if axis == 1 else [hi, lo, hi], axis=axis)


def lead_kernel(front_ref, child_ref, tag_ref, lead_ref, left_ref, place_ref, gram_ref):
    rows = front_ref.shape[0]
    slots = child_ref.shape[0]
    place = jnp.transpose(tag_ref[...])[0:1, :]
    at = lax.broadcasted_iota(jnp.int32, (rows, slots), 0).astype(F32)
    onehot = jnp.where(at == place, 1.0, 0.0).astype(BF16)
    spots = jnp.concatenate([onehot, onehot, onehot], axis=1)
    place_ref[...] = spots
    parts = jnp.concatenate(parts3(child_ref[...])[::-1], axis=0)
    lead = front_ref[...] + jnp.dot(spots, parts, preferred_element_type=F32)
    lead_ref[...] = lead
    turned = jnp.transpose(lead)
    left_ref[...] = triple(turned, 1)
    gram_ref[:, :HALF] = dot_high(turned[:HALF], lead[:, :HALF], ((1,), (0,)))
    gram_ref[:, HALF:] = dot_high(turned[HALF:], lead, ((1,), (0,)))


def lead_setup(front, child, tags):
    rows = front.shape[0]
    slots = child.shape[0]
    return pl.pallas_call(
        lead_kernel,
        out_shape=(
            jax.ShapeDtypeStruct((rows, LEAD), F32),
            jax.ShapeDtypeStruct((LEAD, 3 * rows), BF16),
            jax.ShapeDtypeStruct((rows, 3 * slots), BF16),
            jax.ShapeDtypeStruct((HALF, LEAD + HALF), F32),
        ),
        in_specs=[pl.BlockSpec(memory_space=VMEM)] * 3,
        out_specs=(pl.BlockSpec(memory_space=VMEM),) * 4,
        compiler_params=params(),
        name="lead_setup",
    )(front, child, tags)


def product_kernel(blocks, chunks, base_ref, left_ref, place_ref, front_ref, child_ref, *rest):
    del base_ref
    outs, whole_ref = rest[-1 - chunks : -1], rest[-1]
    parts = jnp.concatenate(parts3(child_ref[...])[::-1], axis=0)
    whole = front_ref[...] + jnp.dot(place_ref[...], parts, preferred_element_type=F32)
    whole_ref[...] = whole
    result = jnp.dot(left_ref[...], triple(whole, 0), preferred_element_type=F32)
    for at, out in enumerate(outs):

        @pl.when(pl.program_id(0) // blocks == at)
        def _():
            out[...] = result


def product(half, left, place, front, child, whole, chunks):
    rows, columns = front.shape
    slots = child.shape[0]
    steps = columns // 2 // BLOCK
    blocks = steps // chunks
    in_specs = [
        pl.BlockSpec(left.shape, lambda i, h: (0, 0)),
        pl.BlockSpec(place.shape, lambda i, h: (0, 0)),
        pl.BlockSpec((rows, BLOCK), lambda i, h: (0, h[0] * steps + i)),
        pl.BlockSpec((slots, BLOCK), lambda i, h: (0, h[0] * steps + i)),
    ]
    operands = [half[None], left, place, front, child]
    aliases = {}
    if whole is not None:
        in_specs.append(pl.BlockSpec(memory_space=pl.ANY))
        operands.append(whole)
        aliases = {5: chunks}

    def out_block(at):
        return lambda i, h: (0, jnp.clip(i - at * blocks, 0, blocks - 1))

    return pl.pallas_call(
        functools.partial(product_kernel, blocks, chunks),
        grid_spec=pltpu.PrefetchScalarGridSpec(
            num_scalar_prefetch=1,
            grid=(steps,),
            in_specs=in_specs,
            out_specs=tuple(pl.BlockSpec((LEAD, BLOCK), out_block(at)) for at in range(chunks))
            + (pl.BlockSpec((rows, BLOCK), lambda i, h: (0, h[0] * steps + i)),),
        ),
        out_shape=(jax.ShapeDtypeStruct((LEAD, columns // 2 // chunks), F32),) * chunks
        + (jax.ShapeDtypeStruct((rows, columns), F32),),
        input_output_aliases=aliases,
        compiler_params=params(),
        name="lead_product",
    )(*operands)


def join_kernel(a_ref, b_ref, after_ref, out_ref):
    del after_ref
    half = a_ref.shape[0]
    out_ref[:half, :] = a_ref[...]
    out_ref[half:, :] = b_ref[...]


def join(a, b, after):
    return pl.pallas_call(
        join_kernel,
        out_shape=jax.ShapeDtypeStruct((2 * a.shape[0], a.shape[1]), F32),
        in_specs=[pl.BlockSpec(memory_space=VMEM)] * 2 + [pl.BlockSpec(memory_space=pl.ANY)],
        out_specs=pl.BlockSpec(memory_space=VMEM),
        compiler_params=params(),
        name="join_pieces",
    )(a, b, after)


def dot_high(a, b, dims):
    return lax.dot_general(a, b, (dims, ((), ())), precision=HIGHEST, preferred_element_type=F32)


def spread_lane(tile, at):
    return jnp.broadcast_to(tile[:, at : at + 1], tile.shape)


def invert_factor(block):
    lane = lax.broadcasted_iota(jnp.int32, (8, PB), 1)
    sub = lax.broadcasted_iota(jnp.int32, (8, PB), 0)
    count = PB // 8
    tiles = [block[8 * t : 8 * t + 8, :] for t in range(count)]
    for b in range(count):
        first = 8 * b
        rows = tiles[b]
        cols = [spread_lane(rows, first + c) for c in range(8)]
        heads, inverses = {}, []
        for c in range(8):
            inverse = 1.0 / cols[c][c : c + 1, :]
            inverses.append(inverse)
            factor = jnp.where(sub > c, cols[c] * inverse, 0.0)
            here = lane == first + c
            source = jnp.where(here[0:1, :], 1.0, rows[c : c + 1, :])
            rows = jnp.where(here & (sub > c), 0.0, rows) - factor * source
            for d in range(c + 1, 8):
                heads[c, d] = cols[d][c : c + 1, :]
                cols[d] = cols[d] - factor * heads[c, d]
        tiles[b] = rows
        inside = (lane >= first) & (lane < first + 8)
        past = inside & (lane - first >= sub)
        used = jnp.where(past, jnp.where(lane - first == sub, 1.0, 0.0), rows)
        for t in range(b + 1, count):
            tile = tiles[t]
            factors = []
            for c in range(8):
                factor = spread_lane(tile, first + c)
                for d in range(c):
                    factor = factor - factors[d] * heads[d, c]
                factors.append(factor * inverses[c])
            tile = jnp.where(inside, 0.0, tile)
            for c in range(8):
                tile = tile - factors[c] * used[c : c + 1, :]
            tiles[t] = tile
    done = []
    for t in range(count):
        diagonal = lane == sub + 8 * t
        pivot = jnp.sum(jnp.where(diagonal, tiles[t], 0.0), axis=1, keepdims=True)
        scale = lax.rsqrt(pivot)
        scale = scale * (1.5 - 0.5 * pivot * scale * scale)
        unit = jnp.where(diagonal, 1.0, jnp.where(lane < sub + 8 * t, tiles[t], 0.0))
        done.append(unit * scale)
    return jnp.concatenate(done, axis=0)


def eliminate_kernel(k, in_ref, out_ref):
    lo, hi = k * PB, (k + 1) * PB
    if k == 0:
        cross = in_ref[:, HALF:LEAD]
        out_ref[:HALF, :HALF] = in_ref[:, :HALF]
        out_ref[HALF:, :HALF] = cross
        out_ref[:HALF, HALF:] = jnp.transpose(cross)
        out_ref[HALF:, HALF:] = in_ref[:, LEAD:]
        in_ref = out_ref
    else:
        out_ref[:lo, :] = in_ref[:lo, :]
    inverse = invert_factor(in_ref[lo:hi, lo:hi])
    pieces = []
    for j in range(PANELS):
        if j == k:
            pieces.append(inverse)
        else:
            pieces.append(dot_high(inverse, in_ref[lo:hi, j * PB : (j + 1) * PB], ((1,), (0,))))
    row = jnp.concatenate(pieces, axis=1)
    out_ref[lo:hi, :] = row
    if k < PANELS - 1:
        column = dot_high(in_ref[hi:, lo:hi], inverse, ((1,), (1,)))
        change = dot_high(column, row, ((1,), (0,)))
        later = in_ref[hi:, :]
        out_ref[hi:, :] = later - change
        out_ref[hi:, lo:hi] = -change[:, lo:hi]


def eliminate(matrix, k):
    return pl.pallas_call(
        functools.partial(eliminate_kernel, k),
        out_shape=jax.ShapeDtypeStruct((LEAD, LEAD), F32),
        in_specs=[pl.BlockSpec(memory_space=VMEM)],
        out_specs=pl.BlockSpec(memory_space=VMEM),
        compiler_params=params(),
        cost_estimate=cost(6 * 10**9),
        name="eliminate_panel",
    )(matrix)


def finish_kernel(scale, matrix_ref, lead_ref, top_ref, bottom_ref, basis3_ref, basis_ref):
    own = lax.broadcasted_iota(jnp.int32, (LEAD, LEAD), 0) // PB
    other = lax.broadcasted_iota(jnp.int32, (LEAD, LEAD), 1) // PB
    inverse = jnp.where(own >= other, matrix_ref[...], 0.0)
    top_ref[...] = triple(inverse[:HALF, :HALF], 1)
    bottom_ref[...] = triple(inverse[HALF:], 1)
    basis = dot_high(lead_ref[...], inverse, ((1,), (1,)))
    basis3_ref[...] = triple(basis, 1)
    basis_ref[...] = basis * scale


def finish(matrix, lead, scale):
    rows = lead.shape[0]
    return pl.pallas_call(
        functools.partial(finish_kernel, scale),
        out_shape=(
            jax.ShapeDtypeStruct((HALF, 3 * HALF), BF16),
            jax.ShapeDtypeStruct((HALF, 3 * LEAD), BF16),
            jax.ShapeDtypeStruct((rows, 3 * LEAD), BF16),
            jax.ShapeDtypeStruct((rows, LEAD), F32),
        ),
        in_specs=[pl.BlockSpec(memory_space=VMEM)] * 2,
        out_specs=(pl.BlockSpec(memory_space=VMEM),) * 4,
        compiler_params=params(),
        cost_estimate=cost(2 * 10**9),
        name="finish_factor",
    )(matrix, lead)


def project_kernel(blocks, places_ref, top_ref, bottom_ref, basis_ref, *rest):
    del places_ref
    near_even, near_odd, far_even, far_odd, front_ref = rest[:5]
    upper_ref, out_ref, done_ref = rest[-3:]
    done_ref[...] = jnp.zeros_like(done_ref)
    near = pl.program_id(0) < blocks
    sums = jnp.concatenate(
        [
            jnp.where(near, near_even[...], far_even[...]),
            jnp.where(near, near_odd[...], far_odd[...]),
        ],
        axis=1,
    )
    hi, lo = parts2(sums)
    upper_ref[:HALF, :] = jnp.dot(
        top_ref[...],
        jnp.concatenate([hi[:HALF], lo[:HALF], hi[:HALF]], axis=0),
        preferred_element_type=F32,
    )
    upper_ref[HALF:, :] = jnp.dot(
        bottom_ref[...], jnp.concatenate([hi, lo, hi], axis=0), preferred_element_type=F32
    )
    out_ref[...] = front_ref[...] - jnp.dot(
        basis_ref[...], triple(upper_ref[...], 0), preferred_element_type=F32
    )


def project(columns_at, order, factor, near, far, front, upper):
    top, bottom, basis = factor
    rows, columns = front.shape
    blocks = near.shape[0] // LEAD // 2
    near_at, far_at = 2 * blocks, 4 * blocks

    def near_piece(odd):
        return lambda i, p: (p[near_at + 2 * jnp.minimum(i, blocks - 1) + odd], 0)

    def far_piece(odd):
        return lambda i, p: (p[far_at + 2 * jnp.maximum(i - blocks, 0) + odd], 0)

    in_specs = [
        pl.BlockSpec(top.shape, lambda i, p: (0, 0)),
        pl.BlockSpec(bottom.shape, lambda i, p: (0, 0)),
        pl.BlockSpec(basis.shape, lambda i, p: (0, 0)),
        pl.BlockSpec((LEAD, PB), near_piece(0)),
        pl.BlockSpec((LEAD, PB), near_piece(1)),
        pl.BlockSpec((LEAD, PB), far_piece(0)),
        pl.BlockSpec((LEAD, PB), far_piece(1)),
        pl.BlockSpec((rows, BLOCK), lambda i, p: (0, p[i])),
    ]
    places = jnp.concatenate([columns_at, order[0], order[1]])
    operands = [places, top, bottom, basis, near, near, far, far, front]
    aliases = {8: 1}
    if upper is not None:
        in_specs.append(pl.BlockSpec(memory_space=pl.ANY))
        operands.append(upper)
        aliases[9] = 0
    return pl.pallas_call(
        functools.partial(project_kernel, blocks),
        grid_spec=pltpu.PrefetchScalarGridSpec(
            num_scalar_prefetch=1,
            grid=(2 * blocks,),
            in_specs=in_specs,
            out_specs=(
                pl.BlockSpec((LEAD, BLOCK), lambda i, p: (0, p[i])),
                pl.BlockSpec((rows, BLOCK), lambda i, p: (0, p[i])),
                pl.BlockSpec((8, PB), lambda i, p: (0, 0)),
            ),
        ),
        out_shape=(
            jax.ShapeDtypeStruct((LEAD, columns), F32),
            jax.ShapeDtypeStruct((rows, columns), F32),
            jax.ShapeDtypeStruct((8, PB), F32),
        ),
        input_output_aliases=aliases,
        compiler_params=params(),
        cost_estimate=cost(3 * 10**9),
        name="project_columns",
    )(*operands)


def exchange(value, row_count):
    slots, width = value.shape
    shaped = value.reshape(row_count, slots // row_count, width)
    return lax.all_to_all(shaped, "row", split_axis=0, concat_axis=0, tiled=True).reshape(
        slots, width
    )


def on_device(front_matrix, child_rows, child_owner, child_offset):
    row_count = lax.axis_size("row")
    col_count = lax.axis_size("col")
    local_rows, local_cols = front_matrix.shape
    child_count = child_rows.shape[0]
    capacity = 2 * child_count // row_count
    me = lax.axis_index("row")

    owner, offset = child_owner[:, 0], child_offset[:, 0]
    lead_child = spread(child_rows[:, :LEAD], col_count)
    cut = local_rows // 2
    lead_front = jnp.concatenate(
        [
            spread(front_matrix[:cut, :LEAD], col_count),
            spread(front_matrix[cut:, :LEAD], col_count),
        ],
        axis=0,
    )
    packed, tags = pack(child_rows, owner, offset, row_count, capacity, local_rows)
    child = exchange(packed, row_count)
    packed, tags = pack(lead_child, owner, offset, row_count, capacity, local_rows, (child,))
    lead_child = exchange(jnp.concatenate([packed, tags], axis=1), row_count)
    lead, left, place, gram = lead_setup(lead_front, lead_child[:, :LEAD], lead_child[:, LEAD:])

    matrix = total(gram, row_count)
    for k in range(PANELS):
        matrix = eliminate(matrix, k)
    scale = math.sqrt(local_rows * row_count)
    top, bottom, basis, scaled = finish(matrix, lead, scale)

    chunks = max(1, min(4, local_cols // (PB * row_count)))
    width = local_cols // 2 // chunks
    blocks = width // BLOCK
    core = upper_side(0, row_count)
    *send, front = product(1 - core, left, place, front_matrix, child, None, chunks)
    *keep, front = product(core, left, place, front_matrix, child, front, chunks)
    shards = [scatter_sum(keep[c], send[c], row_count) for c in range(chunks)]
    steps = row_count.bit_length() - 1
    order = jnp.asarray(piece_order(row_count))[me]
    upper = None
    done = []
    for c in range(chunks):
        buf = shards[c]
        for step in reversed(range(steps)):
            got = swap(buf, step, row_count)
            if step == 1 and c >= LAG:
                buf = join(buf, got, done[c - LAG])
            elif step > 0:
                buf = jnp.concatenate([buf, got], axis=0)
        starts = [(half * chunks + c) * blocks for half in (core, 1 - core)]
        columns_at = jnp.concatenate([s + jnp.arange(blocks, dtype=jnp.int32) for s in starts])
        upper, front, at = project(columns_at, order, (top, bottom, basis), buf, got, front, upper)
        done.append(at)
    return upper, front, scaled


def solution(mesh):
    placed = (P("row", "col"), P("row", "col"), P("row", None), P("row", None))
    return jax.shard_map(
        on_device,
        mesh=mesh,
        in_specs=placed,
        out_specs=(P(None, "col"), P("row", "col"), P("row", None)),
        check_vma=False,
    )
```

```python
import functools
import math

import jax
import jax.numpy as jnp
import numpy as np
from jax import lax
from jax.experimental import pallas as pl
from jax.experimental.pallas import tpu as pltpu
from jax.sharding import PartitionSpec as P

PB = 128
PANELS = 4
LEAD = PB * PANELS
HALF = LEAD // 2
BLOCK = 256
LAG = 2
VMEM_BYTES = 48 * 1024 * 1024
HIGHEST = lax.Precision.HIGHEST
F32 = jnp.float32
BF16 = jnp.bfloat16
SMEM = pltpu.SMEM
VMEM = pltpu.VMEM


def params():
    return pltpu.CompilerParams(vmem_limit_bytes=VMEM_BYTES)


def cost(flops):
    return pl.CostEstimate(flops=flops, bytes_accessed=1 << 20, transcendentals=0)


def mask_orders(count):
    others = [1 << b for b in range(1, count.bit_length() - 1)]
    half = len(others) // 2
    return ([1] + others, [1] + others[half:] + others[:half])


def swap(value, step, count):
    orders = mask_orders(count)
    pairs = [(d, d ^ orders[d & 1][step]) for d in range(count)]
    return lax.ppermute(value, "row", pairs)


def upper_side(step, count):
    orders = mask_orders(count)
    me = lax.axis_index("row")
    mask = jnp.where(me & 1 == 0, orders[0][step], orders[1][step])
    return ((me & mask) != 0).astype(jnp.int32)


def shard_table(count):
    orders = mask_orders(count)
    steps = len(orders[0])
    return np.array(
        [
            sum(((d & orders[d & 1][t]) != 0) << (steps - 1 - t) for t in range(steps))
            for d in range(count)
        ]
    )


def piece_order(count):
    orders = mask_orders(count)
    steps = len(orders[0])
    shard = shard_table(count)

    def pieces(device, done):
        if done == 0:
            return [device]
        mask = orders[device & 1][steps - done]
        return pieces(device, done - 1) + pieces(device ^ mask, done - 1)

    half = count // 2
    order = np.zeros((count, 2, half), np.int32)
    for d in range(count):
        for at, piece in enumerate(pieces(d, steps)):
            order[d, at // half, shard[piece] % half] = at % half
    return order


def in_vmem(count):
    return [pl.BlockSpec(memory_space=VMEM)] * count


def ordered(name, body, operands, outs, after=()):
    count = len(operands)

    def kernel(*refs):
        body(*refs[:count], *refs[count + len(after) :])

    results = pl.pallas_call(
        kernel,
        out_shape=tuple(outs),
        in_specs=in_vmem(count) + [pl.BlockSpec(memory_space=pl.ANY)] * len(after),
        out_specs=tuple(in_vmem(len(outs))),
        compiler_params=params(),
        name=name,
    )(*operands, *after)
    return results if len(outs) > 1 else results[0]


def add_body(a_ref, b_ref, out_ref):
    out_ref[...] = a_ref[...] + b_ref[...]


def split_add(step, count, keep, got, after):
    def body(keep_ref, got_ref, keep_out, send_out):
        half = keep_out.shape[1]
        side = upper_side(step, count)
        for which, out in ((side, keep_out), (1 - side, send_out)):
            part = pl.ds(pl.multiple_of(which * half, 128), half)
            out[...] = keep_ref[:, part] + got_ref[:, part]

    half = jax.ShapeDtypeStruct((keep.shape[0], keep.shape[1] // 2), F32)
    return ordered("split_add", body, [keep, got], [half, half], after)


def scatter_rest(keep, send, count, after):
    steps = count.bit_length() - 1
    for step in range(1, steps):
        got = swap(send, step, count)
        if step == steps - 1:
            return keep + got, keep
        keep, send = split_add(step + 1, count, keep, got, after if step == steps - 2 else ())


def total(value, count, first_after, last_after):
    side = upper_side(0, count)
    half = value.shape[0] // 2
    keep = lax.dynamic_slice_in_dim(value, side * half, half, 0)
    send = lax.dynamic_slice_in_dim(value, (1 - side) * half, half, 0)
    mine = keep + swap(send, 0, count)
    for step in range(1, count.bit_length() - 1):
        got = swap(mine, step, count)
        mine = ordered(
            "add_gram", add_body, [mine, got], [jax.ShapeDtypeStruct(mine.shape, F32)],
            first_after * (step == 1) + last_after * (step == count.bit_length() - 2),
        )
    return mine, swap(mine, 0, count)


def spread(value, count, after):
    stride = count
    while True:
        half = stride // 2
        got = lax.ppermute(value, "col", [(c, c + half) for c in range(0, count, stride)])
        if half == 1:
            return value, got
        value = relay(value, got, stride, after)
        stride = half


def relay(value, got, stride, after):
    def body(value_ref, got_ref, out_ref):
        here = lax.axis_index("col") % stride == stride // 2
        out_ref[...] = jnp.where(here, got_ref[...], value_ref[...])

    return ordered("relay", body, [value, got], [jax.ShapeDtypeStruct(value.shape, F32)], after)


def parts3(x):
    hi = x.astype(BF16)
    rest = x - hi.astype(F32)
    mid = rest.astype(BF16)
    return hi, mid, (rest - mid.astype(F32)).astype(BF16)


def parts2(x):
    hi = x.astype(BF16)
    return hi, (x - hi.astype(F32)).astype(BF16)


def place_rows(row_count, capacity, owner_ref, tally, child_count, write):
    for d in range(row_count):
        tally[d] = 0

    def body(i, carry):
        owner = owner_ref[i]
        rank = tally[owner]
        tally[owner] = rank + 1
        write(i, owner, rank)
        return carry

    lax.fori_loop(0, child_count, body, 0)


def pack_kernel(row_count, capacity, owner_ref, child_ref, out_ref, tally):
    out_ref[...] = jnp.zeros_like(out_ref)

    def write(i, owner, rank):
        out_ref[pl.ds(owner * capacity + rank, 1), :] = child_ref[pl.ds(i, 1), :]

    place_rows(row_count, capacity, owner_ref, tally, child_ref.shape[0], write)


def pack(child_rows, owner, row_count, capacity):
    return pl.pallas_call(
        functools.partial(pack_kernel, row_count, capacity),
        out_shape=jax.ShapeDtypeStruct((row_count * capacity, child_rows.shape[1]), F32),
        in_specs=[pl.BlockSpec(memory_space=SMEM)] + in_vmem(1),
        out_specs=in_vmem(1)[0],
        scratch_shapes=[pltpu.SMEM((row_count,), jnp.int32)],
        compiler_params=params(),
        name="pack_children",
    )(owner, child_rows)


def pack_lead_kernel(row_count, capacity, sentinel, owner_ref, offset_ref, even_ref, odd_ref, *refs):
    outs, (child_ref, rows_ref, tag_ref, tally) = refs[:row_count], refs[row_count:]
    child_ref[...] = jnp.where(lax.axis_index("col") % 2 == 0, even_ref[...], odd_ref[...])
    rows_ref[...] = jnp.zeros_like(rows_ref)
    tag_ref[...] = jnp.full(tag_ref.shape, sentinel, F32)
    me = lax.axis_index("row")

    def write(i, owner, rank):
        slot = (owner ^ me) * capacity + rank
        rows_ref[pl.ds(slot, 1), :] = child_ref[pl.ds(i, 1), :]
        tag_ref[pl.ds(slot, 1), :] = jnp.full((1, PB), offset_ref[i].astype(F32))

    place_rows(row_count, capacity, owner_ref, tally, child_ref.shape[0], write)
    for at, out in enumerate(outs):
        part = slice(at * capacity, (at + 1) * capacity)
        out[:, :LEAD] = rows_ref[part, :]
        out[:, LEAD:] = tag_ref[part, :]


def pack_lead(even, odd, owner, offset, row_count, capacity, sentinel):
    slots = row_count * capacity
    return pl.pallas_call(
        functools.partial(pack_lead_kernel, row_count, capacity, float(sentinel)),
        out_shape=(jax.ShapeDtypeStruct((capacity, LEAD + PB), F32),) * row_count,
        in_specs=[pl.BlockSpec(memory_space=SMEM)] * 2 + in_vmem(2),
        out_specs=tuple(in_vmem(row_count)),
        scratch_shapes=[
            pltpu.VMEM(even.shape, F32),
            pltpu.VMEM((slots, LEAD), F32),
            pltpu.VMEM((slots, PB), F32),
            pltpu.SMEM((row_count,), jnp.int32),
        ],
        compiler_params=params(),
        name="pack_lead",
    )(owner, offset, even, odd)


def triple(x, axis):
    hi, lo = parts2(x)
    return jnp.concatenate([hi, hi, lo] if axis == 1 else [hi, lo, hi], axis=axis)


def lead_kernel(row_count, *refs):
    front_refs, piece_refs = refs[:4], refs[4 : 4 + row_count]
    lead_ref, left_ref, place_ref, gram_ref = refs[4 + row_count :]
    even = lax.axis_index("col") % 2 == 0
    front = jnp.concatenate(
        [jnp.where(even, a[...], b[...]) for a, b in zip(front_refs[::2], front_refs[1::2])], axis=0
    )
    me = lax.axis_index("row")
    pieces = [ref[...] for ref in piece_refs]
    bit = 1
    while bit < row_count:
        swapped = [pieces[at ^ bit] for at in range(row_count)]
        pieces = [jnp.where((me & bit) != 0, b, a) for a, b in zip(pieces, swapped)]
        bit *= 2
    child = jnp.concatenate(pieces, axis=0)
    rows, slots = front.shape[0], child.shape[0]
    place = jnp.transpose(child[:, LEAD:])[0:1, :]
    at = lax.broadcasted_iota(jnp.int32, (rows, slots), 0).astype(F32)
    onehot = jnp.where(at == place, 1.0, 0.0).astype(BF16)
    spots = jnp.concatenate([onehot, onehot, onehot], axis=1)
    place_ref[...] = spots
    parts = jnp.concatenate(parts3(child[:, :LEAD])[::-1], axis=0)
    lead = front + jnp.dot(spots, parts, preferred_element_type=F32)
    lead_ref[...] = lead
    turned = jnp.transpose(lead)
    left_ref[...] = triple(turned, 1)
    gram_ref[:, :HALF] = dot_high(turned[:HALF], lead[:, :HALF], ((1,), (0,)))
    gram_ref[:, HALF:] = dot_high(turned[HALF:], lead, ((1,), (0,)))


def lead_setup(fronts, pieces, rows):
    slots = len(pieces) * pieces[0].shape[0]
    operands = list(fronts) + list(pieces)
    return pl.pallas_call(
        functools.partial(lead_kernel, len(pieces)),
        out_shape=(
            jax.ShapeDtypeStruct((rows, LEAD), F32),
            jax.ShapeDtypeStruct((LEAD, 3 * rows), BF16),
            jax.ShapeDtypeStruct((rows, 3 * slots), BF16),
            jax.ShapeDtypeStruct((HALF, LEAD + HALF), F32),
        ),
        in_specs=in_vmem(len(operands)),
        out_specs=tuple(in_vmem(4)),
        compiler_params=params(),
        name="lead_setup",
    )(*operands)


def product_kernel(blocks, chunks, base_ref, left_ref, place_ref, front_ref, child_ref, *rest):
    del base_ref
    outs, whole_ref = rest[-1 - chunks : -1], rest[-1]
    parts = jnp.concatenate(parts3(child_ref[...])[::-1], axis=0)
    whole = front_ref[...] + jnp.dot(place_ref[...], parts, preferred_element_type=F32)
    whole_ref[...] = whole
    result = jnp.dot(left_ref[...], triple(whole, 0), preferred_element_type=F32)
    for at, out in enumerate(outs):

        @pl.when(pl.program_id(0) // blocks == at)
        def _():
            out[...] = result


def product(half, left, place, front, child, whole, chunks):
    rows, columns = front.shape
    slots = child.shape[0]
    steps = columns // 2 // BLOCK
    blocks = steps // chunks
    in_specs = [
        pl.BlockSpec(left.shape, lambda i, h: (0, 0)),
        pl.BlockSpec(place.shape, lambda i, h: (0, 0)),
        pl.BlockSpec((rows, BLOCK), lambda i, h: (0, h[0] * steps + i)),
        pl.BlockSpec((slots, BLOCK), lambda i, h: (0, h[0] * steps + i)),
    ]
    operands = [half[None], left, place, front, child]
    aliases = {}
    if whole is not None:
        in_specs.append(pl.BlockSpec(memory_space=pl.ANY))
        operands.append(whole)
        aliases = {5: chunks}

    def out_block(at):
        return lambda i, h: (0, jnp.clip(i - at * blocks, 0, blocks - 1))

    return pl.pallas_call(
        functools.partial(product_kernel, blocks, chunks),
        grid_spec=pltpu.PrefetchScalarGridSpec(
            num_scalar_prefetch=1,
            grid=(steps,),
            in_specs=in_specs,
            out_specs=tuple(pl.BlockSpec((LEAD, BLOCK), out_block(at)) for at in range(chunks))
            + (pl.BlockSpec((rows, BLOCK), lambda i, h: (0, h[0] * steps + i)),),
        ),
        out_shape=(jax.ShapeDtypeStruct((LEAD, columns // 2 // chunks), F32),) * chunks
        + (jax.ShapeDtypeStruct((rows, columns), F32),),
        input_output_aliases=aliases,
        compiler_params=params(),
        name="lead_product",
    )(*operands)


def join(a, b, after):
    def body(a_ref, b_ref, out_ref):
        half = a_ref.shape[0]
        out_ref[:half, :] = a_ref[...]
        out_ref[half:, :] = b_ref[...]

    shape = jax.ShapeDtypeStruct((2 * a.shape[0], a.shape[1]), F32)
    return ordered("join_pieces", body, [a, b], [shape], after)


def dot_high(a, b, dims):
    return lax.dot_general(a, b, (dims, ((), ())), precision=HIGHEST, preferred_element_type=F32)


def spread_lane(tile, at):
    return jnp.broadcast_to(tile[:, at : at + 1], tile.shape)


def invert_factor(block):
    lane = lax.broadcasted_iota(jnp.int32, (8, PB), 1)
    sub = lax.broadcasted_iota(jnp.int32, (8, PB), 0)
    count = PB // 8
    tiles = [block[8 * t : 8 * t + 8, :] for t in range(count)]
    for b in range(count):
        first = 8 * b
        rows = tiles[b]
        cols = [spread_lane(rows, first + c) for c in range(8)]
        heads, inverses = {}, []
        for c in range(8):
            inverse = 1.0 / cols[c][c : c + 1, :]
            inverses.append(inverse)
            factor = jnp.where(sub > c, cols[c] * inverse, 0.0)
            here = lane == first + c
            source = jnp.where(here[0:1, :], 1.0, rows[c : c + 1, :])
            rows = jnp.where(here & (sub > c), 0.0, rows) - factor * source
            for d in range(c + 1, 8):
                heads[c, d] = cols[d][c : c + 1, :]
                cols[d] = cols[d] - factor * heads[c, d]
        tiles[b] = rows
        inside = (lane >= first) & (lane < first + 8)
        past = inside & (lane - first >= sub)
        used = jnp.where(past, jnp.where(lane - first == sub, 1.0, 0.0), rows)
        for t in range(b + 1, count):
            tile = tiles[t]
            factors = []
            for c in range(8):
                factor = spread_lane(tile, first + c)
                for d in range(c):
                    factor = factor - factors[d] * heads[d, c]
                factors.append(factor * inverses[c])
            tile = jnp.where(inside, 0.0, tile)
            for c in range(8):
                tile = tile - factors[c] * used[c : c + 1, :]
            tiles[t] = tile
    done = []
    for t in range(count):
        diagonal = lane == sub + 8 * t
        pivot = jnp.sum(jnp.where(diagonal, tiles[t], 0.0), axis=1, keepdims=True)
        scale = lax.rsqrt(pivot)
        scale = scale * (1.5 - 0.5 * pivot * scale * scale)
        unit = jnp.where(diagonal, 1.0, jnp.where(lane < sub + 8 * t, tiles[t], 0.0))
        done.append(unit * scale)
    return jnp.concatenate(done, axis=0)


def eliminate_kernel(k, *refs):
    in_ref, out_ref = refs[0], refs[-1]
    lo, hi = k * PB, (k + 1) * PB
    if k == 0:
        mine, got = refs[0][...], refs[1][...]
        low = lax.axis_index("row") % 2 == 0
        packed = jnp.concatenate([jnp.where(low, mine, got), jnp.where(low, got, mine)], axis=0)
        cross = packed[:, HALF:LEAD]
        out_ref[:HALF, :HALF] = packed[:, :HALF]
        out_ref[HALF:, :HALF] = cross
        out_ref[:HALF, HALF:] = jnp.transpose(cross)
        out_ref[HALF:, HALF:] = packed[:, LEAD:]
        in_ref = out_ref
    else:
        out_ref[:lo, :] = in_ref[:lo, :]
    inverse = invert_factor(in_ref[lo:hi, lo:hi])
    pieces = []
    for j in range(PANELS):
        if j == k:
            pieces.append(inverse)
        else:
            pieces.append(dot_high(inverse, in_ref[lo:hi, j * PB : (j + 1) * PB], ((1,), (0,))))
    row = jnp.concatenate(pieces, axis=1)
    out_ref[lo:hi, :] = row
    if k < PANELS - 1:
        column = dot_high(in_ref[hi:, lo:hi], inverse, ((1,), (1,)))
        change = dot_high(column, row, ((1,), (0,)))
        later = in_ref[hi:, :]
        out_ref[hi:, :] = later - change
        out_ref[hi:, lo:hi] = -change[:, lo:hi]


def eliminate(operands, k):
    return pl.pallas_call(
        functools.partial(eliminate_kernel, k),
        out_shape=jax.ShapeDtypeStruct((LEAD, LEAD), F32),
        in_specs=in_vmem(len(operands)),
        out_specs=in_vmem(1)[0],
        compiler_params=params(),
        cost_estimate=cost(6 * 10**9),
        name="eliminate_panel",
    )(*operands)


def finish_kernel(scale, matrix_ref, lead_ref, top_ref, bottom_ref, basis3_ref, basis_ref):
    own = lax.broadcasted_iota(jnp.int32, (LEAD, LEAD), 0) // PB
    other = lax.broadcasted_iota(jnp.int32, (LEAD, LEAD), 1) // PB
    inverse = jnp.where(own >= other, matrix_ref[...], 0.0)
    top_ref[...] = triple(inverse[:HALF, :HALF], 1)
    bottom_ref[...] = triple(inverse[HALF:], 1)
    basis = dot_high(lead_ref[...], inverse, ((1,), (1,)))
    basis3_ref[...] = triple(basis, 1)
    basis_ref[...] = basis * scale


def finish(matrix, lead, scale):
    rows = lead.shape[0]
    return pl.pallas_call(
        functools.partial(finish_kernel, scale),
        out_shape=(
            jax.ShapeDtypeStruct((HALF, 3 * HALF), BF16),
            jax.ShapeDtypeStruct((HALF, 3 * LEAD), BF16),
            jax.ShapeDtypeStruct((rows, 3 * LEAD), BF16),
            jax.ShapeDtypeStruct((rows, LEAD), F32),
        ),
        in_specs=[pl.BlockSpec(memory_space=VMEM)] * 2,
        out_specs=(pl.BlockSpec(memory_space=VMEM),) * 4,
        compiler_params=params(),
        cost_estimate=cost(2 * 10**9),
        name="finish_factor",
    )(matrix, lead)


def project_kernel(blocks, places_ref, top_ref, bottom_ref, basis_ref, *rest):
    del places_ref
    near_even, near_odd, far_even, far_odd, front_ref = rest[:5]
    upper_ref, out_ref, done_ref = rest[-3:]
    done_ref[...] = jnp.zeros_like(done_ref)
    near = pl.program_id(0) < blocks
    sums = jnp.concatenate(
        [
            jnp.where(near, near_even[...], far_even[...]),
            jnp.where(near, near_odd[...], far_odd[...]),
        ],
        axis=1,
    )
    hi, lo = parts2(sums)
    upper_ref[:HALF, :] = jnp.dot(
        top_ref[...],
        jnp.concatenate([hi[:HALF], lo[:HALF], hi[:HALF]], axis=0),
        preferred_element_type=F32,
    )
    upper_ref[HALF:, :] = jnp.dot(
        bottom_ref[...], jnp.concatenate([hi, lo, hi], axis=0), preferred_element_type=F32
    )
    out_ref[...] = front_ref[...] - jnp.dot(
        basis_ref[...], triple(upper_ref[...], 0), preferred_element_type=F32
    )


def project(places, c, chunks, factor, near, far, front, upper):
    top, bottom, basis = factor
    rows, columns = front.shape
    blocks = near.shape[0] // LEAD // 2
    begin = c * 2 * blocks
    near_at = chunks * 2 * blocks
    far_at = near_at + 2 * blocks

    def near_piece(odd):
        return lambda i, p: (p[near_at + 2 * jnp.minimum(i, blocks - 1) + odd], 0)

    def far_piece(odd):
        return lambda i, p: (p[far_at + 2 * jnp.maximum(i - blocks, 0) + odd], 0)

    in_specs = [
        pl.BlockSpec(top.shape, lambda i, p: (0, 0)),
        pl.BlockSpec(bottom.shape, lambda i, p: (0, 0)),
        pl.BlockSpec(basis.shape, lambda i, p: (0, 0)),
        pl.BlockSpec((LEAD, PB), near_piece(0)),
        pl.BlockSpec((LEAD, PB), near_piece(1)),
        pl.BlockSpec((LEAD, PB), far_piece(0)),
        pl.BlockSpec((LEAD, PB), far_piece(1)),
        pl.BlockSpec((rows, BLOCK), lambda i, p: (0, p[begin + i])),
    ]
    operands = [places, top, bottom, basis, near, near, far, far, front]
    aliases = {8: 1}
    if upper is not None:
        in_specs.append(pl.BlockSpec(memory_space=pl.ANY))
        operands.append(upper)
        aliases[9] = 0
    return pl.pallas_call(
        functools.partial(project_kernel, blocks),
        grid_spec=pltpu.PrefetchScalarGridSpec(
            num_scalar_prefetch=1,
            grid=(2 * blocks,),
            in_specs=in_specs,
            out_specs=(
                pl.BlockSpec((LEAD, BLOCK), lambda i, p: (0, p[begin + i])),
                pl.BlockSpec((rows, BLOCK), lambda i, p: (0, p[begin + i])),
                pl.BlockSpec((8, PB), lambda i, p: (0, 0)),
            ),
        ),
        out_shape=(
            jax.ShapeDtypeStruct((LEAD, columns), F32),
            jax.ShapeDtypeStruct((rows, columns), F32),
            jax.ShapeDtypeStruct((8, PB), F32),
        ),
        input_output_aliases=aliases,
        compiler_params=params(),
        cost_estimate=cost(3 * 10**9),
        name="project_columns",
    )(*operands)


def exchange(value, row_count):
    slots, width = value.shape
    shaped = value.reshape(row_count, slots // row_count, width)
    return lax.all_to_all(shaped, "row", split_axis=0, concat_axis=0, tiled=True).reshape(
        slots, width
    )


def on_device(front_matrix, child_rows, child_owner, child_offset):
    row_count = lax.axis_size("row")
    col_count = lax.axis_size("col")
    local_rows, local_cols = front_matrix.shape
    child_count = child_rows.shape[0]
    capacity = 2 * child_count // row_count
    me = lax.axis_index("row")

    owner, offset = child_owner[:, 0], child_offset[:, 0]
    packed = pack(child_rows, owner, row_count, capacity)
    child = exchange(packed, row_count)
    lead_rows = child_rows[:, :LEAD]
    first = lax.ppermute(lead_rows, "col", [(0, col_count // 2)])
    cut = local_rows // 2

    def cut_body(front_ref, low_ref, high_ref):
        low_ref[...] = front_ref[:cut, :]
        high_ref[...] = front_ref[cut:, :]

    low, high = ordered(
        "cut_lead", cut_body, [front_matrix[:, :LEAD]],
        [jax.ShapeDtypeStruct((cut, LEAD), F32)] * 2, (first,),
    )
    passed = relay(lead_rows, first, col_count, ())
    stride = col_count // 2
    pairs = [(c, c + stride // 2) for c in range(0, col_count, stride)]
    pieces = list(
        pack_lead(passed, lax.ppermute(passed, "col", pairs), owner, offset, row_count, capacity, local_rows)
    )
    for mask in range(1, row_count):
        pairs = [(d, d ^ mask) for d in range(row_count)]
        pieces[mask] = lax.ppermute(pieces[mask], "row", pairs)
    fronts = spread(low, col_count, (passed,)) + spread(high, col_count, (child, pieces[0]))
    lead, left, place, gram = lead_setup(fronts, pieces, local_rows)

    chunks = max(1, min(4, local_cols // (PB * row_count)))
    width = local_cols // 2 // chunks
    blocks = width // BLOCK
    core = upper_side(0, row_count)
    *send, front = product(1 - core, left, place, front_matrix, child, None, chunks)
    *keep, front = product(core, left, place, front_matrix, child, front, chunks)

    halves = [split_add(1, row_count, keep[c], swap(send[c], 0, row_count), ()) for c in range(chunks)]

    matrix = total(gram, row_count, (keep[0],), tuple(h[0] for h in halves))
    made = []
    for k in range(PANELS):
        matrix = [eliminate(matrix, k)]
        made.append(matrix[0])
    matrix = matrix[0]
    scale = math.sqrt(local_rows * row_count)
    top, bottom, basis, scaled = finish(matrix, lead, scale)

    shards = [
        scatter_rest(*halves[c], row_count, (made[min(c, PANELS - 1)],))
        for c in range(chunks)
    ]
    steps = row_count.bit_length() - 1
    columns_at = [
        [
            ((d & 1) ^ side) * chunks * blocks + c * blocks + b
            for c in range(chunks)
            for side in range(2)
            for b in range(blocks)
        ]
        for d in range(row_count)
    ]
    order = piece_order(row_count).reshape(row_count, -1)
    table = np.concatenate([np.array(columns_at, np.int32), order], axis=1)
    places = lax.dynamic_index_in_dim(jnp.asarray(table), me, 0, keepdims=False)
    upper = None
    done = []
    for c in range(chunks):
        buf = shards[c][0]
        for step in reversed(range(steps)):
            got = swap(buf, step, row_count)
            if step == steps - 1 and step > 1:
                buf = join(buf, got, tuple(keep for _, keep in shards))
            elif step == 1 and c >= LAG:
                buf = join(buf, got, (done[c - LAG],))
            elif step > 0:
                buf = jnp.concatenate([buf, got], axis=0)
        upper, front, at = project(places, c, chunks, (top, bottom, basis), buf, got, front, upper)
        done.append(at)
    return upper, front, scaled


def solution(mesh):
    placed = (P("row", "col"), P("row", "col"), P("row", None), P("row", None))
    return jax.shard_map(
        on_device,
        mesh=mesh,
        in_specs=placed,
        out_specs=(P(None, "col"), P("row", "col"), P("row", None)),
        check_vma=False,
    )
```

```python
import functools
import math

import jax
import jax.numpy as jnp
import numpy as np
from jax import lax
from jax.experimental import pallas as pl
from jax.experimental.pallas import tpu as pltpu
from jax.sharding import PartitionSpec as P

PB = 128
PANELS = 4
LEAD = PB * PANELS
HALF = LEAD // 2
BLOCK = 256
LAG = 2
WIDE = 512
VMEM_BYTES = 48 * 1024 * 1024
HIGHEST = lax.Precision.HIGHEST
F32 = jnp.float32
BF16 = jnp.bfloat16
SMEM = pltpu.SMEM
VMEM = pltpu.VMEM


def params():
    return pltpu.CompilerParams(vmem_limit_bytes=VMEM_BYTES)


def cost(flops):
    return pl.CostEstimate(flops=flops, bytes_accessed=1 << 20, transcendentals=0)


def mask_orders(count):
    others = [1 << b for b in range(1, count.bit_length() - 1)]
    half = len(others) // 2
    return ([1] + others, [1] + others[half:] + others[:half])


def swap(value, step, count):
    orders = mask_orders(count)
    pairs = [(d, d ^ orders[d & 1][step]) for d in range(count)]
    return lax.ppermute(value, "row", pairs)


def upper_side(step, count):
    orders = mask_orders(count)
    me = lax.axis_index("row")
    mask = jnp.where(me & 1 == 0, orders[0][step], orders[1][step])
    return ((me & mask) != 0).astype(jnp.int32)


def shard_table(count):
    orders = mask_orders(count)
    steps = len(orders[0])
    return np.array(
        [
            sum(((d & orders[d & 1][t]) != 0) << (steps - 1 - t) for t in range(steps))
            for d in range(count)
        ]
    )


def piece_order(count):
    orders = mask_orders(count)
    steps = len(orders[0])
    shard = shard_table(count)

    def pieces(device, done):
        if done == 0:
            return [device]
        mask = orders[device & 1][steps - done]
        return pieces(device, done - 1) + pieces(device ^ mask, done - 1)

    half = count // 2
    order = np.zeros((count, 2, half), np.int32)
    for d in range(count):
        for at, piece in enumerate(pieces(d, steps)):
            order[d, at // half, shard[piece] % half] = at % half
    return order


def in_vmem(count):
    return [pl.BlockSpec(memory_space=VMEM)] * count


def ordered(name, body, operands, outs, after=()):
    count = len(operands)

    def kernel(*refs):
        body(*refs[:count], *refs[count + len(after) :])

    results = pl.pallas_call(
        kernel,
        out_shape=tuple(outs),
        in_specs=in_vmem(count) + [pl.BlockSpec(memory_space=pl.ANY)] * len(after),
        out_specs=tuple(in_vmem(len(outs))),
        compiler_params=params(),
        name=name,
    )(*operands, *after)
    return results if len(outs) > 1 else results[0]


def add_body(a_ref, b_ref, out_ref):
    out_ref[...] = a_ref[...] + b_ref[...]


def split_add(step, count, keep, got, after):
    def body(keep_ref, got_ref, keep_out, send_out):
        half = keep_out.shape[1]
        side = upper_side(step, count)
        for which, out in ((side, keep_out), (1 - side, send_out)):
            part = pl.ds(pl.multiple_of(which * half, 128), half)
            out[...] = keep_ref[:, part] + got_ref[:, part]

    half = jax.ShapeDtypeStruct((keep.shape[0], keep.shape[1] // 2), F32)
    return ordered("split_add", body, [keep, got], [half, half], after)


def scatter_rest(keep, send, count, after):
    steps = count.bit_length() - 1
    for step in range(1, steps):
        got = swap(send, step, count)
        if step == steps - 1:
            return keep + got, keep
        keep, send = split_add(step + 1, count, keep, got, after if step == steps - 2 else ())


def total(value, count, first_after, last_after):
    side = upper_side(0, count)
    half = value.shape[0] // 2
    keep = lax.dynamic_slice_in_dim(value, side * half, half, 0)
    send = lax.dynamic_slice_in_dim(value, (1 - side) * half, half, 0)
    mine = keep + swap(send, 0, count)
    for step in range(1, count.bit_length() - 1):
        got = swap(mine, step, count)
        mine = ordered(
            "add_gram", add_body, [mine, got], [jax.ShapeDtypeStruct(mine.shape, F32)],
            first_after * (step == 1) + last_after * (step == count.bit_length() - 2),
        )
    return mine, swap(mine, 0, count)


def spread(value, got, count, after, paired):
    middle = count // 2

    def body(value_ref, got_ref, out_ref):
        here = lax.axis_index("col") == middle
        out_ref[...] = jnp.where(here, got_ref[...], value_ref[...])

    passed = ordered("relay", body, [value, got], [jax.ShapeDtypeStruct(value.shape, F32)], after)
    others = [c for c in range(count - 1, 0, -1) if c != middle]
    if paired and count == 4:
        return [passed, lax.ppermute(passed, "col", [(0, 1), (2, 3)])]
    return [passed] + [lax.ppermute(passed, "col", [(middle, c)]) for c in others]


def pick(refs, count):
    me = lax.axis_index("col")
    held = (me == 0) | (me == count // 2)
    arrived = refs[1][...]
    for ref in refs[2:]:
        arrived = arrived + ref[...]
    return jnp.where(held, refs[0][...], arrived)


def first_hop(value, count):
    return lax.ppermute(value, "col", [(0, count // 2)])


def parts3(x):
    hi = x.astype(BF16)
    rest = x - hi.astype(F32)
    mid = rest.astype(BF16)
    return hi, mid, (rest - mid.astype(F32)).astype(BF16)


def parts2(x):
    hi = x.astype(BF16)
    return hi, (x - hi.astype(F32)).astype(BF16)


def place_rows(row_count, capacity, owner_ref, tally, child_count, write):
    for d in range(row_count):
        tally[d] = 0

    def body(i, carry):
        owner = owner_ref[i]
        rank = tally[owner]
        tally[owner] = rank + 1
        write(i, owner, rank)
        return carry

    lax.fori_loop(0, child_count, body, 0)


def pack_kernel(row_count, capacity, owner_ref, child_ref, out_ref, tally):
    out_ref[...] = jnp.zeros_like(out_ref)

    def write(i, owner, rank):
        out_ref[pl.ds(owner * capacity + rank, 1), :] = child_ref[pl.ds(i, 1), :]

    place_rows(row_count, capacity, owner_ref, tally, child_ref.shape[0], write)


def pack(child_rows, owner, row_count, capacity):
    return pl.pallas_call(
        functools.partial(pack_kernel, row_count, capacity),
        out_shape=jax.ShapeDtypeStruct((row_count * capacity, child_rows.shape[1]), F32),
        in_specs=[pl.BlockSpec(memory_space=SMEM)] + in_vmem(1),
        out_specs=in_vmem(1)[0],
        scratch_shapes=[pltpu.SMEM((row_count,), jnp.int32)],
        compiler_params=params(),
        name="pack_children",
    )(owner, child_rows)


def pack_lead_kernel(row_count, capacity, sentinel, col_count, given_count, owner_ref, offset_ref, *refs):
    given, refs = refs[:given_count], refs[given_count:]
    outs, (child_ref, rows_ref, tag_ref, tally) = refs[:row_count], refs[row_count:]
    child_ref[...] = pick(given, col_count)
    rows_ref[...] = jnp.zeros_like(rows_ref)
    tag_ref[...] = jnp.full(tag_ref.shape, sentinel, F32)
    me = lax.axis_index("row")

    def write(i, owner, rank):
        slot = (owner ^ me) * capacity + rank
        rows_ref[pl.ds(slot, 1), :] = child_ref[pl.ds(i, 1), :]
        tag_ref[pl.ds(slot, 1), :] = jnp.full((1, PB), offset_ref[i].astype(F32))

    place_rows(row_count, capacity, owner_ref, tally, child_ref.shape[0], write)
    for at, out in enumerate(outs):
        part = slice(at * capacity, (at + 1) * capacity)
        out[:, :LEAD] = rows_ref[part, :]
        out[:, LEAD:] = tag_ref[part, :]


def pack_lead(given, owner, offset, row_count, capacity, sentinel, col_count):
    slots = row_count * capacity
    return pl.pallas_call(
        functools.partial(pack_lead_kernel, row_count, capacity, float(sentinel), col_count, len(given)),
        out_shape=(jax.ShapeDtypeStruct((capacity, LEAD + PB), F32),) * row_count,
        in_specs=[pl.BlockSpec(memory_space=SMEM)] * 2 + in_vmem(len(given)),
        out_specs=tuple(in_vmem(row_count)),
        scratch_shapes=[
            pltpu.VMEM(given[0].shape, F32),
            pltpu.VMEM((slots, LEAD), F32),
            pltpu.VMEM((slots, PB), F32),
            pltpu.SMEM((row_count,), jnp.int32),
        ],
        compiler_params=params(),
        name="pack_lead",
    )(owner, offset, *given)


def triple(x, axis):
    hi, lo = parts2(x)
    return jnp.concatenate([hi, hi, lo] if axis == 1 else [hi, lo, hi], axis=axis)


def lead_kernel(row_count, col_count, each, *refs):
    front_refs, piece_refs = refs[: 2 * each], refs[2 * each : 2 * each + row_count]
    lead_ref, left_ref, place_ref, gram_ref = refs[2 * each + row_count :]
    front = jnp.concatenate(
        [pick(front_refs[:each], col_count), pick(front_refs[each:], col_count)], axis=0
    )
    me = lax.axis_index("row")
    pieces = [ref[...] for ref in piece_refs]
    bit = 1
    while bit < row_count:
        swapped = [pieces[at ^ bit] for at in range(row_count)]
        pieces = [jnp.where((me & bit) != 0, b, a) for a, b in zip(pieces, swapped)]
        bit *= 2
    child = jnp.concatenate(pieces, axis=0)
    rows, slots = front.shape[0], child.shape[0]
    place = jnp.transpose(child[:, LEAD:])[0:1, :]
    at = lax.broadcasted_iota(jnp.int32, (rows, slots), 0).astype(F32)
    onehot = jnp.where(at == place, 1.0, 0.0).astype(BF16)
    spots = jnp.concatenate([onehot, onehot, onehot], axis=1)
    place_ref[...] = spots
    parts = jnp.concatenate(parts3(child[:, :LEAD])[::-1], axis=0)
    lead = front + jnp.dot(spots, parts, preferred_element_type=F32)
    lead_ref[...] = lead
    turned = jnp.transpose(lead)
    left_ref[...] = triple(turned, 1)
    gram_ref[:, :HALF] = dot_high(turned[:HALF], lead[:, :HALF], ((1,), (0,)))
    gram_ref[:, HALF:] = dot_high(turned[HALF:], lead, ((1,), (0,)))


def lead_setup(fronts, pieces, rows, col_count):
    slots = len(pieces) * pieces[0].shape[0]
    operands = list(fronts) + list(pieces)
    return pl.pallas_call(
        functools.partial(lead_kernel, len(pieces), col_count, len(fronts) // 2),
        out_shape=(
            jax.ShapeDtypeStruct((rows, LEAD), F32),
            jax.ShapeDtypeStruct((LEAD, 3 * rows), BF16),
            jax.ShapeDtypeStruct((rows, 3 * slots), BF16),
            jax.ShapeDtypeStruct((HALF, LEAD + HALF), F32),
        ),
        in_specs=in_vmem(len(operands)),
        out_specs=tuple(in_vmem(4)),
        compiler_params=params(),
        name="lead_setup",
    )(*operands)


def product_kernel(blocks, chunks, base_ref, left_ref, place_ref, front_ref, child_ref, *rest):
    del base_ref
    outs, whole_ref = rest[-1 - chunks : -1], rest[-1]
    parts = jnp.concatenate(parts3(child_ref[...])[::-1], axis=0)
    whole = front_ref[...] + jnp.dot(place_ref[...], parts, preferred_element_type=F32)
    whole_ref[...] = whole
    result = jnp.dot(left_ref[...], triple(whole, 0), preferred_element_type=F32)
    for at, out in enumerate(outs):

        @pl.when(pl.program_id(0) // blocks == at)
        def _():
            out[...] = result


def product(half, left, place, front, child, whole, chunks):
    rows, columns = front.shape
    slots = child.shape[0]
    steps = columns // 2 // WIDE
    blocks = steps // chunks
    in_specs = [
        pl.BlockSpec(left.shape, lambda i, h: (0, 0)),
        pl.BlockSpec(place.shape, lambda i, h: (0, 0)),
        pl.BlockSpec((rows, WIDE), lambda i, h: (0, h[0] * steps + i)),
        pl.BlockSpec((slots, WIDE), lambda i, h: (0, h[0] * steps + i)),
    ]
    operands = [half[None], left, place, front, child]
    aliases = {}
    if whole is not None:
        in_specs.append(pl.BlockSpec(memory_space=pl.ANY))
        operands.append(whole)
        aliases = {5: chunks}

    def out_block(at):
        return lambda i, h: (0, jnp.clip(i - at * blocks, 0, blocks - 1))

    return pl.pallas_call(
        functools.partial(product_kernel, blocks, chunks),
        grid_spec=pltpu.PrefetchScalarGridSpec(
            num_scalar_prefetch=1,
            grid=(steps,),
            in_specs=in_specs,
            out_specs=tuple(pl.BlockSpec((LEAD, WIDE), out_block(at)) for at in range(chunks))
            + (pl.BlockSpec((rows, WIDE), lambda i, h: (0, h[0] * steps + i)),),
        ),
        out_shape=(jax.ShapeDtypeStruct((LEAD, columns // 2 // chunks), F32),) * chunks
        + (jax.ShapeDtypeStruct((rows, columns), F32),),
        input_output_aliases=aliases,
        compiler_params=params(),
        name="lead_product",
    )(*operands)


def join(a, b, after):
    def body(a_ref, b_ref, out_ref):
        half = a_ref.shape[0]
        out_ref[:half, :] = a_ref[...]
        out_ref[half:, :] = b_ref[...]

    shape = jax.ShapeDtypeStruct((2 * a.shape[0], a.shape[1]), F32)
    return ordered("join_pieces", body, [a, b], [shape], after)


def dot_high(a, b, dims):
    return lax.dot_general(a, b, (dims, ((), ())), precision=HIGHEST, preferred_element_type=F32)


def spread_lane(tile, at):
    return jnp.broadcast_to(tile[:, at : at + 1], tile.shape)


def invert_factor(block):
    lane = lax.broadcasted_iota(jnp.int32, (8, PB), 1)
    sub = lax.broadcasted_iota(jnp.int32, (8, PB), 0)
    count = PB // 8
    tiles = [block[8 * t : 8 * t + 8, :] for t in range(count)]
    for b in range(count):
        first = 8 * b
        rows = tiles[b]
        cols = [spread_lane(rows, first + c) for c in range(8)]
        heads, inverses = {}, []
        for c in range(8):
            inverse = 1.0 / cols[c][c : c + 1, :]
            inverses.append(inverse)
            factor = jnp.where(sub > c, cols[c] * inverse, 0.0)
            here = lane == first + c
            source = jnp.where(here[0:1, :], 1.0, rows[c : c + 1, :])
            rows = jnp.where(here & (sub > c), 0.0, rows) - factor * source
            for d in range(c + 1, 8):
                heads[c, d] = cols[d][c : c + 1, :]
                cols[d] = cols[d] - factor * heads[c, d]
        tiles[b] = rows
        inside = (lane >= first) & (lane < first + 8)
        past = inside & (lane - first >= sub)
        used = jnp.where(past, jnp.where(lane - first == sub, 1.0, 0.0), rows)
        for t in range(b + 1, count):
            tile = tiles[t]
            factors = []
            for c in range(8):
                factor = spread_lane(tile, first + c)
                for d in range(c):
                    factor = factor - factors[d] * heads[d, c]
                factors.append(factor * inverses[c])
            tile = jnp.where(inside, 0.0, tile)
            for c in range(8):
                tile = tile - factors[c] * used[c : c + 1, :]
            tiles[t] = tile
    done = []
    for t in range(count):
        diagonal = lane == sub + 8 * t
        pivot = jnp.sum(jnp.where(diagonal, tiles[t], 0.0), axis=1, keepdims=True)
        scale = lax.rsqrt(pivot)
        scale = scale * (1.5 - 0.5 * pivot * scale * scale)
        unit = jnp.where(diagonal, 1.0, jnp.where(lane < sub + 8 * t, tiles[t], 0.0))
        done.append(unit * scale)
    return jnp.concatenate(done, axis=0)


def eliminate_kernel(k, *refs):
    in_ref, out_ref = refs[0], refs[-1]
    lo, hi = k * PB, (k + 1) * PB
    if k == 0:
        mine, got = refs[0][...], refs[1][...]
        low = lax.axis_index("row") % 2 == 0
        packed = jnp.concatenate([jnp.where(low, mine, got), jnp.where(low, got, mine)], axis=0)
        cross = packed[:, HALF:LEAD]
        out_ref[:HALF, :HALF] = packed[:, :HALF]
        out_ref[HALF:, :HALF] = cross
        out_ref[:HALF, HALF:] = jnp.transpose(cross)
        out_ref[HALF:, HALF:] = packed[:, LEAD:]
        in_ref = out_ref
    else:
        out_ref[:lo, :] = in_ref[:lo, :]
    inverse = invert_factor(in_ref[lo:hi, lo:hi])
    pieces = []
    for j in range(PANELS):
        if j == k:
            pieces.append(inverse)
        else:
            pieces.append(dot_high(inverse, in_ref[lo:hi, j * PB : (j + 1) * PB], ((1,), (0,))))
    row = jnp.concatenate(pieces, axis=1)
    out_ref[lo:hi, :] = row
    if k < PANELS - 1:
        column = dot_high(in_ref[hi:, lo:hi], inverse, ((1,), (1,)))
        change = dot_high(column, row, ((1,), (0,)))
        later = in_ref[hi:, :]
        out_ref[hi:, :] = later - change
        out_ref[hi:, lo:hi] = -change[:, lo:hi]


def eliminate(operands, k):
    return pl.pallas_call(
        functools.partial(eliminate_kernel, k),
        out_shape=jax.ShapeDtypeStruct((LEAD, LEAD), F32),
        in_specs=in_vmem(len(operands)),
        out_specs=in_vmem(1)[0],
        compiler_params=params(),
        cost_estimate=cost(6 * 10**9),
        name="eliminate_panel",
    )(*operands)


def finish_kernel(scale, matrix_ref, lead_ref, top_ref, bottom_ref, basis3_ref, basis_ref):
    own = lax.broadcasted_iota(jnp.int32, (LEAD, LEAD), 0) // PB
    other = lax.broadcasted_iota(jnp.int32, (LEAD, LEAD), 1) // PB
    inverse = jnp.where(own >= other, matrix_ref[...], 0.0)
    top_ref[...] = triple(inverse[:HALF, :HALF], 1)
    bottom_ref[...] = triple(inverse[HALF:], 1)
    basis = dot_high(lead_ref[...], inverse, ((1,), (1,)))
    basis3_ref[...] = triple(basis, 1)
    basis_ref[...] = basis * scale


def finish(matrix, lead, scale):
    rows = lead.shape[0]
    return pl.pallas_call(
        functools.partial(finish_kernel, scale),
        out_shape=(
            jax.ShapeDtypeStruct((HALF, 3 * HALF), BF16),
            jax.ShapeDtypeStruct((HALF, 3 * LEAD), BF16),
            jax.ShapeDtypeStruct((rows, 3 * LEAD), BF16),
            jax.ShapeDtypeStruct((rows, LEAD), F32),
        ),
        in_specs=[pl.BlockSpec(memory_space=VMEM)] * 2,
        out_specs=(pl.BlockSpec(memory_space=VMEM),) * 4,
        compiler_params=params(),
        cost_estimate=cost(2 * 10**9),
        name="finish_factor",
    )(matrix, lead)


def project_kernel(blocks, places_ref, top_ref, bottom_ref, basis_ref, *rest):
    del places_ref
    near_even, near_odd, far_even, far_odd, front_ref = rest[:5]
    upper_ref, out_ref, done_ref = rest[-3:]
    done_ref[...] = jnp.zeros_like(done_ref)
    near = pl.program_id(0) < blocks
    sums = jnp.concatenate(
        [
            jnp.where(near, near_even[...], far_even[...]),
            jnp.where(near, near_odd[...], far_odd[...]),
        ],
        axis=1,
    )
    hi, lo = parts2(sums)
    upper_ref[:HALF, :] = jnp.dot(
        top_ref[...],
        jnp.concatenate([hi[:HALF], lo[:HALF], hi[:HALF]], axis=0),
        preferred_element_type=F32,
    )
    upper_ref[HALF:, :] = jnp.dot(
        bottom_ref[...], jnp.concatenate([hi, lo, hi], axis=0), preferred_element_type=F32
    )
    out_ref[...] = front_ref[...] - jnp.dot(
        basis_ref[...], triple(upper_ref[...], 0), preferred_element_type=F32
    )


def project(places, c, chunks, factor, near, far, front, upper):
    top, bottom, basis = factor
    rows, columns = front.shape
    blocks = near.shape[0] // LEAD // 2
    begin = c * 2 * blocks
    near_at = chunks * 2 * blocks
    far_at = near_at + 2 * blocks

    def near_piece(odd):
        return lambda i, p: (p[near_at + 2 * jnp.minimum(i, blocks - 1) + odd], 0)

    def far_piece(odd):
        return lambda i, p: (p[far_at + 2 * jnp.maximum(i - blocks, 0) + odd], 0)

    in_specs = [
        pl.BlockSpec(top.shape, lambda i, p: (0, 0)),
        pl.BlockSpec(bottom.shape, lambda i, p: (0, 0)),
        pl.BlockSpec(basis.shape, lambda i, p: (0, 0)),
        pl.BlockSpec((LEAD, PB), near_piece(0)),
        pl.BlockSpec((LEAD, PB), near_piece(1)),
        pl.BlockSpec((LEAD, PB), far_piece(0)),
        pl.BlockSpec((LEAD, PB), far_piece(1)),
        pl.BlockSpec((rows, BLOCK), lambda i, p: (0, p[begin + i])),
    ]
    operands = [places, top, bottom, basis, near, near, far, far, front]
    aliases = {8: 1}
    if upper is not None:
        in_specs.append(pl.BlockSpec(memory_space=pl.ANY))
        operands.append(upper)
        aliases[9] = 0
    return pl.pallas_call(
        functools.partial(project_kernel, blocks),
        grid_spec=pltpu.PrefetchScalarGridSpec(
            num_scalar_prefetch=1,
            grid=(2 * blocks,),
            in_specs=in_specs,
            out_specs=(
                pl.BlockSpec((LEAD, BLOCK), lambda i, p: (0, p[begin + i])),
                pl.BlockSpec((rows, BLOCK), lambda i, p: (0, p[begin + i])),
                pl.BlockSpec((8, PB), lambda i, p: (0, 0)),
            ),
        ),
        out_shape=(
            jax.ShapeDtypeStruct((LEAD, columns), F32),
            jax.ShapeDtypeStruct((rows, columns), F32),
            jax.ShapeDtypeStruct((8, PB), F32),
        ),
        input_output_aliases=aliases,
        compiler_params=params(),
        cost_estimate=cost(3 * 10**9),
        name="project_columns",
    )(*operands)


def exchange(value, row_count):
    slots, width = value.shape
    shaped = value.reshape(row_count, slots // row_count, width)
    return lax.all_to_all(shaped, "row", split_axis=0, concat_axis=0, tiled=True).reshape(
        slots, width
    )


def on_device(front_matrix, child_rows, child_owner, child_offset):
    row_count = lax.axis_size("row")
    col_count = lax.axis_size("col")
    local_rows, local_cols = front_matrix.shape
    child_count = child_rows.shape[0]
    capacity = 2 * child_count // row_count
    me = lax.axis_index("row")

    owner, offset = child_owner[:, 0], child_offset[:, 0]
    packed = pack(child_rows, owner, row_count, capacity)
    child = exchange(packed, row_count)
    lead_rows = child_rows[:, :LEAD]
    first = first_hop(lead_rows, col_count)
    cut = local_rows // 2

    def cut_body(front_ref, low_ref, high_ref):
        low_ref[...] = front_ref[:cut, :]
        high_ref[...] = front_ref[cut:, :]

    low, high = ordered(
        "cut_lead", cut_body, [front_matrix[:, :LEAD]],
        [jax.ShapeDtypeStruct((cut, LEAD), F32)] * 2, (first,),
    )
    given = spread(lead_rows, first, col_count, (), False)
    pieces = list(pack_lead(given, owner, offset, row_count, capacity, local_rows, col_count))
    for mask in range(1, row_count):
        pairs = [(d, d ^ mask) for d in range(row_count)]
        pieces[mask] = lax.ppermute(pieces[mask], "row", pairs)
    low_got, high_got = first_hop(low, col_count), first_hop(high, col_count)
    own_piece = pieces[0]
    fronts = spread(low, low_got, col_count, (given[0],), True)
    fronts += spread(high, high_got, col_count, (child, own_piece), True)
    lead, left, place, gram = lead_setup(fronts, pieces, local_rows, col_count)

    chunks = max(1, min(4, local_cols // (PB * row_count)))
    width = local_cols // 2 // chunks
    blocks = width // BLOCK
    core = upper_side(0, row_count)
    *send, front = product(1 - core, left, place, front_matrix, child, None, chunks)
    *keep, front = product(core, left, place, front_matrix, child, front, chunks)

    halves = [split_add(1, row_count, keep[c], swap(send[c], 0, row_count), ()) for c in range(chunks)]

    matrix = total(gram, row_count, (keep[0],), tuple(h[0] for h in halves))
    made = []
    for k in range(PANELS):
        matrix = [eliminate(matrix, k)]
        made.append(matrix[0])
    matrix = matrix[0]
    scale = math.sqrt(local_rows * row_count)
    top, bottom, basis, scaled = finish(matrix, lead, scale)

    shards = [
        scatter_rest(*halves[c], row_count, (made[min(c, PANELS - 1)],))
        for c in range(chunks)
    ]
    steps = row_count.bit_length() - 1
    columns_at = [
        [
            ((d & 1) ^ side) * chunks * blocks + c * blocks + b
            for c in range(chunks)
            for side in range(2)
            for b in range(blocks)
        ]
        for d in range(row_count)
    ]
    order = piece_order(row_count).reshape(row_count, -1)
    table = np.concatenate([np.array(columns_at, np.int32), order], axis=1)
    places = lax.dynamic_index_in_dim(jnp.asarray(table), me, 0, keepdims=False)
    upper = None
    done = []
    for c in range(chunks):
        buf = shards[c][0]
        for step in reversed(range(steps)):
            got = swap(buf, step, row_count)
            if step == steps - 1 and step > 1:
                buf = join(buf, got, tuple(keep for _, keep in shards) + (top,))
            elif step == 1 and c >= LAG:
                buf = join(buf, got, (done[c - LAG],))
            elif step > 0:
                buf = jnp.concatenate([buf, got], axis=0)
        upper, front, at = project(places, c, chunks, (top, bottom, basis), buf, got, front, upper)
        done.append(at)
    return upper, front, scaled


def solution(mesh):
    placed = (P("row", "col"), P("row", "col"), P("row", None), P("row", None))
    return jax.shard_map(
        on_device,
        mesh=mesh,
        in_specs=placed,
        out_specs=(P(None, "col"), P("row", "col"), P("row", None)),
        check_vma=False,
    )
```

```python
import functools
import math

import jax
import jax.numpy as jnp
import numpy as np
from jax import lax
from jax.experimental import pallas as pl
from jax.experimental.pallas import tpu as pltpu
from jax.sharding import PartitionSpec as P

PB = 128
PANELS = 4
LEAD = PB * PANELS
HALF = LEAD // 2
LAG = 2
WIDE = 512
VMEM_BYTES = 48 * 1024 * 1024
HIGHEST = lax.Precision.HIGHEST
F32 = jnp.float32
BF16 = jnp.bfloat16
SMEM = pltpu.SMEM
VMEM = pltpu.VMEM


def params():
    return pltpu.CompilerParams(vmem_limit_bytes=VMEM_BYTES)


def cost(flops):
    return pl.CostEstimate(flops=flops, bytes_accessed=1 << 20, transcendentals=0)


def mask_orders(count):
    others = [1 << b for b in range(1, count.bit_length() - 1)]
    half = len(others) // 2
    return ([1] + others, [1] + others[half:] + others[:half])


def swap(value, step, count):
    orders = mask_orders(count)
    pairs = [(d, d ^ orders[d & 1][step]) for d in range(count)]
    return lax.ppermute(value, "row", pairs)


def upper_side(step, count):
    orders = mask_orders(count)
    me = lax.axis_index("row")
    mask = jnp.where(me & 1 == 0, orders[0][step], orders[1][step])
    return ((me & mask) != 0).astype(jnp.int32)


def shard_table(count):
    orders = mask_orders(count)
    steps = len(orders[0])
    return np.array(
        [
            sum(((d & orders[d & 1][t]) != 0) << (steps - 1 - t) for t in range(steps))
            for d in range(count)
        ]
    )


def piece_order(count):
    orders = mask_orders(count)
    steps = len(orders[0])
    shard = shard_table(count)

    def pieces(device, done):
        if done == 0:
            return [device]
        mask = orders[device & 1][steps - done]
        return pieces(device, done - 1) + pieces(device ^ mask, done - 1)

    half = count // 2
    order = np.zeros((count, 2, half), np.int32)
    for d in range(count):
        for at, piece in enumerate(pieces(d, steps)):
            order[d, at // half, shard[piece] % half] = at % half
    return order


def in_vmem(count):
    return [pl.BlockSpec(memory_space=VMEM)] * count


def ordered(name, body, operands, outs, after=()):
    count = len(operands)

    def kernel(*refs):
        body(*refs[:count], *refs[count + len(after) :])

    results = pl.pallas_call(
        kernel,
        out_shape=tuple(outs),
        in_specs=in_vmem(count) + [pl.BlockSpec(memory_space=pl.ANY)] * len(after),
        out_specs=tuple(in_vmem(len(outs))),
        compiler_params=params(),
        name=name,
    )(*operands, *after)
    return results if len(outs) > 1 else results[0]


def add_body(a_ref, b_ref, out_ref):
    out_ref[...] = a_ref[...] + b_ref[...]


def split_add(step, count, keep, got, after):
    def body(keep_ref, got_ref, keep_out, send_out):
        half = keep_out.shape[1]
        side = upper_side(step, count)
        for which, out in ((side, keep_out), (1 - side, send_out)):
            part = pl.ds(pl.multiple_of(which * half, 128), half)
            out[...] = keep_ref[:, part] + got_ref[:, part]

    half = jax.ShapeDtypeStruct((keep.shape[0], keep.shape[1] // 2), F32)
    return ordered("split_add", body, [keep, got], [half, half], after)


def scatter_rest(keep, send, count, after):
    steps = count.bit_length() - 1
    for step in range(1, steps):
        got = swap(send, step, count)
        if step == steps - 1:
            return keep + got, keep
        keep, send = split_add(step + 1, count, keep, got, after if step == steps - 2 else ())


def total(value, count, first_after, last_after):
    side = upper_side(0, count)
    half = value.shape[0] // 2
    keep = lax.dynamic_slice_in_dim(value, side * half, half, 0)
    send = lax.dynamic_slice_in_dim(value, (1 - side) * half, half, 0)
    mine = keep + swap(send, 0, count)
    for step in range(1, count.bit_length() - 1):
        got = swap(mine, step, count)
        mine = ordered(
            "add_gram", add_body, [mine, got], [jax.ShapeDtypeStruct(mine.shape, F32)],
            first_after * (step == 1) + last_after * (step == count.bit_length() - 2),
        )
    return mine, swap(mine, 0, count)


def spread(value, got, count, after, paired):
    middle = count // 2

    def body(value_ref, got_ref, out_ref):
        here = lax.axis_index("col") == middle
        out_ref[...] = jnp.where(here, got_ref[...], value_ref[...])

    passed = ordered("relay", body, [value, got], [jax.ShapeDtypeStruct(value.shape, F32)], after)
    others = [c for c in range(count - 1, 0, -1) if c != middle]
    if paired and count == 4:
        return [passed, lax.ppermute(passed, "col", [(0, 1), (2, 3)])]
    return [passed] + [lax.ppermute(passed, "col", [(middle, c)]) for c in others]


def pick(refs, count):
    me = lax.axis_index("col")
    held = (me == 0) | (me == count // 2)
    arrived = refs[1][...]
    for ref in refs[2:]:
        arrived = arrived + ref[...]
    return jnp.where(held, refs[0][...], arrived)


def first_hop(value, count):
    return lax.ppermute(value, "col", [(0, count // 2)])


def parts3(x):
    hi = x.astype(BF16)
    rest = x - hi.astype(F32)
    mid = rest.astype(BF16)
    return hi, mid, (rest - mid.astype(F32)).astype(BF16)


def parts2(x):
    hi = x.astype(BF16)
    return hi, (x - hi.astype(F32)).astype(BF16)


def place_rows(row_count, capacity, owner_ref, tally, child_count, write):
    for d in range(row_count):
        tally[d] = 0

    def body(i, carry):
        owner = owner_ref[i]
        rank = tally[owner]
        tally[owner] = rank + 1
        write(i, owner, rank)
        return carry

    lax.fori_loop(0, child_count, body, 0)


def pack_kernel(row_count, capacity, owner_ref, child_ref, out_ref, tally):
    out_ref[...] = jnp.zeros_like(out_ref)

    def write(i, owner, rank):
        out_ref[pl.ds(owner * capacity + rank, 1), :] = child_ref[pl.ds(i, 1), :]

    place_rows(row_count, capacity, owner_ref, tally, child_ref.shape[0], write)


def pack(child_rows, owner, row_count, capacity):
    return pl.pallas_call(
        functools.partial(pack_kernel, row_count, capacity),
        out_shape=jax.ShapeDtypeStruct((row_count * capacity, child_rows.shape[1]), F32),
        in_specs=[pl.BlockSpec(memory_space=SMEM)] + in_vmem(1),
        out_specs=in_vmem(1)[0],
        scratch_shapes=[pltpu.SMEM((row_count,), jnp.int32)],
        compiler_params=params(),
        name="pack_children",
    )(owner, child_rows)


def pack_lead_kernel(row_count, capacity, sentinel, col_count, given_count, owner_ref, offset_ref, *refs):
    given, refs = refs[:given_count], refs[given_count:]
    outs, (child_ref, rows_ref, tag_ref, tally) = refs[:row_count], refs[row_count:]
    child_ref[...] = pick(given, col_count)
    rows_ref[...] = jnp.zeros_like(rows_ref)
    tag_ref[...] = jnp.full(tag_ref.shape, sentinel, F32)
    me = lax.axis_index("row")

    def write(i, owner, rank):
        slot = (owner ^ me) * capacity + rank
        rows_ref[pl.ds(slot, 1), :] = child_ref[pl.ds(i, 1), :]
        tag_ref[pl.ds(slot, 1), :] = jnp.full((1, PB), offset_ref[i].astype(F32))

    place_rows(row_count, capacity, owner_ref, tally, child_ref.shape[0], write)
    for at, out in enumerate(outs):
        part = slice(at * capacity, (at + 1) * capacity)
        out[:, :LEAD] = rows_ref[part, :]
        out[:, LEAD:] = tag_ref[part, :]


def pack_lead(given, owner, offset, row_count, capacity, sentinel, col_count):
    slots = row_count * capacity
    return pl.pallas_call(
        functools.partial(pack_lead_kernel, row_count, capacity, float(sentinel), col_count, len(given)),
        out_shape=(jax.ShapeDtypeStruct((capacity, LEAD + PB), F32),) * row_count,
        in_specs=[pl.BlockSpec(memory_space=SMEM)] * 2 + in_vmem(len(given)),
        out_specs=tuple(in_vmem(row_count)),
        scratch_shapes=[
            pltpu.VMEM(given[0].shape, F32),
            pltpu.VMEM((slots, LEAD), F32),
            pltpu.VMEM((slots, PB), F32),
            pltpu.SMEM((row_count,), jnp.int32),
        ],
        compiler_params=params(),
        name="pack_lead",
    )(owner, offset, *given)


def triple(x, axis):
    hi, lo = parts2(x)
    return jnp.concatenate([hi, hi, lo] if axis == 1 else [hi, lo, hi], axis=axis)


def lead_kernel(row_count, col_count, each, *refs):
    front_refs, piece_refs = refs[: 2 * each], refs[2 * each : 2 * each + row_count]
    lead_ref, left_ref, place_ref, gram_ref = refs[2 * each + row_count :]
    front = jnp.concatenate(
        [pick(front_refs[:each], col_count), pick(front_refs[each:], col_count)], axis=0
    )
    me = lax.axis_index("row")
    pieces = [ref[...] for ref in piece_refs]
    bit = 1
    while bit < row_count:
        swapped = [pieces[at ^ bit] for at in range(row_count)]
        pieces = [jnp.where((me & bit) != 0, b, a) for a, b in zip(pieces, swapped)]
        bit *= 2
    child = jnp.concatenate(pieces, axis=0)
    rows, slots = front.shape[0], child.shape[0]
    place = jnp.transpose(child[:, LEAD:])[0:1, :]
    at = lax.broadcasted_iota(jnp.int32, (rows, slots), 0).astype(F32)
    onehot = jnp.where(at == place, 1.0, 0.0).astype(BF16)
    spots = jnp.concatenate([onehot, onehot, onehot], axis=1)
    place_ref[...] = spots
    parts = jnp.concatenate(parts3(child[:, :LEAD])[::-1], axis=0)
    lead = front + jnp.dot(spots, parts, preferred_element_type=F32)
    lead_ref[...] = lead
    turned = jnp.transpose(lead)
    left_ref[...] = triple(turned, 1)
    gram_ref[:, :HALF] = dot_high(turned[:HALF], lead[:, :HALF], ((1,), (0,)))
    gram_ref[:, HALF:] = dot_high(turned[HALF:], lead, ((1,), (0,)))


def lead_setup(fronts, pieces, rows, col_count):
    slots = len(pieces) * pieces[0].shape[0]
    operands = list(fronts) + list(pieces)
    return pl.pallas_call(
        functools.partial(lead_kernel, len(pieces), col_count, len(fronts) // 2),
        out_shape=(
            jax.ShapeDtypeStruct((rows, LEAD), F32),
            jax.ShapeDtypeStruct((LEAD, 3 * rows), BF16),
            jax.ShapeDtypeStruct((rows, 3 * slots), BF16),
            jax.ShapeDtypeStruct((HALF, LEAD + HALF), F32),
        ),
        in_specs=in_vmem(len(operands)),
        out_specs=tuple(in_vmem(4)),
        compiler_params=params(),
        name="lead_setup",
    )(*operands)


def product_kernel(blocks, chunks, base_ref, left_ref, place_ref, front_ref, child_ref, *rest):
    del base_ref
    outs, whole_ref = rest[-1 - chunks : -1], rest[-1]
    parts = jnp.concatenate(parts3(child_ref[...])[::-1], axis=0)
    whole = front_ref[...] + jnp.dot(place_ref[...], parts, preferred_element_type=F32)
    whole_ref[...] = whole
    result = jnp.dot(left_ref[...], triple(whole, 0), preferred_element_type=F32)
    for at, out in enumerate(outs):

        @pl.when(pl.program_id(0) // blocks == at)
        def _():
            out[...] = result


def product(half, left, place, front, child, whole, chunks):
    rows, columns = front.shape
    slots = child.shape[0]
    steps = columns // 2 // WIDE
    blocks = steps // chunks
    in_specs = [
        pl.BlockSpec(left.shape, lambda i, h: (0, 0)),
        pl.BlockSpec(place.shape, lambda i, h: (0, 0)),
        pl.BlockSpec((rows, WIDE), lambda i, h: (0, h[0] * steps + i)),
        pl.BlockSpec((slots, WIDE), lambda i, h: (0, h[0] * steps + i)),
    ]
    operands = [half[None], left, place, front, child]
    aliases = {}
    if whole is not None:
        in_specs.append(pl.BlockSpec(memory_space=pl.ANY))
        operands.append(whole)
        aliases = {5: chunks}

    def out_block(at):
        return lambda i, h: (0, jnp.clip(i - at * blocks, 0, blocks - 1))

    return pl.pallas_call(
        functools.partial(product_kernel, blocks, chunks),
        grid_spec=pltpu.PrefetchScalarGridSpec(
            num_scalar_prefetch=1,
            grid=(steps,),
            in_specs=in_specs,
            out_specs=tuple(pl.BlockSpec((LEAD, WIDE), out_block(at)) for at in range(chunks))
            + (pl.BlockSpec((rows, WIDE), lambda i, h: (0, h[0] * steps + i)),),
        ),
        out_shape=(jax.ShapeDtypeStruct((LEAD, columns // 2 // chunks), F32),) * chunks
        + (jax.ShapeDtypeStruct((rows, columns), F32),),
        input_output_aliases=aliases,
        compiler_params=params(),
        name="lead_product",
    )(*operands)


def join(a, b, after):
    def body(a_ref, b_ref, out_ref):
        half = a_ref.shape[0]
        out_ref[:half, :] = a_ref[...]
        out_ref[half:, :] = b_ref[...]

    shape = jax.ShapeDtypeStruct((2 * a.shape[0], a.shape[1]), F32)
    return ordered("join_pieces", body, [a, b], [shape], after)


def dot_high(a, b, dims):
    return lax.dot_general(a, b, (dims, ((), ())), precision=HIGHEST, preferred_element_type=F32)


def spread_lane(tile, at):
    return jnp.broadcast_to(tile[:, at : at + 1], tile.shape)


def invert_factor(block):
    lane = lax.broadcasted_iota(jnp.int32, (8, PB), 1)
    sub = lax.broadcasted_iota(jnp.int32, (8, PB), 0)
    count = PB // 8
    tiles = [block[8 * t : 8 * t + 8, :] for t in range(count)]
    for b in range(count):
        first = 8 * b
        rows = tiles[b]
        cols = [spread_lane(rows, first + c) for c in range(8)]
        heads, inverses = {}, []
        for c in range(8):
            inverse = 1.0 / cols[c][c : c + 1, :]
            inverses.append(inverse)
            factor = jnp.where(sub > c, cols[c] * inverse, 0.0)
            here = lane == first + c
            source = jnp.where(here[0:1, :], 1.0, rows[c : c + 1, :])
            rows = jnp.where(here & (sub > c), 0.0, rows) - factor * source
            for d in range(c + 1, 8):
                heads[c, d] = cols[d][c : c + 1, :]
                cols[d] = cols[d] - factor * heads[c, d]
        tiles[b] = rows
        inside = (lane >= first) & (lane < first + 8)
        past = inside & (lane - first >= sub)
        used = jnp.where(past, jnp.where(lane - first == sub, 1.0, 0.0), rows)
        for t in range(b + 1, count):
            tile = tiles[t]
            factors = []
            for c in range(8):
                factor = spread_lane(tile, first + c)
                for d in range(c):
                    factor = factor - factors[d] * heads[d, c]
                factors.append(factor * inverses[c])
            tile = jnp.where(inside, 0.0, tile)
            for c in range(8):
                tile = tile - factors[c] * used[c : c + 1, :]
            tiles[t] = tile
    done = []
    for t in range(count):
        diagonal = lane == sub + 8 * t
        pivot = jnp.sum(jnp.where(diagonal, tiles[t], 0.0), axis=1, keepdims=True)
        scale = lax.rsqrt(pivot)
        scale = scale * (1.5 - 0.5 * pivot * scale * scale)
        unit = jnp.where(diagonal, 1.0, jnp.where(lane < sub + 8 * t, tiles[t], 0.0))
        done.append(unit * scale)
    return jnp.concatenate(done, axis=0)


def eliminate_kernel(k, *refs):
    in_ref, out_ref = refs[0], refs[-1]
    lo, hi = k * PB, (k + 1) * PB
    if k == 0:
        mine, got = refs[0][...], refs[1][...]
        low = lax.axis_index("row") % 2 == 0
        packed = jnp.concatenate([jnp.where(low, mine, got), jnp.where(low, got, mine)], axis=0)
        cross = packed[:, HALF:LEAD]
        out_ref[:HALF, :HALF] = packed[:, :HALF]
        out_ref[HALF:, :HALF] = cross
        out_ref[:HALF, HALF:] = jnp.transpose(cross)
        out_ref[HALF:, HALF:] = packed[:, LEAD:]
        in_ref = out_ref
    else:
        out_ref[:lo, :] = in_ref[:lo, :]
    inverse = invert_factor(in_ref[lo:hi, lo:hi])
    pieces = []
    for j in range(PANELS):
        if j == k:
            pieces.append(inverse)
        else:
            pieces.append(dot_high(inverse, in_ref[lo:hi, j * PB : (j + 1) * PB], ((1,), (0,))))
    row = jnp.concatenate(pieces, axis=1)
    out_ref[lo:hi, :] = row
    if k < PANELS - 1:
        column = dot_high(in_ref[hi:, lo:hi], inverse, ((1,), (1,)))
        change = dot_high(column, row, ((1,), (0,)))
        later = in_ref[hi:, :]
        out_ref[hi:, :] = later - change
        out_ref[hi:, lo:hi] = -change[:, lo:hi]


def eliminate(operands, k):
    return pl.pallas_call(
        functools.partial(eliminate_kernel, k),
        out_shape=jax.ShapeDtypeStruct((LEAD, LEAD), F32),
        in_specs=in_vmem(len(operands)),
        out_specs=in_vmem(1)[0],
        compiler_params=params(),
        cost_estimate=cost(6 * 10**9),
        name="eliminate_panel",
    )(*operands)


def finish_kernel(scale, matrix_ref, lead_ref, top_ref, bottom_ref, basis3_ref, basis_ref):
    own = lax.broadcasted_iota(jnp.int32, (LEAD, LEAD), 0) // PB
    other = lax.broadcasted_iota(jnp.int32, (LEAD, LEAD), 1) // PB
    inverse = jnp.where(own >= other, matrix_ref[...], 0.0)
    top_ref[...] = triple(inverse[:HALF, :HALF], 1)
    bottom_ref[...] = triple(inverse[HALF:], 1)
    basis = dot_high(lead_ref[...], inverse, ((1,), (1,)))
    basis3_ref[...] = triple(basis, 1)
    basis_ref[...] = basis * scale


def finish(matrix, lead, scale):
    rows = lead.shape[0]
    return pl.pallas_call(
        functools.partial(finish_kernel, scale),
        out_shape=(
            jax.ShapeDtypeStruct((HALF, 3 * HALF), BF16),
            jax.ShapeDtypeStruct((HALF, 3 * LEAD), BF16),
            jax.ShapeDtypeStruct((rows, 3 * LEAD), BF16),
            jax.ShapeDtypeStruct((rows, LEAD), F32),
        ),
        in_specs=[pl.BlockSpec(memory_space=VMEM)] * 2,
        out_specs=(pl.BlockSpec(memory_space=VMEM),) * 4,
        compiler_params=params(),
        cost_estimate=cost(2 * 10**9),
        name="finish_factor",
    )(matrix, lead)


def project_kernel(blocks, places_ref, top_ref, bottom_ref, basis_ref, *rest):
    del places_ref
    each = WIDE // PB
    near_refs, far_refs, front_ref = rest[:each], rest[each : 2 * each], rest[2 * each]
    upper_ref, out_ref, done_ref = rest[-3:]
    done_ref[...] = jnp.zeros_like(done_ref)
    near = pl.program_id(0) < blocks
    sums = jnp.concatenate(
        [jnp.where(near, a[...], b[...]) for a, b in zip(near_refs, far_refs)], axis=1
    )
    hi, lo = parts2(sums)
    upper_ref[:HALF, :] = jnp.dot(
        top_ref[...],
        jnp.concatenate([hi[:HALF], lo[:HALF], hi[:HALF]], axis=0),
        preferred_element_type=F32,
    )
    upper_ref[HALF:, :] = jnp.dot(
        bottom_ref[...], jnp.concatenate([hi, lo, hi], axis=0), preferred_element_type=F32
    )
    out_ref[...] = front_ref[...] - jnp.dot(
        basis_ref[...], triple(upper_ref[...], 0), preferred_element_type=F32
    )


def project(places, c, chunks, factor, near, far, front, upper):
    top, bottom, basis = factor
    rows, columns = front.shape
    each = WIDE // PB
    blocks = near.shape[0] // LEAD // each
    begin = c * 2 * blocks
    near_at = chunks * 2 * blocks
    far_at = near_at + each * blocks

    def near_piece(j):
        return lambda i, p: (p[near_at + each * jnp.minimum(i, blocks - 1) + j], 0)

    def far_piece(j):
        return lambda i, p: (p[far_at + each * jnp.maximum(i - blocks, 0) + j], 0)

    in_specs = [
        pl.BlockSpec(top.shape, lambda i, p: (0, 0)),
        pl.BlockSpec(bottom.shape, lambda i, p: (0, 0)),
        pl.BlockSpec(basis.shape, lambda i, p: (0, 0)),
        *[pl.BlockSpec((LEAD, PB), near_piece(j)) for j in range(each)],
        *[pl.BlockSpec((LEAD, PB), far_piece(j)) for j in range(each)],
        pl.BlockSpec((rows, WIDE), lambda i, p: (0, p[begin + i])),
    ]
    operands = [places, top, bottom, basis] + [near] * each + [far] * each + [front]
    aliases = {4 + 2 * each: 1}
    if upper is not None:
        in_specs.append(pl.BlockSpec(memory_space=pl.ANY))
        operands.append(upper)
        aliases[5 + 2 * each] = 0
    return pl.pallas_call(
        functools.partial(project_kernel, blocks),
        grid_spec=pltpu.PrefetchScalarGridSpec(
            num_scalar_prefetch=1,
            grid=(2 * blocks,),
            in_specs=in_specs,
            out_specs=(
                pl.BlockSpec((LEAD, WIDE), lambda i, p: (0, p[begin + i])),
                pl.BlockSpec((rows, WIDE), lambda i, p: (0, p[begin + i])),
                pl.BlockSpec((8, PB), lambda i, p: (0, 0)),
            ),
        ),
        out_shape=(
            jax.ShapeDtypeStruct((LEAD, columns), F32),
            jax.ShapeDtypeStruct((rows, columns), F32),
            jax.ShapeDtypeStruct((8, PB), F32),
        ),
        input_output_aliases=aliases,
        compiler_params=params(),
        cost_estimate=cost(3 * 10**9),
        name="project_columns",
    )(*operands)


def exchange(value, row_count):
    slots, width = value.shape
    shaped = value.reshape(row_count, slots // row_count, width)
    return lax.all_to_all(shaped, "row", split_axis=0, concat_axis=0, tiled=True).reshape(
        slots, width
    )


def on_device(front_matrix, child_rows, child_owner, child_offset):
    row_count = lax.axis_size("row")
    col_count = lax.axis_size("col")
    local_rows, local_cols = front_matrix.shape
    child_count = child_rows.shape[0]
    capacity = 2 * child_count // row_count
    me = lax.axis_index("row")

    owner, offset = child_owner[:, 0], child_offset[:, 0]
    packed = pack(child_rows, owner, row_count, capacity)
    child = exchange(packed, row_count)
    lead_rows = child_rows[:, :LEAD]
    first = first_hop(lead_rows, col_count)
    cut = local_rows // 2

    def cut_body(front_ref, low_ref, high_ref):
        low_ref[...] = front_ref[:cut, :]
        high_ref[...] = front_ref[cut:, :]

    low, high = ordered(
        "cut_lead", cut_body, [front_matrix[:, :LEAD]],
        [jax.ShapeDtypeStruct((cut, LEAD), F32)] * 2, (first,),
    )
    given = spread(lead_rows, first, col_count, (), False)
    pieces = list(pack_lead(given, owner, offset, row_count, capacity, local_rows, col_count))
    for mask in range(1, row_count):
        pairs = [(d, d ^ mask) for d in range(row_count)]
        pieces[mask] = lax.ppermute(pieces[mask], "row", pairs)
    low_got, high_got = first_hop(low, col_count), first_hop(high, col_count)
    own_piece = pieces[0]
    fronts = spread(low, low_got, col_count, (given[0],), True)
    fronts += spread(high, high_got, col_count, (child, own_piece), True)
    lead, left, place, gram = lead_setup(fronts, pieces, local_rows, col_count)

    chunks = max(1, min(4, local_cols // (PB * row_count)))
    width = local_cols // 2 // chunks
    blocks = width // WIDE
    core = upper_side(0, row_count)
    *send, front = product(1 - core, left, place, front_matrix, child, None, chunks)
    *keep, front = product(core, left, place, front_matrix, child, front, chunks)

    halves = [split_add(1, row_count, keep[c], swap(send[c], 0, row_count), ()) for c in range(chunks)]

    matrix = total(gram, row_count, (keep[0],), tuple(h[0] for h in halves))
    made = []
    for k in range(PANELS):
        matrix = [eliminate(matrix, k)]
        made.append(matrix[0])
    matrix = matrix[0]
    scale = math.sqrt(local_rows * row_count)
    top, bottom, basis, scaled = finish(matrix, lead, scale)

    shards = [
        scatter_rest(*halves[c], row_count, (made[min(c, PANELS - 1)],))
        for c in range(chunks)
    ]
    steps = row_count.bit_length() - 1
    columns_at = [
        [
            ((d & 1) ^ side) * chunks * blocks + c * blocks + b
            for c in range(chunks)
            for side in range(2)
            for b in range(blocks)
        ]
        for d in range(row_count)
    ]
    order = piece_order(row_count).reshape(row_count, -1)
    table = np.concatenate([np.array(columns_at, np.int32), order], axis=1)
    places = lax.dynamic_index_in_dim(jnp.asarray(table), me, 0, keepdims=False)
    upper = None
    done = []
    for c in range(chunks):
        buf = shards[c][0]
        for step in reversed(range(steps)):
            got = swap(buf, step, row_count)
            if step == steps - 1 and step > 1:
                buf = join(buf, got, tuple(keep for _, keep in shards) + (top,))
            elif step == 1 and c >= LAG:
                buf = join(buf, got, (done[c - LAG],))
            elif step > 0:
                buf = jnp.concatenate([buf, got], axis=0)
        upper, front, at = project(places, c, chunks, (top, bottom, basis), buf, got, front, upper)
        done.append(at)
    return upper, front, scaled


def solution(mesh):
    placed = (P("row", "col"), P("row", "col"), P("row", None), P("row", None))
    return jax.shard_map(
        on_device,
        mesh=mesh,
        in_specs=placed,
        out_specs=(P(None, "col"), P("row", "col"), P("row", None)),
        check_vma=False,
    )
```

```python
import functools
import math

import jax
import jax.numpy as jnp
import numpy as np
from jax import lax
from jax.experimental import pallas as pl
from jax.experimental.pallas import tpu as pltpu
from jax.sharding import PartitionSpec as P

PB = 128
PANELS = 4
LEAD = PB * PANELS
HALF = LEAD // 2
LAG = 2
WIDE = 512
VMEM_BYTES = 40 * 1024 * 1024
HIGHEST = lax.Precision.HIGHEST
F32 = jnp.float32
BF16 = jnp.bfloat16
SMEM = pltpu.SMEM
VMEM = pltpu.VMEM


def params():
    return pltpu.CompilerParams(vmem_limit_bytes=VMEM_BYTES)


def cost(flops):
    return pl.CostEstimate(flops=flops, bytes_accessed=1 << 20, transcendentals=0)


def mask_orders(count):
    others = [1 << b for b in range(1, count.bit_length() - 1)]
    half = len(others) // 2
    return ([1] + others, [1] + others[half:] + others[:half])


def swap(value, step, count):
    orders = mask_orders(count)
    pairs = [(d, d ^ orders[d & 1][step]) for d in range(count)]
    return lax.ppermute(value, "row", pairs)


def upper_side(step, count):
    orders = mask_orders(count)
    me = lax.axis_index("row")
    mask = jnp.where(me & 1 == 0, orders[0][step], orders[1][step])
    return ((me & mask) != 0).astype(jnp.int32)


def shard_table(count):
    orders = mask_orders(count)
    steps = len(orders[0])
    return np.array(
        [
            sum(((d & orders[d & 1][t]) != 0) << (steps - 1 - t) for t in range(steps))
            for d in range(count)
        ]
    )


def piece_order(count):
    orders = mask_orders(count)
    steps = len(orders[0])
    shard = shard_table(count)

    def pieces(device, done):
        if done == 0:
            return [device]
        mask = orders[device & 1][steps - done]
        return pieces(device, done - 1) + pieces(device ^ mask, done - 1)

    half = count // 2
    order = np.zeros((count, 2, half), np.int32)
    for d in range(count):
        for at, piece in enumerate(pieces(d, steps)):
            order[d, at // half, shard[piece] % half] = at % half
    return order


def in_vmem(count):
    return [pl.BlockSpec(memory_space=VMEM)] * count


def ordered(name, body, operands, outs, after=()):
    count = len(operands)

    def kernel(*refs):
        body(*refs[:count], *refs[count + len(after) :])

    results = pl.pallas_call(
        kernel,
        out_shape=tuple(outs),
        in_specs=in_vmem(count) + [pl.BlockSpec(memory_space=pl.ANY)] * len(after),
        out_specs=tuple(in_vmem(len(outs))),
        compiler_params=params(),
        name=name,
    )(*operands, *after)
    return results if len(outs) > 1 else results[0]


def add_body(a_ref, b_ref, out_ref):
    out_ref[...] = a_ref[...] + b_ref[...]


def split_add(step, count, keep, got, after):
    def body(keep_ref, got_ref, keep_out, send_out):
        half = keep_out.shape[1]
        side = upper_side(step, count)
        for which, out in ((side, keep_out), (1 - side, send_out)):
            part = pl.ds(pl.multiple_of(which * half, 128), half)
            out[...] = keep_ref[:, part] + got_ref[:, part]

    half = jax.ShapeDtypeStruct((keep.shape[0], keep.shape[1] // 2), F32)
    return ordered("split_add", body, [keep, got], [half, half], after)


def scatter_rest(keep, send, count, after):
    steps = count.bit_length() - 1
    for step in range(1, steps):
        got = swap(send, step, count)
        if step == steps - 1:
            return keep + got, keep
        keep, send = split_add(step + 1, count, keep, got, after if step == steps - 2 else ())


def total(value, count, first_after, last_after):
    side = upper_side(0, count)
    half = value.shape[0] // 2
    keep = lax.dynamic_slice_in_dim(value, side * half, half, 0)
    send = lax.dynamic_slice_in_dim(value, (1 - side) * half, half, 0)
    mine = keep + swap(send, 0, count)
    for step in range(1, count.bit_length() - 1):
        got = swap(mine, step, count)
        mine = ordered(
            "add_gram", add_body, [mine, got], [jax.ShapeDtypeStruct(mine.shape, F32)],
            first_after * (step == 1) + last_after * (step == count.bit_length() - 2),
        )
    return mine, swap(mine, 0, count)


def spread(value, got, count, after, paired):
    middle = count // 2

    def body(value_ref, got_ref, out_ref):
        here = lax.axis_index("col") == middle
        out_ref[...] = jnp.where(here, got_ref[...], value_ref[...])

    passed = ordered("relay", body, [value, got], [jax.ShapeDtypeStruct(value.shape, F32)], after)
    others = [c for c in range(count - 1, 0, -1) if c != middle]
    if paired and count == 4:
        return [passed, lax.ppermute(passed, "col", [(0, 1), (2, 3)])]
    return [passed] + [lax.ppermute(passed, "col", [(middle, c)]) for c in others]


def pick(refs, count):
    me = lax.axis_index("col")
    held = (me == 0) | (me == count // 2)
    arrived = refs[1][...]
    for ref in refs[2:]:
        arrived = arrived + ref[...]
    return jnp.where(held, refs[0][...], arrived)


def first_hop(value, count):
    return lax.ppermute(value, "col", [(0, count // 2)])


def parts3(x):
    hi = x.astype(BF16)
    rest = x - hi.astype(F32)
    mid = rest.astype(BF16)
    return hi, mid, (rest - mid.astype(F32)).astype(BF16)


def parts2(x):
    hi = x.astype(BF16)
    return hi, (x - hi.astype(F32)).astype(BF16)


def place_rows(row_count, capacity, owner_ref, tally, child_count, write):
    for d in range(row_count):
        tally[d] = 0

    def body(i, carry):
        owner = owner_ref[i]
        rank = tally[owner]
        tally[owner] = rank + 1
        write(i, owner, rank)
        return carry

    lax.fori_loop(0, child_count, body, 0)


def pack_kernel(row_count, capacity, owner_ref, child_ref, out_ref, tally):
    out_ref[...] = jnp.zeros_like(out_ref)

    def write(i, owner, rank):
        out_ref[pl.ds(owner * capacity + rank, 1), :] = child_ref[pl.ds(i, 1), :]

    place_rows(row_count, capacity, owner_ref, tally, child_ref.shape[0], write)


def pack(child_rows, owner, row_count, capacity):
    return pl.pallas_call(
        functools.partial(pack_kernel, row_count, capacity),
        out_shape=jax.ShapeDtypeStruct((row_count * capacity, child_rows.shape[1]), F32),
        in_specs=[pl.BlockSpec(memory_space=SMEM)] + in_vmem(1),
        out_specs=in_vmem(1)[0],
        scratch_shapes=[pltpu.SMEM((row_count,), jnp.int32)],
        compiler_params=params(),
        name="pack_children",
    )(owner, child_rows)


def pack_lead_kernel(row_count, capacity, sentinel, col_count, given_count, owner_ref, offset_ref, *refs):
    given, refs = refs[:given_count], refs[given_count:]
    outs, (child_ref, rows_ref, tag_ref, tally) = refs[:row_count], refs[row_count:]
    child_ref[...] = pick(given, col_count)
    rows_ref[...] = jnp.zeros_like(rows_ref)
    tag_ref[...] = jnp.full(tag_ref.shape, sentinel, F32)
    me = lax.axis_index("row")

    def write(i, owner, rank):
        slot = (owner ^ me) * capacity + rank
        rows_ref[pl.ds(slot, 1), :] = child_ref[pl.ds(i, 1), :]
        tag_ref[pl.ds(slot, 1), :] = jnp.full((1, PB), offset_ref[i].astype(F32))

    place_rows(row_count, capacity, owner_ref, tally, child_ref.shape[0], write)
    for at, out in enumerate(outs):
        part = slice(at * capacity, (at + 1) * capacity)
        out[:, :LEAD] = rows_ref[part, :]
        out[:, LEAD:] = tag_ref[part, :]


def pack_lead(given, owner, offset, row_count, capacity, sentinel, col_count):
    slots = row_count * capacity
    return pl.pallas_call(
        functools.partial(pack_lead_kernel, row_count, capacity, float(sentinel), col_count, len(given)),
        out_shape=(jax.ShapeDtypeStruct((capacity, LEAD + PB), F32),) * row_count,
        in_specs=[pl.BlockSpec(memory_space=SMEM)] * 2 + in_vmem(len(given)),
        out_specs=tuple(in_vmem(row_count)),
        scratch_shapes=[
            pltpu.VMEM(given[0].shape, F32),
            pltpu.VMEM((slots, LEAD), F32),
            pltpu.VMEM((slots, PB), F32),
            pltpu.SMEM((row_count,), jnp.int32),
        ],
        compiler_params=params(),
        name="pack_lead",
    )(owner, offset, *given)


def triple(x, axis):
    hi, lo = parts2(x)
    return jnp.concatenate([hi, hi, lo] if axis == 1 else [hi, lo, hi], axis=axis)


def lead_kernel(row_count, col_count, each, *refs):
    front_refs, piece_refs = refs[: 2 * each], refs[2 * each : 2 * each + row_count]
    lead_ref, left_ref, place_ref, gram_ref = refs[2 * each + row_count :]
    front = jnp.concatenate(
        [pick(front_refs[:each], col_count), pick(front_refs[each:], col_count)], axis=0
    )
    me = lax.axis_index("row")
    pieces = [ref[...] for ref in piece_refs]
    bit = 1
    while bit < row_count:
        swapped = [pieces[at ^ bit] for at in range(row_count)]
        pieces = [jnp.where((me & bit) != 0, b, a) for a, b in zip(pieces, swapped)]
        bit *= 2
    child = jnp.concatenate(pieces, axis=0)
    rows, slots = front.shape[0], child.shape[0]
    place = jnp.transpose(child[:, LEAD:])[0:1, :]
    at = lax.broadcasted_iota(jnp.int32, (rows, slots), 0).astype(F32)
    onehot = jnp.where(at == place, 1.0, 0.0).astype(BF16)
    spots = jnp.concatenate([onehot, onehot, onehot], axis=1)
    place_ref[...] = spots
    parts = jnp.concatenate(parts3(child[:, :LEAD])[::-1], axis=0)
    lead = front + jnp.dot(spots, parts, preferred_element_type=F32)
    lead_ref[...] = lead
    turned = jnp.transpose(lead)
    left_ref[...] = triple(turned, 1)
    gram_ref[:, :HALF] = dot_high(turned[:HALF], lead[:, :HALF], ((1,), (0,)))
    gram_ref[:, HALF:] = dot_high(turned[HALF:], lead, ((1,), (0,)))


def lead_setup(fronts, pieces, rows, col_count):
    slots = len(pieces) * pieces[0].shape[0]
    operands = list(fronts) + list(pieces)
    return pl.pallas_call(
        functools.partial(lead_kernel, len(pieces), col_count, len(fronts) // 2),
        out_shape=(
            jax.ShapeDtypeStruct((rows, LEAD), F32),
            jax.ShapeDtypeStruct((LEAD, 3 * rows), BF16),
            jax.ShapeDtypeStruct((rows, 3 * slots), BF16),
            jax.ShapeDtypeStruct((HALF, LEAD + HALF), F32),
        ),
        in_specs=in_vmem(len(operands)),
        out_specs=tuple(in_vmem(4)),
        compiler_params=params(),
        name="lead_setup",
    )(*operands)


def product_kernel(blocks, chunks, base_ref, left_ref, place_ref, front_ref, child_ref, *rest):
    del base_ref
    outs, whole_ref = rest[-1 - chunks : -1], rest[-1]
    parts = jnp.concatenate(parts3(child_ref[...])[::-1], axis=0)
    whole = front_ref[...] + jnp.dot(place_ref[...], parts, preferred_element_type=F32)
    whole_ref[...] = whole
    result = jnp.dot(left_ref[...], triple(whole, 0), preferred_element_type=F32)
    for at, out in enumerate(outs):

        @pl.when(pl.program_id(0) // blocks == at)
        def _():
            out[...] = result


def product(half, left, place, front, child, whole, chunks):
    rows, columns = front.shape
    slots = child.shape[0]
    steps = columns // 2 // WIDE
    blocks = steps // chunks
    in_specs = [
        pl.BlockSpec(left.shape, lambda i, h: (0, 0)),
        pl.BlockSpec(place.shape, lambda i, h: (0, 0)),
        pl.BlockSpec((rows, WIDE), lambda i, h: (0, h[0] * steps + i)),
        pl.BlockSpec((slots, WIDE), lambda i, h: (0, h[0] * steps + i)),
    ]
    operands = [half[None], left, place, front, child]
    aliases = {}
    if whole is not None:
        in_specs.append(pl.BlockSpec(memory_space=pl.ANY))
        operands.append(whole)
        aliases = {5: chunks}

    def out_block(at):
        return lambda i, h: (0, jnp.clip(i - at * blocks, 0, blocks - 1))

    return pl.pallas_call(
        functools.partial(product_kernel, blocks, chunks),
        grid_spec=pltpu.PrefetchScalarGridSpec(
            num_scalar_prefetch=1,
            grid=(steps,),
            in_specs=in_specs,
            out_specs=tuple(pl.BlockSpec((LEAD, WIDE), out_block(at)) for at in range(chunks))
            + (pl.BlockSpec((rows, WIDE), lambda i, h: (0, h[0] * steps + i)),),
        ),
        out_shape=(jax.ShapeDtypeStruct((LEAD, columns // 2 // chunks), F32),) * chunks
        + (jax.ShapeDtypeStruct((rows, columns), F32),),
        input_output_aliases=aliases,
        compiler_params=params(),
        name="lead_product",
    )(*operands)


def join(a, b, after):
    def body(a_ref, b_ref, out_ref):
        half = a_ref.shape[0]
        out_ref[:half, :] = a_ref[...]
        out_ref[half:, :] = b_ref[...]

    shape = jax.ShapeDtypeStruct((2 * a.shape[0], a.shape[1]), F32)
    return ordered("join_pieces", body, [a, b], [shape], after)


def dot_high(a, b, dims):
    return lax.dot_general(a, b, (dims, ((), ())), precision=HIGHEST, preferred_element_type=F32)


def spread_lane(tile, at):
    return jnp.broadcast_to(tile[:, at : at + 1], tile.shape)


def invert_factor(block):
    lane = lax.broadcasted_iota(jnp.int32, (8, PB), 1)
    sub = lax.broadcasted_iota(jnp.int32, (8, PB), 0)
    count = PB // 8
    tiles = [block[8 * t : 8 * t + 8, :] for t in range(count)]
    for b in range(count):
        first = 8 * b
        rows = tiles[b]
        cols = [spread_lane(rows, first + c) for c in range(8)]
        heads, inverses = {}, []
        for c in range(8):
            inverse = 1.0 / cols[c][c : c + 1, :]
            inverses.append(inverse)
            factor = jnp.where(sub > c, cols[c] * inverse, 0.0)
            here = lane == first + c
            source = jnp.where(here[0:1, :], 1.0, rows[c : c + 1, :])
            rows = jnp.where(here & (sub > c), 0.0, rows) - factor * source
            for d in range(c + 1, 8):
                heads[c, d] = cols[d][c : c + 1, :]
                cols[d] = cols[d] - factor * heads[c, d]
        tiles[b] = rows
        inside = (lane >= first) & (lane < first + 8)
        past = inside & (lane - first >= sub)
        used = jnp.where(past, jnp.where(lane - first == sub, 1.0, 0.0), rows)
        for t in range(b + 1, count):
            tile = tiles[t]
            factors = []
            for c in range(8):
                factor = spread_lane(tile, first + c)
                for d in range(c):
                    factor = factor - factors[d] * heads[d, c]
                factors.append(factor * inverses[c])
            tile = jnp.where(inside, 0.0, tile)
            for c in range(8):
                tile = tile - factors[c] * used[c : c + 1, :]
            tiles[t] = tile
    done = []
    for t in range(count):
        diagonal = lane == sub + 8 * t
        pivot = jnp.sum(jnp.where(diagonal, tiles[t], 0.0), axis=1, keepdims=True)
        scale = lax.rsqrt(pivot)
        scale = scale * (1.5 - 0.5 * pivot * scale * scale)
        unit = jnp.where(diagonal, 1.0, jnp.where(lane < sub + 8 * t, tiles[t], 0.0))
        done.append(unit * scale)
    return jnp.concatenate(done, axis=0)


def eliminate_kernel(k, *refs):
    in_ref, out_ref = refs[0], refs[-1]
    lo, hi = k * PB, (k + 1) * PB
    if k == 0:
        mine, got = refs[0][...], refs[1][...]
        low = lax.axis_index("row") % 2 == 0
        packed = jnp.concatenate([jnp.where(low, mine, got), jnp.where(low, got, mine)], axis=0)
        cross = packed[:, HALF:LEAD]
        out_ref[:HALF, :HALF] = packed[:, :HALF]
        out_ref[HALF:, :HALF] = cross
        out_ref[:HALF, HALF:] = jnp.transpose(cross)
        out_ref[HALF:, HALF:] = packed[:, LEAD:]
        in_ref = out_ref
    else:
        out_ref[:lo, :] = in_ref[:lo, :]
    inverse = invert_factor(in_ref[lo:hi, lo:hi])
    pieces = []
    for j in range(PANELS):
        if j == k:
            pieces.append(inverse)
        else:
            pieces.append(dot_high(inverse, in_ref[lo:hi, j * PB : (j + 1) * PB], ((1,), (0,))))
    row = jnp.concatenate(pieces, axis=1)
    out_ref[lo:hi, :] = row
    if k < PANELS - 1:
        column = dot_high(in_ref[hi:, lo:hi], inverse, ((1,), (1,)))
        change = dot_high(column, row, ((1,), (0,)))
        later = in_ref[hi:, :]
        out_ref[hi:, :] = later - change
        out_ref[hi:, lo:hi] = -change[:, lo:hi]


def eliminate(operands, k):
    return pl.pallas_call(
        functools.partial(eliminate_kernel, k),
        out_shape=jax.ShapeDtypeStruct((LEAD, LEAD), F32),
        in_specs=in_vmem(len(operands)),
        out_specs=in_vmem(1)[0],
        compiler_params=params(),
        cost_estimate=cost(6 * 10**9),
        name="eliminate_panel",
    )(*operands)


def finish_kernel(scale, matrix_ref, lead_ref, top_ref, bottom_ref, basis3_ref, basis_ref):
    own = lax.broadcasted_iota(jnp.int32, (LEAD, LEAD), 0) // PB
    other = lax.broadcasted_iota(jnp.int32, (LEAD, LEAD), 1) // PB
    inverse = jnp.where(own >= other, matrix_ref[...], 0.0)
    top_ref[...] = triple(inverse[:HALF, :HALF], 1)
    bottom_ref[...] = triple(inverse[HALF:], 1)
    basis = dot_high(lead_ref[...], inverse, ((1,), (1,)))
    basis3_ref[...] = triple(basis, 1)
    basis_ref[...] = basis * scale


def finish(matrix, lead, scale):
    rows = lead.shape[0]
    return pl.pallas_call(
        functools.partial(finish_kernel, scale),
        out_shape=(
            jax.ShapeDtypeStruct((HALF, 3 * HALF), BF16),
            jax.ShapeDtypeStruct((HALF, 3 * LEAD), BF16),
            jax.ShapeDtypeStruct((rows, 3 * LEAD), BF16),
            jax.ShapeDtypeStruct((rows, LEAD), F32),
        ),
        in_specs=[pl.BlockSpec(memory_space=VMEM)] * 2,
        out_specs=(pl.BlockSpec(memory_space=VMEM),) * 4,
        compiler_params=params(),
        cost_estimate=cost(2 * 10**9),
        name="finish_factor",
    )(matrix, lead)


def project_kernel(blocks, places_ref, top_ref, bottom_ref, basis_ref, *rest):
    del places_ref
    each = WIDE // PB
    near_refs, far_refs, front_ref = rest[:each], rest[each : 2 * each], rest[2 * each]
    upper_ref, out_ref, done_ref = rest[-3:]
    done_ref[...] = jnp.zeros_like(done_ref)
    near = pl.program_id(0) < blocks
    sums = jnp.concatenate(
        [jnp.where(near, a[...], b[...]) for a, b in zip(near_refs, far_refs)], axis=1
    )
    hi, lo = parts2(sums)
    upper_ref[:HALF, :] = jnp.dot(
        top_ref[...],
        jnp.concatenate([hi[:HALF], lo[:HALF], hi[:HALF]], axis=0),
        preferred_element_type=F32,
    )
    upper_ref[HALF:, :] = jnp.dot(
        bottom_ref[...], jnp.concatenate([hi, lo, hi], axis=0), preferred_element_type=F32
    )
    out_ref[...] = front_ref[...] - jnp.dot(
        basis_ref[...], triple(upper_ref[...], 0), preferred_element_type=F32
    )


def project(places, c, chunks, factor, near, far, front, upper):
    top, bottom, basis = factor
    rows, columns = front.shape
    each = WIDE // PB
    blocks = near.shape[0] // LEAD // each
    begin = c * 2 * blocks
    near_at = chunks * 2 * blocks
    far_at = near_at + each * blocks

    def near_piece(j):
        return lambda i, p: (p[near_at + each * jnp.minimum(i, blocks - 1) + j], 0)

    def far_piece(j):
        return lambda i, p: (p[far_at + each * jnp.maximum(i - blocks, 0) + j], 0)

    in_specs = [
        pl.BlockSpec(top.shape, lambda i, p: (0, 0)),
        pl.BlockSpec(bottom.shape, lambda i, p: (0, 0)),
        pl.BlockSpec(basis.shape, lambda i, p: (0, 0)),
        *[pl.BlockSpec((LEAD, PB), near_piece(j)) for j in range(each)],
        *[pl.BlockSpec((LEAD, PB), far_piece(j)) for j in range(each)],
        pl.BlockSpec((rows, WIDE), lambda i, p: (0, p[begin + i])),
    ]
    operands = [places, top, bottom, basis] + [near] * each + [far] * each + [front]
    aliases = {4 + 2 * each: 1}
    if upper is not None:
        in_specs.append(pl.BlockSpec(memory_space=pl.ANY))
        operands.append(upper)
        aliases[5 + 2 * each] = 0
    return pl.pallas_call(
        functools.partial(project_kernel, blocks),
        grid_spec=pltpu.PrefetchScalarGridSpec(
            num_scalar_prefetch=1,
            grid=(2 * blocks,),
            in_specs=in_specs,
            out_specs=(
                pl.BlockSpec((LEAD, WIDE), lambda i, p: (0, p[begin + i])),
                pl.BlockSpec((rows, WIDE), lambda i, p: (0, p[begin + i])),
                pl.BlockSpec((8, PB), lambda i, p: (0, 0)),
            ),
        ),
        out_shape=(
            jax.ShapeDtypeStruct((LEAD, columns), F32),
            jax.ShapeDtypeStruct((rows, columns), F32),
            jax.ShapeDtypeStruct((8, PB), F32),
        ),
        input_output_aliases=aliases,
        compiler_params=params(),
        cost_estimate=cost(3 * 10**9),
        name="project_columns",
    )(*operands)


def exchange(value, row_count):
    slots, width = value.shape
    shaped = value.reshape(row_count, slots // row_count, width)
    return lax.all_to_all(shaped, "row", split_axis=0, concat_axis=0, tiled=True).reshape(
        slots, width
    )


def on_device(front_matrix, child_rows, child_owner, child_offset):
    row_count = lax.axis_size("row")
    col_count = lax.axis_size("col")
    local_rows, local_cols = front_matrix.shape
    child_count = child_rows.shape[0]
    capacity = 2 * child_count // row_count
    me = lax.axis_index("row")

    owner, offset = child_owner[:, 0], child_offset[:, 0]
    packed = pack(child_rows, owner, row_count, capacity)
    child = exchange(packed, row_count)
    lead_rows = child_rows[:, :LEAD]
    first = first_hop(lead_rows, col_count)
    cut = local_rows // 2

    def cut_body(front_ref, low_ref, high_ref):
        low_ref[...] = front_ref[:cut, :]
        high_ref[...] = front_ref[cut:, :]

    low, high = ordered(
        "cut_lead", cut_body, [front_matrix[:, :LEAD]],
        [jax.ShapeDtypeStruct((cut, LEAD), F32)] * 2, (first,),
    )
    given = spread(lead_rows, first, col_count, (), False)
    pieces = list(pack_lead(given, owner, offset, row_count, capacity, local_rows, col_count))
    for mask in range(1, row_count):
        pairs = [(d, d ^ mask) for d in range(row_count)]
        pieces[mask] = lax.ppermute(pieces[mask], "row", pairs)
    low_got, high_got = first_hop(low, col_count), first_hop(high, col_count)
    own_piece = pieces[0]
    fronts = spread(low, low_got, col_count, (given[0],), True)
    fronts += spread(high, high_got, col_count, (child, own_piece), True)
    lead, left, place, gram = lead_setup(fronts, pieces, local_rows, col_count)

    chunks = max(1, min(4, local_cols // (PB * row_count)))
    width = local_cols // 2 // chunks
    blocks = width // WIDE
    core = upper_side(0, row_count)
    *send, front = product(1 - core, left, place, front_matrix, child, None, chunks)
    *keep, front = product(core, left, place, front_matrix, child, front, chunks)

    halves = [split_add(1, row_count, keep[c], swap(send[c], 0, row_count), ()) for c in range(chunks)]

    matrix = total(gram, row_count, (keep[0],), tuple(h[0] for h in halves))
    made = []
    for k in range(PANELS):
        matrix = [eliminate(matrix, k)]
        made.append(matrix[0])
    matrix = matrix[0]
    scale = math.sqrt(local_rows * row_count)
    top, bottom, basis, scaled = finish(matrix, lead, scale)

    shards = [
        scatter_rest(*halves[c], row_count, (made[min(c, PANELS - 1)],))
        for c in range(chunks)
    ]
    steps = row_count.bit_length() - 1
    columns_at = [
        [
            ((d & 1) ^ side) * chunks * blocks + c * blocks + b
            for c in range(chunks)
            for side in range(2)
            for b in range(blocks)
        ]
        for d in range(row_count)
    ]
    order = piece_order(row_count).reshape(row_count, -1)
    table = np.concatenate([np.array(columns_at, np.int32), order], axis=1)
    places = lax.dynamic_index_in_dim(jnp.asarray(table), me, 0, keepdims=False)
    upper = None
    done = []
    for c in range(chunks):
        buf = shards[c][0]
        for step in reversed(range(steps)):
            got = swap(buf, step, row_count)
            if step == steps - 1 and step > 1:
                buf = join(buf, got, tuple(keep for _, keep in shards) + (top,))
            elif step == 1 and c >= LAG:
                buf = join(buf, got, (done[c - LAG],))
            elif step > 0:
                buf = jnp.concatenate([buf, got], axis=0)
        upper, front, at = project(places, c, chunks, (top, bottom, basis), buf, got, front, upper)
        done.append(at)
    return upper, front, scaled


def solution(mesh):
    placed = (P("row", "col"), P("row", "col"), P("row", None), P("row", None))
    return jax.shard_map(
        on_device,
        mesh=mesh,
        in_specs=placed,
        out_specs=(P(None, "col"), P("row", "col"), P("row", None)),
        check_vma=False,
    )
```
